32 devices in a mesh: groups: 2 (over y), expert: 4 (over z), dp: 4 (over x, core).
Axes of the slice: x: 2, y: 2, z: 4, core: 2. Of those that a mesh axis runs over, the one named last changes fastest.
Arguments:
- tokens: bfloat16 [4096, 2048], P(('groups', 'expert', 'dp')), parts along dimension 0, may hold values from -6 to 6
- routes: int32 [4096, 8], P(('groups', 'expert', 'dp')), parts along dimension 0, may hold values from 0 to 127, all different within a row; in each aligned block of 128 rows (0 to 127, 128 to 255, ...) at most 16 rows name the same one
- route_weight: float32 [4096, 8], P(('groups', 'expert', 'dp')), parts along dimension 0, may hold values from 0.1 to 1
- norm_gain: float32 [2048], replicated, may hold values from 0.25 to 1.75
- w_gate: bfloat16 [128, 2048, 768], P(('expert', 'dp')), may hold values from -0.125 to 0.125
- w_up: bfloat16 [128, 2048, 768], P(('expert', 'dp')), may hold values from -0.125 to 0.125
- w_down: bfloat16 [128, 768, 2048], P(('expert', 'dp')), may hold values from -0.21875 to 0.21875
Outputs:
- mixed: bfloat16 [4096, 2048], P(('groups', 'expert', 'dp')), parts along dimension 0
The draws below stay inside these ranges and needn't reach their ends.
There are 2 independent parts, one for each index of `groups`. The reference program is written for one: setup_inputs(seed, part) draws one part's arguments, and reference() takes and returns one part's arrays. A program takes and returns all parts, laid end to end along the dimension named above; an argument that names none is the same for every part. Nothing has to cross between parts.
Inputs may be any that keep to these rules, and one draw needn't show every extreme that they name: `routes`: each row names 8 different experts. In the 128 rows of one device (aligned blocks), no expert is named by more than 16 rows, and in every draw some expert is named by exactly 16 rows of some device; every expert is named somewhere.
All inputs are finite; a program needn't handle non-finite values.
Results may differ from the reference program's by a relative error of at most 0.007.
Values may be sent and summed in bfloat16 or wider, within the bound.
No kernel may reach another device: no remote copies, remote signals or barrier semaphores. Data moves between devices by JAX's collectives and lax.ppermute only.
A program may use at most 256 MiB of HBM per device.

```python
import math
import jax
import jax.numpy as jnp
import numpy as np
from jax import lax

D = 2048
FF = 768
EXPERTS = 128
TOP = 8
TOK_DEV = 128
CAP = 16
TOKENS = 2048
N_EXPERT = 4
N_DP = 4


def levels(key, dims, pieces, least, top_value):
    def one(dim, parts):
        heights = jax.random.uniform(jax.random.fold_in(jax.random.fold_in(key, 6), dim), (parts,), jnp.float32, least / len(pieces), top_value / len(pieces))
        return jnp.repeat(jnp.exp(heights), dims[dim] // parts).reshape((-1,) + (1,) * (len(dims) - dim - 1))

    factor_of = one(*pieces[0])
    for cut in pieces[1:]:
        factor_of = factor_of * one(*cut)
    return factor_of


def shared_out(key, own, number, rows, number_of, top, bound, lean):
    ranking = jax.random.permutation(key, number_of)
    crowded, usual = shares(number_of, rows * top, bound, lean, True), shares(number_of, rows * top, bound, lean, False)
    places = jnp.arange(number_of)

    def named(lengths, offset_by):
        used = int((lengths > 0).sum())
        fixed = max(1, used // 4)
        shifted = fixed + (places - fixed + offset_by * (used - fixed)) % max(1, number_of - fixed)
        return jnp.zeros((number_of,), jnp.int32).at[ranking[jnp.where(places < fixed, places, shifted)]].set(jnp.asarray(lengths, jnp.int32))

    lengths = jnp.where(number % 4 == 0, named(crowded, number // 4), named(usual, number - number // 4 - 1))
    mixed = jax.random.permutation(jax.random.fold_in(own, 3), number_of)
    donor, sink = mixed[0:number_of // 2 * 2:2], mixed[1:number_of // 2 * 2:2]
    room = jnp.minimum(lengths[donor] - 1, bound - lengths[sink]) // 2
    room = jnp.where((donor == ranking[0]) | (sink == ranking[0]) | (lengths[sink] == 0), 0, jnp.maximum(room, 0))
    shifted = jax.random.randint(jax.random.fold_in(own, 4), (number_of // 2,), 0, 1 << 20) % (room + 1)
    lengths = lengths.at[donor].add(-shifted).at[sink].add(shifted)
    items = jnp.searchsorted(jnp.cumsum(lengths), jnp.arange(rows * top), side="right").astype(jnp.int32)
    table = items.reshape(top, rows).T
    table = table[jax.random.permutation(jax.random.fold_in(own, 1), rows)]
    offset_by = jax.random.randint(jax.random.fold_in(own, 2), (rows, 1), 0, top)
    return jnp.take_along_axis(table, (jnp.arange(top)[None, :] + offset_by) % top, axis=1)


def shares(number_of, total, limit, slope, full):
    weights = [(1 << 20) // math.isqrt(rank ** slope) + 1 for rank in range(1, number_of + 1)]
    largest = limit if full else min(limit, max(-(-total // number_of), total * weights[0] // sum(weights)))
    least = 1 if total - largest >= number_of - 1 else 0
    holding, surplus = [largest] + [least] * (number_of - 1), total - largest - least * (number_of - 1)
    while surplus > 0:
        candidates = [i for i in range(1, number_of) if holding[i] < largest] or [i for i in range(1, number_of) if holding[i] < limit]
        pool, remaining = sum([weights[i] for i in candidates]), surplus
        for i in candidates:
            more = min(limit - holding[i], max(1, remaining * weights[i] // pool), surplus)
            holding[i] = holding[i] + more
            surplus = surplus - more
    return np.array(holding)


def gaussian(stream_key, shape, spread, reach, cuts=(), held_as=jnp.bfloat16):
    drawn = jax.random.normal(stream_key, shape, jnp.float32) * spread
    if len(cuts) > 0:
        drawn = levels(stream_key, shape, cuts, -0.22, 0.18) * drawn
    return jnp.clip(drawn, min=-reach, max=reach).astype(held_as)


def setup_inputs(seed: int = 0, part: int = 0) -> dict:
    key_list = jax.random.split(jax.random.key(seed), 8)
    part_keys = jax.random.split(jax.random.fold_in(key_list[7], part), 8)
    tokens = gaussian(part_keys[0], (TOKENS, D), 1.0, 6.0, ((0, 16),))
    routes_keys = jax.random.split(jax.random.fold_in(part_keys[1], 1), TOKENS // TOK_DEV)
    routes_turns = jax.random.permutation(jax.random.fold_in(part_keys[1], 3), TOKENS // TOK_DEV)
    routes = jax.vmap(lambda own, number: shared_out(jax.random.fold_in(part_keys[1], 2), own, number, TOK_DEV, EXPERTS, TOP, CAP, 2))(routes_keys, routes_turns).reshape((TOKENS, TOP))
    route_weight = jnp.clip(jnp.exp(math.log(1.0) - 2.3025851 * jax.random.uniform(part_keys[2], (TOKENS, TOP), jnp.float32) ** levels(part_keys[2], (TOKENS, TOP), ((0, 16),), -0.2, 0.2)), 0.1, 1.0)
    norm_gain = jnp.clip(1.0 + 0.15 * jax.random.normal(key_list[3], (D,), jnp.float32), 0.25, 1.75)
    w_gate = gaussian(key_list[4], (EXPERTS, D, FF), D ** -0.5, 0.125, ((0, 16),))
    w_up = gaussian(key_list[5], (EXPERTS, D, FF), D ** -0.5, 0.125, ((0, 16),))
    w_down = gaussian(key_list[6], (EXPERTS, FF, D), FF ** -0.5, 0.21875, ((0, 16),))
    return {"tokens": tokens, "routes": routes, "route_weight": route_weight, "norm_gain": norm_gain, "w_gate": w_gate, "w_up": w_up, "w_down": w_down}


def reference(tokens, routes, route_weight, norm_gain, w_gate, w_up, w_down):
    as_float = tokens.astype(jnp.float32)
    normed = (as_float * lax.rsqrt(lax.optimization_barrier(jnp.mean(as_float * as_float, axis=-1, keepdims=True)) + 1e-06) * norm_gain.astype(jnp.float32)).astype(jnp.bfloat16)
    token_count = routes.shape[0]
    top_count = routes.shape[1]
    expert_count = w_gate.shape[0]
    feature_dim = tokens.shape[1]
    flat_routes = routes.reshape(-1).astype(jnp.int32)
    pair_order = jnp.argsort(flat_routes, stable=True).astype(jnp.int32)
    loads = jnp.zeros((expert_count,), jnp.int32).at[flat_routes].add(1)
    starts = (jnp.cumsum(loads) - loads).astype(jnp.int32)
    most_rows = N_EXPERT * N_DP * CAP
    padded_order = jnp.concatenate([pair_order, jnp.zeros((most_rows,), jnp.int32)])
    flat_weight = route_weight.reshape(-1)

    def one_expert(total, expert_index):
        pairs = lax.dynamic_slice(padded_order, (starts[expert_index],), (most_rows,))
        live = jnp.arange(most_rows, dtype=jnp.int32) < loads[expert_index]
        token_index = (pairs // top_count).astype(jnp.int32)
        chosen = normed[token_index]
        gate_part = jnp.dot(chosen, w_gate[expert_index], preferred_element_type=jnp.float32)
        up_part = jnp.dot(chosen, w_up[expert_index], preferred_element_type=jnp.float32)
        hidden = (jax.nn.silu(gate_part) * up_part).astype(jnp.bfloat16)
        produced = jnp.dot(hidden, w_down[expert_index], preferred_element_type=jnp.float32).astype(jnp.bfloat16)
        scaled = flat_weight[pairs][:, None] * produced.astype(jnp.float32)
        scaled = jnp.where(live[:, None], scaled, jnp.zeros_like(scaled))
        return (total.at[token_index].add(scaled), None)
    total, unused = lax.scan(one_expert, jnp.zeros((token_count, feature_dim), jnp.float32), jnp.arange(expert_count, dtype=jnp.int32))
    return total.astype(jnp.bfloat16)
```

```python
import functools

import jax
import jax.numpy as jnp
from jax import lax
from jax.experimental import pallas as pl
from jax.experimental.pallas import tpu as pltpu
from jax.sharding import PartitionSpec as P

slots = 16
gather_chunks = 2
return_chunks = 4
grant = 56 * 1024 * 1024


def rounded_sum(first, *others):
    total = first.astype(jnp.float32)
    for other in others:
        total = total + other.astype(jnp.float32)
    return total.astype(jnp.bfloat16)


def pick_kernel(picker_ref, tokens_ref, rows_ref):
    sources = tokens_ref.shape[0]
    experts = rows_ref.shape[0]
    for source in range(sources):
        picked = jnp.dot(
            picker_ref[source], tokens_ref[source], preferred_element_type=jnp.float32
        ).astype(jnp.bfloat16)
        for expert in range(experts):
            rows_ref[expert, source] = picked[expert * slots : (expert + 1) * slots]


def pick_rows(picker, tokens, experts):
    sources, token_count, width = tokens.shape
    block = min(sources, 8)
    return pl.pallas_call(
        pick_kernel,
        grid=(sources // block,),
        in_specs=[
            pl.BlockSpec((block, experts * slots, token_count), lambda i: (i, 0, 0)),
            pl.BlockSpec((block, token_count, width), lambda i: (i, 0, 0)),
        ],
        out_specs=pl.BlockSpec((experts, block, slots, width), lambda i: (0, i, 0, 0)),
        out_shape=jax.ShapeDtypeStruct((experts, sources, slots, width), jnp.bfloat16),
        compiler_params=pltpu.CompilerParams(vmem_limit_bytes=grant),
        cost_estimate=pl.CostEstimate(
            flops=2 * sources * experts * slots * token_count * width,
            bytes_accessed=2 * sources * width * (token_count + experts * slots),
            transcendentals=0,
        ),
    )(picker, tokens)


def hidden_kernel(chunks, *refs):
    row_refs = refs[: 2 * chunks]
    scale_ref, gate_ref, up_ref, hidden_ref = refs[2 * chunks :]
    gate_part = None
    width = row_refs[0].shape[-1]
    for chunk in range(chunks):
        rows = jnp.concatenate([row_refs[2 * chunk][0], row_refs[2 * chunk + 1][0]], axis=0)
        depth = pl.ds(chunk * width, width)
        gate_add = jnp.dot(rows, gate_ref[0, depth, :], preferred_element_type=jnp.float32)
        up_add = jnp.dot(rows, up_ref[0, depth, :], preferred_element_type=jnp.float32)
        if gate_part is None:
            gate_part, up_part = gate_add, up_add
        else:
            gate_part, up_part = gate_part + gate_add, up_part + up_add
    hidden = gate_part / (1.0 + jnp.exp(-gate_part)) * up_part * scale_ref[0]
    hidden_ref[0] = hidden.astype(jnp.bfloat16)


def hidden_rows(row_chunks, scale, w_gate, w_up):
    experts, feature_dim, hidden_dim = w_gate.shape
    half = row_chunks[0].shape[1]
    chunks = len(row_chunks) // 2
    width = row_chunks[0].shape[2]
    whole = 2 * half
    return pl.pallas_call(
        functools.partial(hidden_kernel, chunks),
        grid=(experts,),
        in_specs=[pl.BlockSpec((1, half, width), lambda e: (e, 0, 0))] * (2 * chunks)
        + [
            pl.BlockSpec((1, whole, 1), lambda e: (e, 0, 0)),
            pl.BlockSpec((1, feature_dim, hidden_dim), lambda e: (e, 0, 0)),
            pl.BlockSpec((1, feature_dim, hidden_dim), lambda e: (e, 0, 0)),
        ],
        out_specs=pl.BlockSpec((1, whole, hidden_dim), lambda e: (e, 0, 0)),
        out_shape=jax.ShapeDtypeStruct((experts, whole, hidden_dim), jnp.bfloat16),
        compiler_params=pltpu.CompilerParams(vmem_limit_bytes=grant),
        cost_estimate=pl.CostEstimate(
            flops=4 * experts * whole * feature_dim * hidden_dim,
            bytes_accessed=4 * experts * feature_dim * hidden_dim,
            transcendentals=experts * whole * hidden_dim,
        ),
    )(*row_chunks, scale, w_gate, w_up)


def mix_kernel(hidden_ref, down_ref, spread_ref, first_ref, second_ref, made):
    expert = pl.program_id(0)
    experts = pl.num_programs(0)
    sources = spread_ref.shape[0]
    width = down_ref.shape[2]
    made[expert] = (
        jnp.dot(hidden_ref[0], down_ref[0], preferred_element_type=jnp.float32)
        .astype(jnp.bfloat16)
        .reshape(sources, slots, width)
    )

    @pl.when(expert == experts - 1)
    def _():
        for source in range(sources):
            rows = made[:, source].reshape(spread_ref.shape[2], width)
            mixed = jnp.dot(
                spread_ref[source], rows, preferred_element_type=jnp.float32
            ).astype(jnp.bfloat16)
            if source < sources // 2:
                first_ref[source] = mixed
            else:
                second_ref[source - sources // 2] = mixed


def mix_rows(hidden, w_down, spread, chunk, chunks):
    experts, whole, hidden_dim = hidden.shape
    width = w_down.shape[2] // chunks
    sources, token_count, local_rows = spread.shape
    half = jax.ShapeDtypeStruct((sources // 2, token_count, width), jnp.bfloat16)
    return pl.pallas_call(
        mix_kernel,
        grid=(experts,),
        in_specs=[
            pl.BlockSpec((1, whole, hidden_dim), lambda e: (e, 0, 0)),
            pl.BlockSpec((1, hidden_dim, width), lambda e: (e, 0, chunk)),
            pl.BlockSpec(memory_space=pltpu.VMEM),
        ],
        out_specs=[pl.BlockSpec(memory_space=pltpu.VMEM)] * 2,
        out_shape=[half, half],
        scratch_shapes=[pltpu.VMEM((experts, sources, slots, width), jnp.bfloat16)],
        compiler_params=pltpu.CompilerParams(vmem_limit_bytes=grant),
        cost_estimate=pl.CostEstimate(
            flops=2 * experts * whole * hidden_dim * width
            + 2 * sources * token_count * local_rows * width,
            bytes_accessed=2 * experts * hidden_dim * (width + whole)
            + 2 * sources * token_count * width,
            transcendentals=0,
        ),
    )(hidden, w_down, spread)


axes = ("expert", "dp")


def pairs_of(expert_pairs, dp_pairs, dp_size):
    return [
        (e_from * dp_size + d_from, e_to * dp_size + d_to)
        for e_from, e_to in expert_pairs
        for d_from, d_to in dp_pairs
    ]


stay_z = [(i, i) for i in range(4)]
stay_dp = [(i, i) for i in range(4)]
swap_z = pairs_of([(0, 1), (1, 0), (2, 3), (3, 2)], stay_dp, 4)
middle_z = pairs_of([(1, 2), (2, 1)], stay_dp, 4)
outward_z = pairs_of([(1, 0), (2, 3)], stay_dp, 4)
inward_z = pairs_of([(0, 1), (3, 2)], stay_dp, 4)
swap_x = pairs_of(stay_z, [(0, 2), (2, 0), (1, 3), (3, 1)], 4)
swap_core = pairs_of(stay_z, [(0, 1), (1, 0), (2, 3), (3, 2)], 4)


def send(value, pairs):
    return lax.ppermute(value, axes, pairs)


def tree_gather(own, edge):
    near = send(own, swap_z)
    middle = send(own, middle_z)
    cross = send(near, middle_z)
    outer = send(middle, outward_z)
    far = send(cross, outward_z)
    third = jnp.where(edge, outer, middle)
    fourth = jnp.where(edge, far, cross)
    column = [own, near, third, fourth]
    other = [send(value, swap_x) for value in column]
    return jnp.stack(column + other)


def tree_return(mine, theirs):
    chip = rounded_sum(mine, send(theirs, swap_core))
    arrived = [send(chip[4 + i], swap_x) for i in (3, 2, 1, 0)]
    fourth, third, near, own = [
        rounded_sum(chip[i], value) for i, value in zip((3, 2, 1, 0), arrived)
    ]
    cross = rounded_sum(fourth, send(fourth, inward_z))
    middle = rounded_sum(third, send(third, inward_z))
    near = rounded_sum(near, send(cross, middle_z))
    return rounded_sum(own, send(middle, middle_z), send(near, swap_z))


def slot_sources():
    z = lax.axis_index("expert")
    dp = lax.axis_index("dp")
    x, core = dp // 2, dp % 2
    low = z < 2
    column = jnp.stack([z, z ^ 1, jnp.where(low, 2, 1), jnp.where(low, 3, 0)])
    core_of = core ^ jnp.arange(2)[:, None, None]
    x_of = x ^ jnp.arange(2)[None, :, None]
    return (column[None, None, :] * 4 + x_of * 2 + core_of).reshape(-1)


def shards(tokens, routes, route_weight, norm_gain, w_gate, w_up, w_down):
    token_count, top_count = routes.shape
    feature_dim = tokens.shape[1]
    expert_size = lax.axis_size("expert")
    dp_size = lax.axis_size("dp")
    device_count = expert_size * dp_size
    local_count = w_gate.shape[0]
    as_tree = expert_size == 4 and dp_size == 4
    edge = (lax.axis_index("expert") % 3) == 0

    as_float = tokens.astype(jnp.float32)
    normed = (
        as_float
        * lax.rsqrt(jnp.mean(as_float * as_float, axis=-1, keepdims=True) + 1e-06)
        * norm_gain
    ).astype(jnp.bfloat16)

    choice = jnp.concatenate([routes.astype(jnp.float32).T, route_weight.T], axis=0)
    choices = lax.all_gather(choice, axes)
    if as_tree:
        choices = choices[slot_sources()]
    chosen, weight = choices[:, :top_count], choices[:, top_count:]
    first_expert = (lax.axis_index("expert") * dp_size + lax.axis_index("dp")) * local_count
    local = (first_expert + jnp.arange(local_count)).astype(jnp.float32)
    same = chosen[:, None] == local[None, :, None, None]
    named = jnp.any(same, axis=2)
    named_weight = jnp.sum(jnp.where(same, weight[:, None], 0.0), axis=2)
    before = (jnp.arange(token_count)[:, None] < jnp.arange(token_count)[None, :]).astype(
        jnp.bfloat16
    )
    rank = jnp.dot(named.astype(jnp.bfloat16), before, preferred_element_type=jnp.float32)
    rank = jnp.where(named, rank, -1.0)
    match = rank[:, :, None, :] == jnp.arange(slots, dtype=jnp.float32)[None, None, :, None]
    picker = match.astype(jnp.bfloat16).reshape(device_count, local_count * slots, token_count)
    spread = picker.transpose(0, 2, 1)
    scale = jnp.sum(jnp.where(match, named_weight[:, :, None, :], 0.0), axis=3)
    scale = scale.transpose(1, 0, 2).reshape(local_count, device_count * slots, 1)

    width = feature_dim // gather_chunks
    half = device_count // 2
    row_chunks = []
    for chunk in range(gather_chunks):
        part = normed[:, chunk * width : (chunk + 1) * width]
        if as_tree:
            mine = tree_gather(part, edge)
            theirs = send(mine, swap_core)
        else:
            gathered = lax.all_gather(part, axes)
            mine, theirs = gathered[:half], gathered[half:]
        for value, which in ((mine, picker[:half]), (theirs, picker[half:])):
            rows = pick_rows(which, value, local_count)
            row_chunks.append(rows.reshape(local_count, half * slots, width))
    hidden = hidden_rows(row_chunks, scale, w_gate, w_up)

    results = []
    for chunk in range(return_chunks):
        mine, theirs = mix_rows(hidden, w_down, spread, chunk, return_chunks)
        if as_tree:
            results.append(tree_return(mine, theirs))
        else:
            whole = jnp.concatenate([mine, theirs], axis=0).astype(jnp.float32)
            total = lax.psum_scatter(whole, axes, scatter_dimension=0)
            results.append(total.astype(jnp.bfloat16))
    return jnp.concatenate(results, axis=1)


def solution(mesh):
    split = P(("groups", "expert", "dp"), None)
    by_expert = P(("expert", "dp"), None, None)
    return jax.shard_map(
        shards,
        mesh=mesh,
        in_specs=(split, split, split, P(), by_expert, by_expert, by_expert),
        out_specs=split,
        check_vma=False,
    )
```

```python
import functools

import jax
import jax.numpy as jnp
from jax import lax
from jax.experimental import pallas as pl
from jax.experimental.pallas import tpu as pltpu
from jax.sharding import PartitionSpec as P

slots = 16
gather_chunks = 2
return_chunks = 2
grant = 56 * 1024 * 1024


def rounded_sum(first, *others):
    total = first.astype(jnp.float32)
    for other in others:
        total = total + other.astype(jnp.float32)
    return total.astype(jnp.bfloat16)


def pick_kernel(picker_ref, tokens_ref, rows_ref):
    sources = tokens_ref.shape[0]
    experts = rows_ref.shape[0]
    for source in range(sources):
        picked = jnp.dot(
            picker_ref[source], tokens_ref[source], preferred_element_type=jnp.float32
        ).astype(jnp.bfloat16)
        for expert in range(experts):
            rows_ref[expert, source] = picked[expert * slots : (expert + 1) * slots]


def pick_rows(picker, tokens, experts):
    sources, token_count, width = tokens.shape
    block = min(sources, 8)
    return pl.pallas_call(
        pick_kernel,
        grid=(sources // block,),
        in_specs=[
            pl.BlockSpec((block, experts * slots, token_count), lambda i: (i, 0, 0)),
            pl.BlockSpec((block, token_count, width), lambda i: (i, 0, 0)),
        ],
        out_specs=pl.BlockSpec((experts, block, slots, width), lambda i: (0, i, 0, 0)),
        out_shape=jax.ShapeDtypeStruct((experts, sources, slots, width), jnp.bfloat16),
        compiler_params=pltpu.CompilerParams(vmem_limit_bytes=grant),
        cost_estimate=pl.CostEstimate(
            flops=2 * sources * experts * slots * token_count * width,
            bytes_accessed=2 * sources * width * (token_count + experts * slots),
            transcendentals=0,
        ),
    )(picker, tokens)


def hidden_kernel(chunks, groups, *refs):
    row_refs = refs[: chunks * groups]
    scale_ref, gate_ref, up_ref, hidden_ref = refs[chunks * groups :]
    gate_part = None
    width = row_refs[0].shape[-1]
    for chunk in range(chunks):
        pieces = [ref[0] for ref in row_refs[chunk * groups : (chunk + 1) * groups]]
        rows = jnp.concatenate(pieces, axis=0)
        depth = pl.ds(chunk * width, width)
        gate_add = jnp.dot(rows, gate_ref[0, depth, :], preferred_element_type=jnp.float32)
        up_add = jnp.dot(rows, up_ref[0, depth, :], preferred_element_type=jnp.float32)
        if gate_part is None:
            gate_part, up_part = gate_add, up_add
        else:
            gate_part, up_part = gate_part + gate_add, up_part + up_add
    hidden = gate_part / (1.0 + jnp.exp(-gate_part)) * up_part * scale_ref[0]
    hidden_ref[0] = hidden.astype(jnp.bfloat16)


def hidden_rows(row_chunks, scale, w_gate, w_up):
    experts, feature_dim, hidden_dim = w_gate.shape
    groups = len(row_chunks[0])
    chunks = len(row_chunks)
    pieces = [piece for row_groups in row_chunks for piece in row_groups]
    whole = scale.shape[1]
    return pl.pallas_call(
        functools.partial(hidden_kernel, chunks, groups),
        grid=(experts,),
        in_specs=[pl.BlockSpec((1,) + piece.shape[1:], lambda e: (e, 0, 0)) for piece in pieces]
        + [
            pl.BlockSpec((1, whole, 1), lambda e: (e, 0, 0)),
            pl.BlockSpec((1, feature_dim, hidden_dim), lambda e: (e, 0, 0)),
            pl.BlockSpec((1, feature_dim, hidden_dim), lambda e: (e, 0, 0)),
        ],
        out_specs=pl.BlockSpec((1, whole, hidden_dim), lambda e: (e, 0, 0)),
        out_shape=jax.ShapeDtypeStruct((experts, whole, hidden_dim), jnp.bfloat16),
        compiler_params=pltpu.CompilerParams(vmem_limit_bytes=grant),
        cost_estimate=pl.CostEstimate(
            flops=4 * experts * whole * feature_dim * hidden_dim,
            bytes_accessed=4 * experts * feature_dim * hidden_dim,
            transcendentals=experts * whole * hidden_dim,
        ),
    )(*pieces, scale, w_gate, w_up)


def mix_kernel(hidden_ref, down_ref, spread_ref, first_ref, second_ref, made):
    expert = pl.program_id(0)
    experts = pl.num_programs(0)
    sources = spread_ref.shape[0]
    width = down_ref.shape[2]
    made[expert] = (
        jnp.dot(hidden_ref[0], down_ref[0], preferred_element_type=jnp.float32)
        .astype(jnp.bfloat16)
        .reshape(sources, slots, width)
    )

    @pl.when(expert == experts - 1)
    def _():
        for source in range(sources):
            rows = made[:, source].reshape(spread_ref.shape[2], width)
            mixed = jnp.dot(
                spread_ref[source], rows, preferred_element_type=jnp.float32
            ).astype(jnp.bfloat16)
            if source < sources // 2:
                first_ref[source] = mixed
            else:
                second_ref[source - sources // 2] = mixed


def mix_rows(hidden, w_down, spread, chunk, chunks):
    experts, whole, hidden_dim = hidden.shape
    width = w_down.shape[2] // chunks
    sources, token_count, local_rows = spread.shape
    half = jax.ShapeDtypeStruct((sources // 2, token_count, width), jnp.bfloat16)
    return pl.pallas_call(
        mix_kernel,
        grid=(experts,),
        in_specs=[
            pl.BlockSpec((1, whole, hidden_dim), lambda e: (e, 0, 0)),
            pl.BlockSpec((1, hidden_dim, width), lambda e: (e, 0, chunk)),
            pl.BlockSpec(memory_space=pltpu.VMEM),
        ],
        out_specs=[pl.BlockSpec(memory_space=pltpu.VMEM)] * 2,
        out_shape=[half, half],
        scratch_shapes=[pltpu.VMEM((experts, sources, slots, width), jnp.bfloat16)],
        compiler_params=pltpu.CompilerParams(vmem_limit_bytes=grant),
        cost_estimate=pl.CostEstimate(
            flops=2 * experts * whole * hidden_dim * width
            + 2 * sources * token_count * local_rows * width,
            bytes_accessed=2 * experts * hidden_dim * (width + whole)
            + 2 * sources * token_count * width,
            transcendentals=0,
        ),
    )(hidden, w_down, spread)


axes = ("expert", "dp")


def pairs_of(expert_pairs, dp_pairs, dp_size):
    return [
        (e_from * dp_size + d_from, e_to * dp_size + d_to)
        for e_from, e_to in expert_pairs
        for d_from, d_to in dp_pairs
    ]


stay_z = [(i, i) for i in range(4)]
stay_dp = [(i, i) for i in range(4)]
swap_z = pairs_of([(0, 1), (1, 0), (2, 3), (3, 2)], stay_dp, 4)
middle_z = pairs_of([(1, 2), (2, 1)], stay_dp, 4)
outward_z = pairs_of([(1, 0), (2, 3)], stay_dp, 4)
inward_z = pairs_of([(0, 1), (3, 2)], stay_dp, 4)
swap_x = pairs_of(stay_z, [(0, 2), (2, 0), (1, 3), (3, 1)], 4)
swap_core = pairs_of(stay_z, [(0, 1), (1, 0), (2, 3), (3, 2)], 4)


def send(value, pairs):
    return lax.ppermute(value, axes, pairs)


def together(*values):
    return lax.optimization_barrier(values)


def tree_gather(own, edge):
    near, middle, own_x = together(
        send(own, swap_z), send(own, middle_z), send(own, swap_x)
    )
    cross, outer, near_x = together(
        send(near, middle_z), send(middle, outward_z), send(near, swap_x)
    )
    third = jnp.where(edge, outer, middle)
    far, third_x = together(send(cross, outward_z), send(third, swap_x))
    fourth = jnp.where(edge, far, cross)
    early = jnp.stack([own, near, third, own_x, near_x, third_x])
    fourth_x = send(fourth, swap_x)
    return early, jnp.stack([fourth, fourth_x])


def chip_sums(mine, theirs):
    return rounded_sum(mine, send(theirs, swap_core))


def tree_return(chip):
    own, near, third, own_x, near_x, third_x, fourth, fourth_x = [chip[i] for i in range(8)]
    fourth = rounded_sum(fourth, send(fourth_x, swap_x))
    far, third_in = together(send(fourth, inward_z), send(third_x, swap_x))
    cross = rounded_sum(fourth, far)
    third = rounded_sum(third, third_in)
    outer, crossed, near_in = together(
        send(third, inward_z), send(cross, middle_z), send(near_x, swap_x)
    )
    middle = rounded_sum(third, outer)
    near = rounded_sum(near, near_in, crossed)
    return rounded_sum(
        own, send(own_x, swap_x), send(middle, middle_z), send(near, swap_z)
    )


def slot_sources():
    z = lax.axis_index("expert")
    dp = lax.axis_index("dp")
    x, core = dp // 2, dp % 2
    low = z < 2
    column = jnp.stack([z, z ^ 1, jnp.where(low, 2, 1), jnp.where(low, 3, 0)])
    slot_z = column[jnp.array([0, 1, 2, 0, 1, 2, 3, 3])]
    slot_x = x ^ jnp.array([0, 0, 0, 1, 1, 1, 0, 1])
    core_of = core ^ jnp.arange(2)[:, None]
    return (slot_z * 4 + slot_x * 2 + core_of).reshape(-1)


def shards(tokens, routes, route_weight, norm_gain, w_gate, w_up, w_down):
    token_count, top_count = routes.shape
    feature_dim = tokens.shape[1]
    expert_size = lax.axis_size("expert")
    dp_size = lax.axis_size("dp")
    device_count = expert_size * dp_size
    local_count = w_gate.shape[0]
    as_tree = expert_size == 4 and dp_size == 4
    edge = (lax.axis_index("expert") % 3) == 0

    as_float = tokens.astype(jnp.float32)
    normed = (
        as_float
        * lax.rsqrt(jnp.mean(as_float * as_float, axis=-1, keepdims=True) + 1e-06)
        * norm_gain
    ).astype(jnp.bfloat16)

    every = jnp.arange(device_count * local_count, dtype=jnp.int32)
    same = routes[:, :, None] == every
    named = jnp.any(same, axis=1)
    named_weight = jnp.sum(jnp.where(same, route_weight[:, :, None], 0.0), axis=1)
    before = (jnp.arange(token_count)[:, None] > jnp.arange(token_count)[None, :]).astype(
        jnp.bfloat16
    )
    rank = jnp.dot(before, named.astype(jnp.bfloat16), preferred_element_type=jnp.float32)
    rank = jnp.where(named, rank, -1.0)
    choice = jnp.stack([rank.T, named_weight.T]).reshape(2, device_count, local_count, token_count)
    choice = choice.transpose(1, 0, 2, 3).reshape(device_count, 2 * local_count, token_count)
    choices = lax.all_to_all(choice, axes, split_axis=0, concat_axis=0, tiled=True)
    if as_tree:
        choices = choices[slot_sources()]
    rank, named_weight = choices[:, :local_count], choices[:, local_count:]
    match = rank[:, :, None, :] == jnp.arange(slots, dtype=jnp.float32)[None, None, :, None]
    picker = match.astype(jnp.bfloat16).reshape(device_count, local_count * slots, token_count)
    spread = picker.transpose(0, 2, 1)
    scale = jnp.sum(jnp.where(match, named_weight[:, :, None, :], 0.0), axis=3)
    scale = scale.transpose(1, 0, 2).reshape(local_count, device_count * slots, 1)

    width = feature_dim // gather_chunks
    half = device_count // 2
    row_chunks = []
    for chunk in range(gather_chunks):
        part = normed[:, chunk * width : (chunk + 1) * width]
        if as_tree:
            early, late = tree_gather(part, edge)
            groups = [early, late, send(early, swap_core), send(late, swap_core)]
        else:
            groups = [lax.all_gather(part, axes)]
        first = 0
        row_groups = []
        for group in groups:
            count = group.shape[0]
            rows = pick_rows(picker[first : first + count], group, local_count)
            row_groups.append(rows.reshape(local_count, count * slots, width))
            first += count
        row_chunks.append(row_groups)
    hidden = hidden_rows(row_chunks, scale, w_gate, w_up)

    sums = []
    for chunk in range(return_chunks):
        mine, theirs = mix_rows(hidden, w_down, spread, chunk, return_chunks)
        if as_tree:
            sums.append(chip_sums(mine, theirs))
        else:
            whole = jnp.concatenate([mine, theirs], axis=0).astype(jnp.float32)
            total = lax.psum_scatter(whole, axes, scatter_dimension=0)
            sums.append(total.astype(jnp.bfloat16))
    results = [tree_return(chip) for chip in sums] if as_tree else sums
    return jnp.concatenate(results, axis=1)


def solution(mesh):
    split = P(("groups", "expert", "dp"), None)
    by_expert = P(("expert", "dp"), None, None)
    return jax.shard_map(
        shards,
        mesh=mesh,
        in_specs=(split, split, split, P(), by_expert, by_expert, by_expert),
        out_specs=split,
        check_vma=False,
    )
```

```python
import functools

import jax
import jax.numpy as jnp
from jax import lax
from jax.experimental import pallas as pl
from jax.experimental.pallas import tpu as pltpu
from jax.sharding import PartitionSpec as P

slots = 16
gather_chunks = 2
return_chunks = 2
mebi = 1024 * 1024


def grant(sources, tree_mebi):
    return (tree_mebi if sources <= 16 else 56) * mebi


def rounded_sum(first, *others):
    total = first.astype(jnp.float32)
    for other in others:
        total = total + other.astype(jnp.float32)
    return total.astype(jnp.bfloat16)


def pick_kernel(picker_ref, tokens_ref, rows_ref):
    sources = tokens_ref.shape[0]
    experts = rows_ref.shape[0]
    for source in range(sources):
        picked = jnp.dot(
            picker_ref[source], tokens_ref[source], preferred_element_type=jnp.float32
        ).astype(jnp.bfloat16)
        for expert in range(experts):
            rows_ref[expert, source] = picked[expert * slots : (expert + 1) * slots]


def pick_rows(picker, tokens, experts):
    sources, token_count, width = tokens.shape
    block = min(sources, 8)
    return pl.pallas_call(
        pick_kernel,
        grid=(sources // block,),
        in_specs=[
            pl.BlockSpec((block, experts * slots, token_count), lambda i: (i, 0, 0)),
            pl.BlockSpec((block, token_count, width), lambda i: (i, 0, 0)),
        ],
        out_specs=pl.BlockSpec((experts, block, slots, width), lambda i: (0, i, 0, 0)),
        out_shape=jax.ShapeDtypeStruct((experts, sources, slots, width), jnp.bfloat16),
        compiler_params=pltpu.CompilerParams(vmem_limit_bytes=grant(sources, 16)),
        cost_estimate=pl.CostEstimate(
            flops=2 * sources * experts * slots * token_count * width,
            bytes_accessed=2 * sources * width * (token_count + experts * slots),
            transcendentals=0,
        ),
    )(picker, tokens)


def table_kernel(source_ref, choices_ref, *refs):
    picker_refs, spread_ref, scale_ref = refs[:3], refs[3], refs[4]
    experts = scale_ref.shape[0]
    token_count = choices_ref.shape[2]
    early, late = picker_refs[0].shape[0], picker_refs[2].shape[0] // 2
    place = lax.broadcasted_iota(jnp.int32, (experts, slots, token_count), 1).astype(jnp.float32)
    for slot in range(2 * (early + late)):
        choice = choices_ref[source_ref[slot]]
        match = choice[:experts][:, None, :] == place
        weight = jnp.where(match, choice[experts:][:, None, :], 0.0)
        scale_ref[:, slot * slots : (slot + 1) * slots, :] = jnp.sum(weight, axis=2, keepdims=True)
        picker = jnp.where(match, 1.0, 0.0).reshape(experts * slots, token_count)
        if slot < 2 * early:
            picker_refs[slot // early][slot % early] = picker.astype(jnp.bfloat16)
        else:
            picker_refs[2][slot - 2 * early] = picker.astype(jnp.bfloat16)
        spread_ref[slot] = picker.T.astype(jnp.bfloat16)


def tables(source, choices, experts):
    count, _, token_count = choices.shape
    rows = experts * slots
    late = count // 8
    early = count // 2 - late
    shapes = [(early, rows, token_count), (early, rows, token_count), (2 * late, rows, token_count)]
    shapes = [jax.ShapeDtypeStruct(shape, jnp.bfloat16) for shape in shapes]
    shapes.append(jax.ShapeDtypeStruct((count, token_count, rows), jnp.bfloat16))
    shapes.append(jax.ShapeDtypeStruct((experts, count * slots, 1), jnp.float32))
    return pl.pallas_call(
        table_kernel,
        in_specs=[
            pl.BlockSpec(memory_space=pltpu.SMEM),
            pl.BlockSpec(memory_space=pltpu.VMEM),
        ],
        out_specs=[pl.BlockSpec(memory_space=pltpu.VMEM)] * 5,
        out_shape=shapes,
        compiler_params=pltpu.CompilerParams(vmem_limit_bytes=grant(count, 12)),
    )(source, choices)


def pair_kernel(count, *refs):
    token_refs = refs[:count]
    mine_ref, theirs_ref, mine_rows_ref, theirs_rows_ref = refs[count:]
    experts = mine_rows_ref.shape[0]
    for source in range(count):
        for picker_ref, rows_ref in ((mine_ref, mine_rows_ref), (theirs_ref, theirs_rows_ref)):
            picked = jnp.dot(
                picker_ref[source], token_refs[source][...], preferred_element_type=jnp.float32
            ).astype(jnp.bfloat16)
            rows_ref[:, source] = picked.reshape(experts, slots, picked.shape[1])


def pick_pair(blocks, mine, theirs, experts):
    count = len(blocks)
    token_count, width = blocks[0].shape
    rows = jax.ShapeDtypeStruct((experts, count, slots, width), jnp.bfloat16)
    return pl.pallas_call(
        functools.partial(pair_kernel, count),
        in_specs=[pl.BlockSpec(memory_space=pltpu.VMEM)] * (count + 2),
        out_specs=[pl.BlockSpec(memory_space=pltpu.VMEM)] * 2,
        out_shape=[rows, rows],
        compiler_params=pltpu.CompilerParams(vmem_limit_bytes=grant(count, 16)),
        cost_estimate=pl.CostEstimate(
            flops=4 * count * experts * slots * token_count * width,
            bytes_accessed=2 * count * width * (token_count + 2 * experts * slots),
            transcendentals=0,
        ),
    )(*blocks, mine, theirs)


def hidden_kernel(chunks, groups, late, *refs):
    row_refs = refs[: chunks * groups]
    refs = refs[chunks * groups :]
    late_refs = refs[: chunks * late]
    refs = refs[chunks * late :]
    width = row_refs[0].shape[-1]
    if late:
        picker_ref, scale_ref, gate_ref, up_ref, hidden_ref, late_rows = refs

        @pl.when(pl.program_id(0) == 0)
        def _():
            for chunk in range(chunks):
                for source in range(late):
                    picked = jnp.dot(
                        picker_ref[source],
                        late_refs[chunk * late + source][...],
                        preferred_element_type=jnp.float32,
                    ).astype(jnp.bfloat16)
                    late_rows[:, source, :, chunk * width : (chunk + 1) * width] = picked.reshape(
                        late_rows.shape[0], slots, width
                    )

    else:
        scale_ref, gate_ref, up_ref, hidden_ref = refs
    gate_part = None
    for chunk in range(chunks):
        pieces = [ref[0] for ref in row_refs[chunk * groups : (chunk + 1) * groups]]
        if late:
            extra = late_rows[pl.program_id(0), :, :, chunk * width : (chunk + 1) * width]
            pieces.append(extra.reshape(late * slots, width))
        rows = jnp.concatenate(pieces, axis=0)
        depth = pl.ds(chunk * width, width)
        gate_add = jnp.dot(rows, gate_ref[0, depth, :], preferred_element_type=jnp.float32)
        up_add = jnp.dot(rows, up_ref[0, depth, :], preferred_element_type=jnp.float32)
        if gate_part is None:
            gate_part, up_part = gate_add, up_add
        else:
            gate_part, up_part = gate_part + gate_add, up_part + up_add
    hidden = gate_part / (1.0 + jnp.exp(-gate_part)) * up_part * scale_ref[0]
    hidden_ref[0] = hidden.astype(jnp.bfloat16)


def hidden_rows(row_chunks, late_chunks, late_picker, scale, w_gate, w_up):
    experts, feature_dim, hidden_dim = w_gate.shape
    chunks, groups, late = len(row_chunks), len(row_chunks[0]), len(late_chunks[0])
    pieces = [piece for row_groups in row_chunks for piece in row_groups]
    late_pieces = [piece for blocks in late_chunks for piece in blocks]
    scratch = []
    if late:
        late_pieces.append(late_picker)
        scratch = [pltpu.VMEM((experts, late, slots, feature_dim), jnp.bfloat16)]
    whole = scale.shape[1]
    return pl.pallas_call(
        functools.partial(hidden_kernel, chunks, groups, late),
        grid=(experts,),
        in_specs=[pl.BlockSpec((1,) + piece.shape[1:], lambda e: (e, 0, 0)) for piece in pieces]
        + [pl.BlockSpec(memory_space=pltpu.VMEM)] * len(late_pieces)
        + [
            pl.BlockSpec((1, whole, 1), lambda e: (e, 0, 0)),
            pl.BlockSpec((1, feature_dim, hidden_dim), lambda e: (e, 0, 0)),
            pl.BlockSpec((1, feature_dim, hidden_dim), lambda e: (e, 0, 0)),
        ],
        out_specs=pl.BlockSpec((1, whole, hidden_dim), lambda e: (e, 0, 0)),
        out_shape=jax.ShapeDtypeStruct((experts, whole, hidden_dim), jnp.bfloat16),
        scratch_shapes=scratch,
        compiler_params=pltpu.CompilerParams(vmem_limit_bytes=grant(whole // slots, 32)),
        cost_estimate=pl.CostEstimate(
            flops=4 * experts * whole * feature_dim * hidden_dim,
            bytes_accessed=4 * experts * feature_dim * hidden_dim,
            transcendentals=experts * whole * hidden_dim,
        ),
    )(*pieces, *late_pieces, scale, w_gate, w_up)


def mix_kernel(order, hidden_ref, down_ref, spread_ref, first_ref, second_ref, made):
    step = pl.program_id(0)
    group = hidden_ref.shape[0]
    sources = spread_ref.shape[0]
    width = down_ref.shape[2]
    for one in range(group):
        made[step * group + one] = (
            jnp.dot(hidden_ref[one], down_ref[one], preferred_element_type=jnp.float32)
            .astype(jnp.bfloat16)
            .reshape(sources, slots, width)
        )

    @pl.when(step == pl.num_programs(0) - 1)
    def _():
        for source in range(sources):
            rows = made[:, source].reshape(spread_ref.shape[2], width)
            mixed = jnp.dot(
                spread_ref[source], rows, preferred_element_type=jnp.float32
            ).astype(jnp.bfloat16)
            if order[source] < sources // 2:
                first_ref[order[source]] = mixed
            else:
                second_ref[order[source] - sources // 2] = mixed


def mix_rows(hidden, w_down, spread, order, chunk, chunks):
    experts, whole, hidden_dim = hidden.shape
    width = w_down.shape[2] // chunks
    sources, token_count, local_rows = spread.shape
    group = 2 if experts % 2 == 0 else 1
    half = jax.ShapeDtypeStruct((sources // 2, token_count, width), jnp.bfloat16)
    return pl.pallas_call(
        functools.partial(mix_kernel, order),
        grid=(experts // group,),
        in_specs=[
            pl.BlockSpec((group, whole, hidden_dim), lambda e: (e, 0, 0)),
            pl.BlockSpec((group, hidden_dim, width), lambda e: (e, 0, chunk)),
            pl.BlockSpec(memory_space=pltpu.VMEM),
        ],
        out_specs=[pl.BlockSpec(memory_space=pltpu.VMEM)] * 2,
        out_shape=[half, half],
        scratch_shapes=[pltpu.VMEM((experts, sources, slots, width), jnp.bfloat16)],
        compiler_params=pltpu.CompilerParams(vmem_limit_bytes=grant(sources, 28)),
        cost_estimate=pl.CostEstimate(
            flops=2 * experts * whole * hidden_dim * width
            + 2 * sources * token_count * local_rows * width,
            bytes_accessed=2 * experts * hidden_dim * (width + whole)
            + 2 * sources * token_count * width,
            transcendentals=0,
        ),
    )(hidden, w_down, spread)


axes = ("expert", "dp")


def pairs_of(expert_pairs, dp_pairs, dp_size):
    return [
        (e_from * dp_size + d_from, e_to * dp_size + d_to)
        for e_from, e_to in expert_pairs
        for d_from, d_to in dp_pairs
    ]


stay_z = [(i, i) for i in range(4)]
stay_dp = [(i, i) for i in range(4)]
swap_z = pairs_of([(0, 1), (1, 0), (2, 3), (3, 2)], stay_dp, 4)
middle_z = pairs_of([(1, 2), (2, 1)], stay_dp, 4)
outward_z = pairs_of([(1, 0), (2, 3)], stay_dp, 4)
inward_z = pairs_of([(0, 1), (3, 2)], stay_dp, 4)
swap_x = pairs_of(stay_z, [(0, 2), (2, 0), (1, 3), (3, 1)], 4)
swap_core = pairs_of(stay_z, [(0, 1), (1, 0), (2, 3), (3, 2)], 4)


def send(value, pairs):
    return lax.ppermute(value, axes, pairs)


def together(*values):
    return lax.optimization_barrier(values)


def tree_start(own):
    near, middle, own_x = together(
        send(own, swap_z), send(own, middle_z), send(own, swap_x)
    )
    return near, middle, own_x


def tree_second(near, middle, *others):
    return together(
        send(near, middle_z), send(middle, outward_z), send(near, swap_x), *others
    )


def tree_third(cross, outer, middle, edge, *others):
    third = jnp.where(edge, outer, middle)
    far, third_x, *others = together(send(cross, outward_z), send(third, swap_x), *others)
    return third, third_x, jnp.where(edge, far, cross), *others


def tree_rest(early, fourth, mine, theirs, experts):
    mine_rows, theirs_rows, fourth_x = together(
        *pick_pair(early, mine, theirs, experts), send(fourth, swap_x)
    )
    late = [fourth, fourth_x]
    rows = [mine_rows, send(theirs_rows, swap_core)]
    return rows, late + [send(block, swap_core) for block in late]


def chip_sums(mine, theirs):
    return rounded_sum(mine, send(theirs, swap_core))


def tree_return(chip):
    own, near, third, own_x, near_x, third_x, fourth, fourth_x = [chip[i] for i in range(8)]
    fourth_in, third_x, near_x, own_x = together(send(fourth_x, swap_x), third_x, near_x, own_x)
    fourth = rounded_sum(fourth, fourth_in)
    far, third_in, near_x, own_x = together(
        send(fourth, inward_z), send(third_x, swap_x), near_x, own_x
    )
    cross = rounded_sum(fourth, far)
    third = rounded_sum(third, third_in)
    outer, crossed, near_in, own_x = together(
        send(third, inward_z), send(cross, middle_z), send(near_x, swap_x), own_x
    )
    middle = rounded_sum(third, outer)
    near = rounded_sum(near, near_in, crossed)
    return rounded_sum(
        own, send(own_x, swap_x), send(middle, middle_z), send(near, swap_z)
    )


def slot_sources():
    z = lax.axis_index("expert")
    dp = lax.axis_index("dp")
    x, core = dp // 2, dp % 2
    low = z < 2
    column = jnp.stack([z, z ^ 1, jnp.where(low, 2, 1), jnp.where(low, 3, 0)])
    early = jnp.array([0, 1, 2, 0, 1, 2]), jnp.array([0, 0, 0, 1, 1, 1])
    late = jnp.array([3, 3]), jnp.array([0, 1])

    def device(which, core_of):
        return column[which[0]] * 4 + (x ^ which[1]) * 2 + core_of

    return jnp.concatenate(
        [device(early, core), device(early, 1 - core), device(late, core), device(late, 1 - core)]
    )


def shards(tokens, routes, route_weight, norm_gain, w_gate, w_up, w_down):
    token_count, top_count = routes.shape
    feature_dim = tokens.shape[1]
    expert_size = lax.axis_size("expert")
    dp_size = lax.axis_size("dp")
    device_count = expert_size * dp_size
    local_count = w_gate.shape[0]
    as_tree = expert_size == 4 and dp_size == 4
    edge = (lax.axis_index("expert") % 3) == 0

    as_float = tokens.astype(jnp.float32)
    normed = (
        as_float
        * lax.rsqrt(jnp.mean(as_float * as_float, axis=-1, keepdims=True) + 1e-06)
        * norm_gain
    ).astype(jnp.bfloat16)

    every = jnp.arange(device_count * local_count, dtype=jnp.int32)
    same = routes[:, :, None] == every
    named = jnp.any(same, axis=1)
    named_weight = jnp.sum(jnp.where(same, route_weight[:, :, None], 0.0), axis=1)
    before = (jnp.arange(token_count)[:, None] > jnp.arange(token_count)[None, :]).astype(
        jnp.bfloat16
    )
    rank = jnp.dot(before, named.astype(jnp.bfloat16), preferred_element_type=jnp.float32)
    rank = jnp.where(named, rank, -1.0)
    choice = jnp.stack([rank.T, named_weight.T]).reshape(2, device_count, local_count, token_count)
    choice = choice.transpose(1, 0, 2, 3).reshape(device_count, 2 * local_count, token_count)
    choices = lax.all_to_all(choice, axes, split_axis=0, concat_axis=0, tiled=True)

    width = feature_dim // gather_chunks
    parts = [normed[:, chunk * width : (chunk + 1) * width] for chunk in range(gather_chunks)]
    if as_tree:
        firsts = [tree_start(part) for part in parts]
        seconds = []
        for near, middle, own_x in firsts:
            cross, outer, near_x, choices = tree_second(near, middle, choices)
            seconds.append((cross, outer, near_x))
        mine, theirs, late_picker, spread, scale = tables(slot_sources(), choices, local_count)
        theirs = send(theirs, swap_core)
        thirds = []
        for (near, middle, own_x), (cross, outer, near_x) in zip(firsts, seconds):
            third, third_x, fourth, theirs = tree_third(cross, outer, middle, edge, theirs)
            thirds.append((third, third_x, fourth))
        order = (0, 1, 2, 3, 4, 5, 8, 9, 10, 11, 12, 13, 6, 7, 14, 15)
        row_chunks, late_chunks = [], []
        for part, (near, middle, own_x), (cross, outer, near_x), (third, third_x, fourth) in zip(
            parts, firsts, seconds, thirds
        ):
            early = part, near, third, own_x, near_x, third_x
            rows, late = tree_rest(early, fourth, mine, theirs, local_count)
            row_chunks.append([rows_of.reshape(local_count, -1, width) for rows_of in rows])
            late_chunks.append(late)
    else:
        rank, named_weight = choices[:, :local_count], choices[:, local_count:]
        match = rank[:, :, None, :] == jnp.arange(slots, dtype=jnp.float32)[None, None, :, None]
        picker = match.astype(jnp.bfloat16).reshape(device_count, local_count * slots, token_count)
        scale = jnp.sum(jnp.where(match, named_weight[:, :, None, :], 0.0), axis=3)
        scale = scale.transpose(1, 0, 2).reshape(local_count, device_count * slots, 1)
        spread = picker.transpose(0, 2, 1)
        rows = [pick_rows(picker, lax.all_gather(part, axes), local_count) for part in parts]
        row_chunks = [[rows_of.reshape(local_count, -1, width)] for rows_of in rows]
        late_chunks, late_picker = [[]] * gather_chunks, None
        order = tuple(range(device_count))
    hidden = hidden_rows(row_chunks, late_chunks, late_picker, scale, w_gate, w_up)

    sums = []
    for chunk in range(return_chunks):
        mine, theirs = mix_rows(hidden, w_down, spread, order, chunk, return_chunks)
        if as_tree:
            sums.append(chip_sums(mine, theirs))
        else:
            whole = jnp.concatenate([mine, theirs], axis=0).astype(jnp.float32)
            total = lax.psum_scatter(whole, axes, scatter_dimension=0)
            sums.append(total.astype(jnp.bfloat16))
    results = [tree_return(chip) for chip in sums] if as_tree else sums
    return jnp.concatenate(results, axis=1)


def solution(mesh):
    split = P(("groups", "expert", "dp"), None)
    by_expert = P(("expert", "dp"), None, None)
    return jax.shard_map(
        shards,
        mesh=mesh,
        in_specs=(split, split, split, P(), by_expert, by_expert, by_expert),
        out_specs=split,
        check_vma=False,
    )
```

```python
import functools

import jax
import jax.numpy as jnp
from jax import lax
from jax.experimental import pallas as pl
from jax.experimental.pallas import tpu as pltpu
from jax.sharding import PartitionSpec as P

slots = 16
gather_chunks = 2
return_chunks = 2
mebi = 1024 * 1024


def grant(sources, tree_mebi):
    return (tree_mebi if sources <= 16 else 56) * mebi


def rounded_sum(first, *others):
    total = first.astype(jnp.float32)
    for other in others:
        total = total + other.astype(jnp.float32)
    return total.astype(jnp.bfloat16)


def pick_kernel(picker_ref, tokens_ref, rows_ref):
    sources = tokens_ref.shape[0]
    experts = rows_ref.shape[0]
    for source in range(sources):
        picked = jnp.dot(
            picker_ref[source], tokens_ref[source], preferred_element_type=jnp.float32
        ).astype(jnp.bfloat16)
        for expert in range(experts):
            rows_ref[expert, source] = picked[expert * slots : (expert + 1) * slots]


def pick_rows(picker, tokens, experts):
    sources, token_count, width = tokens.shape
    block = min(sources, 8)
    return pl.pallas_call(
        pick_kernel,
        grid=(sources // block,),
        in_specs=[
            pl.BlockSpec((block, experts * slots, token_count), lambda i: (i, 0, 0)),
            pl.BlockSpec((block, token_count, width), lambda i: (i, 0, 0)),
        ],
        out_specs=pl.BlockSpec((experts, block, slots, width), lambda i: (0, i, 0, 0)),
        out_shape=jax.ShapeDtypeStruct((experts, sources, slots, width), jnp.bfloat16),
        compiler_params=pltpu.CompilerParams(vmem_limit_bytes=grant(sources, 16)),
        cost_estimate=pl.CostEstimate(
            flops=2 * sources * experts * slots * token_count * width,
            bytes_accessed=2 * sources * width * (token_count + experts * slots),
            transcendentals=0,
        ),
    )(picker, tokens)


def norm_kernel(tokens_ref, gain_ref, *part_refs):
    as_float = tokens_ref[...].astype(jnp.float32)
    mean = jnp.mean(as_float * as_float, axis=-1, keepdims=True)
    normed = (as_float * lax.rsqrt(mean + 1e-06) * gain_ref[...]).astype(jnp.bfloat16)
    width = part_refs[0].shape[1]
    for chunk, part_ref in enumerate(part_refs):
        part_ref[...] = normed[:, chunk * width : (chunk + 1) * width]


def normed_parts(tokens, norm_gain, chunks):
    token_count, feature_dim = tokens.shape
    part = jax.ShapeDtypeStruct((token_count, feature_dim // chunks), jnp.bfloat16)
    return pl.pallas_call(
        norm_kernel,
        in_specs=[pl.BlockSpec(memory_space=pltpu.VMEM)] * 2,
        out_specs=[pl.BlockSpec(memory_space=pltpu.VMEM)] * chunks,
        out_shape=[part] * chunks,
        compiler_params=pltpu.CompilerParams(vmem_limit_bytes=16 * mebi),
    )(tokens, norm_gain.reshape(1, feature_dim))


def table_kernel(source_ref, choices_ref, *refs):
    picker_refs, spread_ref, scale_ref = refs[:3], refs[3], refs[4]
    experts = scale_ref.shape[0]
    token_count = choices_ref.shape[2]
    early, late = picker_refs[0].shape[0], picker_refs[2].shape[0] // 2
    place = lax.broadcasted_iota(jnp.int32, (experts, slots, token_count), 1).astype(jnp.float32)
    for slot in range(2 * (early + late)):
        choice = choices_ref[source_ref[slot]]
        match = choice[:experts][:, None, :] == place
        weight = jnp.where(match, choice[experts:][:, None, :], 0.0)
        scale_ref[:, slot * slots : (slot + 1) * slots, :] = jnp.sum(weight, axis=2, keepdims=True)
        picker = jnp.where(match, 1.0, 0.0).reshape(experts * slots, token_count)
        if slot < 2 * early:
            picker_refs[slot // early][slot % early] = picker.astype(jnp.bfloat16)
        else:
            picker_refs[2][slot - 2 * early] = picker.astype(jnp.bfloat16)
        spread_ref[slot] = picker.T.astype(jnp.bfloat16)


def tables(source, choices, experts):
    count, _, token_count = choices.shape
    rows = experts * slots
    late = count // 8
    early = count // 2 - late
    shapes = [(early, rows, token_count), (early, rows, token_count), (2 * late, rows, token_count)]
    shapes = [jax.ShapeDtypeStruct(shape, jnp.bfloat16) for shape in shapes]
    shapes.append(jax.ShapeDtypeStruct((count, token_count, rows), jnp.bfloat16))
    shapes.append(jax.ShapeDtypeStruct((experts, count * slots, 1), jnp.float32))
    return pl.pallas_call(
        table_kernel,
        in_specs=[
            pl.BlockSpec(memory_space=pltpu.SMEM),
            pl.BlockSpec(memory_space=pltpu.VMEM),
        ],
        out_specs=[pl.BlockSpec(memory_space=pltpu.VMEM)] * 5,
        out_shape=shapes,
        compiler_params=pltpu.CompilerParams(vmem_limit_bytes=grant(count, 12)),
    )(source, choices)


def pair_kernel(count, *refs):
    token_refs = refs[:count]
    mine_ref, theirs_ref, mine_rows_ref, theirs_rows_ref = refs[count:]
    experts = mine_rows_ref.shape[0]
    for source in range(count):
        for picker_ref, rows_ref in ((mine_ref, mine_rows_ref), (theirs_ref, theirs_rows_ref)):
            picked = jnp.dot(
                picker_ref[source], token_refs[source][...], preferred_element_type=jnp.float32
            ).astype(jnp.bfloat16)
            rows_ref[:, source] = picked.reshape(experts, slots, picked.shape[1])


def pick_pair(blocks, mine, theirs, experts):
    count = len(blocks)
    token_count, width = blocks[0].shape
    rows = jax.ShapeDtypeStruct((experts, count, slots, width), jnp.bfloat16)
    return pl.pallas_call(
        functools.partial(pair_kernel, count),
        in_specs=[pl.BlockSpec(memory_space=pltpu.VMEM)] * (count + 2),
        out_specs=[pl.BlockSpec(memory_space=pltpu.VMEM)] * 2,
        out_shape=[rows, rows],
        compiler_params=pltpu.CompilerParams(vmem_limit_bytes=grant(count, 16)),
        cost_estimate=pl.CostEstimate(
            flops=4 * count * experts * slots * token_count * width,
            bytes_accessed=2 * count * width * (token_count + 2 * experts * slots),
            transcendentals=0,
        ),
    )(*blocks, mine, theirs)


def hidden_kernel(chunks, groups, late, *refs):
    row_refs = refs[: chunks * groups]
    refs = refs[chunks * groups :]
    late_refs = refs[: chunks * late]
    refs = refs[chunks * late :]
    width = row_refs[0].shape[-1]
    if late:
        picker_ref, scale_ref, gate_ref, up_ref, hidden_ref, late_rows = refs

        @pl.when(pl.program_id(0) == 0)
        def _():
            for chunk in range(chunks):
                for source in range(late):
                    picked = jnp.dot(
                        picker_ref[source],
                        late_refs[chunk * late + source][...],
                        preferred_element_type=jnp.float32,
                    ).astype(jnp.bfloat16)
                    late_rows[:, source, :, chunk * width : (chunk + 1) * width] = picked.reshape(
                        late_rows.shape[0], slots, width
                    )

    else:
        scale_ref, gate_ref, up_ref, hidden_ref = refs
    gate_part = None
    for chunk in range(chunks):
        pieces = [ref[0] for ref in row_refs[chunk * groups : (chunk + 1) * groups]]
        if late:
            extra = late_rows[pl.program_id(0), :, :, chunk * width : (chunk + 1) * width]
            pieces.append(extra.reshape(late * slots, width))
        rows = jnp.concatenate(pieces, axis=0)
        depth = pl.ds(chunk * width, width)
        gate_add = jnp.dot(rows, gate_ref[0, depth, :], preferred_element_type=jnp.float32)
        up_add = jnp.dot(rows, up_ref[0, depth, :], preferred_element_type=jnp.float32)
        if gate_part is None:
            gate_part, up_part = gate_add, up_add
        else:
            gate_part, up_part = gate_part + gate_add, up_part + up_add
    hidden = gate_part / (1.0 + jnp.exp(-gate_part)) * up_part * scale_ref[0]
    hidden_ref[0] = hidden.astype(jnp.bfloat16)


def hidden_rows(row_chunks, late_chunks, late_picker, scale, w_gate, w_up):
    experts, feature_dim, hidden_dim = w_gate.shape
    chunks, groups, late = len(row_chunks), len(row_chunks[0]), len(late_chunks[0])
    pieces = [piece for row_groups in row_chunks for piece in row_groups]
    late_pieces = [piece for blocks in late_chunks for piece in blocks]
    scratch = []
    if late:
        late_pieces.append(late_picker)
        scratch = [pltpu.VMEM((experts, late, slots, feature_dim), jnp.bfloat16)]
    whole = scale.shape[1]
    return pl.pallas_call(
        functools.partial(hidden_kernel, chunks, groups, late),
        grid=(experts,),
        in_specs=[pl.BlockSpec((1,) + piece.shape[1:], lambda e: (e, 0, 0)) for piece in pieces]
        + [pl.BlockSpec(memory_space=pltpu.VMEM)] * len(late_pieces)
        + [
            pl.BlockSpec((1, whole, 1), lambda e: (e, 0, 0)),
            pl.BlockSpec((1, feature_dim, hidden_dim), lambda e: (e, 0, 0)),
            pl.BlockSpec((1, feature_dim, hidden_dim), lambda e: (e, 0, 0)),
        ],
        out_specs=pl.BlockSpec((1, whole, hidden_dim), lambda e: (e, 0, 0)),
        out_shape=jax.ShapeDtypeStruct((experts, whole, hidden_dim), jnp.bfloat16),
        scratch_shapes=scratch,
        compiler_params=pltpu.CompilerParams(vmem_limit_bytes=grant(whole // slots, 32)),
        cost_estimate=pl.CostEstimate(
            flops=4 * experts * whole * feature_dim * hidden_dim,
            bytes_accessed=4 * experts * feature_dim * hidden_dim,
            transcendentals=experts * whole * hidden_dim,
        ),
    )(*pieces, *late_pieces, scale, w_gate, w_up)


def mix_kernel(order, hidden_ref, down_ref, spread_ref, first_ref, second_ref, made):
    step = pl.program_id(0)
    group = hidden_ref.shape[0]
    sources = spread_ref.shape[0]
    width = down_ref.shape[2]
    for one in range(group):
        made[step * group + one] = (
            jnp.dot(hidden_ref[one], down_ref[one], preferred_element_type=jnp.float32)
            .astype(jnp.bfloat16)
            .reshape(sources, slots, width)
        )

    @pl.when(step == pl.num_programs(0) - 1)
    def _():
        for source in range(sources):
            rows = made[:, source].reshape(spread_ref.shape[2], width)
            mixed = jnp.dot(
                spread_ref[source], rows, preferred_element_type=jnp.float32
            ).astype(jnp.bfloat16)
            if order[source] < sources // 2:
                first_ref[order[source]] = mixed
            else:
                second_ref[order[source] - sources // 2] = mixed


def mix_rows(hidden, w_down, spread, order, chunk, chunks):
    experts, whole, hidden_dim = hidden.shape
    width = w_down.shape[2] // chunks
    sources, token_count, local_rows = spread.shape
    group = 2 if experts % 2 == 0 else 1
    half = jax.ShapeDtypeStruct((sources // 2, token_count, width), jnp.bfloat16)
    return pl.pallas_call(
        functools.partial(mix_kernel, order),
        grid=(experts // group,),
        in_specs=[
            pl.BlockSpec((group, whole, hidden_dim), lambda e: (e, 0, 0)),
            pl.BlockSpec((group, hidden_dim, width), lambda e: (e, 0, chunk)),
            pl.BlockSpec(memory_space=pltpu.VMEM),
        ],
        out_specs=[pl.BlockSpec(memory_space=pltpu.VMEM)] * 2,
        out_shape=[half, half],
        scratch_shapes=[pltpu.VMEM((experts, sources, slots, width), jnp.bfloat16)],
        compiler_params=pltpu.CompilerParams(vmem_limit_bytes=grant(sources, 28)),
        cost_estimate=pl.CostEstimate(
            flops=2 * experts * whole * hidden_dim * width
            + 2 * sources * token_count * local_rows * width,
            bytes_accessed=2 * experts * hidden_dim * (width + whole)
            + 2 * sources * token_count * width,
            transcendentals=0,
        ),
    )(hidden, w_down, spread)


axes = ("expert", "dp")


def pairs_of(expert_pairs, dp_pairs, dp_size):
    return [
        (e_from * dp_size + d_from, e_to * dp_size + d_to)
        for e_from, e_to in expert_pairs
        for d_from, d_to in dp_pairs
    ]


stay_z = [(i, i) for i in range(4)]
stay_dp = [(i, i) for i in range(4)]
swap_z = pairs_of([(0, 1), (1, 0), (2, 3), (3, 2)], stay_dp, 4)
middle_z = pairs_of([(1, 2), (2, 1)], stay_dp, 4)
outward_z = pairs_of([(1, 0), (2, 3)], stay_dp, 4)
inward_z = pairs_of([(0, 1), (3, 2)], stay_dp, 4)
swap_x = pairs_of(stay_z, [(0, 2), (2, 0), (1, 3), (3, 1)], 4)
swap_core = pairs_of(stay_z, [(0, 1), (1, 0), (2, 3), (3, 2)], 4)


def send(value, pairs):
    return lax.ppermute(value, axes, pairs)


def together(*values):
    return lax.optimization_barrier(values)


def tree_start(own):
    near, middle, own_x = together(
        send(own, swap_z), send(own, middle_z), send(own, swap_x)
    )
    return near, middle, own_x


def tree_second(near, middle, *others):
    return together(
        send(near, middle_z), send(middle, outward_z), send(near, swap_x), *others
    )


def tree_third(cross, outer, middle, edge, *others):
    third = jnp.where(edge, outer, middle)
    far, third_x, *others = together(send(cross, outward_z), send(third, swap_x), *others)
    return third, third_x, jnp.where(edge, far, cross), *others


def tree_rest(early, fourth, mine, theirs, experts):
    mine_rows, theirs_rows = pick_pair(early, mine, theirs, experts)
    fourth_x, theirs_rows = together(send(fourth, swap_x), send(theirs_rows, swap_core))
    late = [fourth, fourth_x]
    return [mine_rows, theirs_rows], late + [send(block, swap_core) for block in late]


def chip_sums(mine, theirs):
    return rounded_sum(mine, send(theirs, swap_core))


def tree_return(chip):
    own, near, third, own_x, near_x, third_x, fourth, fourth_x = [chip[i] for i in range(8)]
    fourth_in, third_x, near_x, own_x = together(send(fourth_x, swap_x), third_x, near_x, own_x)
    fourth = rounded_sum(fourth, fourth_in)
    far, third_in, near_x, own_x = together(
        send(fourth, inward_z), send(third_x, swap_x), near_x, own_x
    )
    cross = rounded_sum(fourth, far)
    third = rounded_sum(third, third_in)
    outer, crossed, near_in, own_x = together(
        send(third, inward_z), send(cross, middle_z), send(near_x, swap_x), own_x
    )
    middle = rounded_sum(third, outer)
    near = rounded_sum(near, near_in, crossed)
    return rounded_sum(
        own, send(own_x, swap_x), send(middle, middle_z), send(near, swap_z)
    )


def slot_sources():
    z = lax.axis_index("expert")
    dp = lax.axis_index("dp")
    x, core = dp // 2, dp % 2
    low = z < 2
    column = jnp.stack([z, z ^ 1, jnp.where(low, 2, 1), jnp.where(low, 3, 0)])
    early = jnp.array([0, 1, 2, 0, 1, 2]), jnp.array([0, 0, 0, 1, 1, 1])
    late = jnp.array([3, 3]), jnp.array([0, 1])

    def device(which, core_of):
        return column[which[0]] * 4 + (x ^ which[1]) * 2 + core_of

    return jnp.concatenate(
        [device(early, core), device(early, 1 - core), device(late, core), device(late, 1 - core)]
    )


def shards(tokens, routes, route_weight, norm_gain, w_gate, w_up, w_down):
    token_count, top_count = routes.shape
    feature_dim = tokens.shape[1]
    expert_size = lax.axis_size("expert")
    dp_size = lax.axis_size("dp")
    device_count = expert_size * dp_size
    local_count = w_gate.shape[0]
    as_tree = expert_size == 4 and dp_size == 4
    edge = (lax.axis_index("expert") % 3) == 0

    width = feature_dim // gather_chunks
    parts = normed_parts(tokens, norm_gain, gather_chunks)
    every = jnp.arange(device_count * local_count, dtype=jnp.int32)
    same = routes[:, :, None] == every
    named = jnp.any(same, axis=1)
    named_weight = jnp.sum(jnp.where(same, route_weight[:, :, None], 0.0), axis=1)
    before = (jnp.arange(token_count)[:, None] > jnp.arange(token_count)[None, :]).astype(
        jnp.bfloat16
    )
    rank = jnp.dot(before, named.astype(jnp.bfloat16), preferred_element_type=jnp.float32)
    rank = jnp.where(named, rank, -1.0)
    choice = jnp.stack([rank.T, named_weight.T]).reshape(2, device_count, local_count, token_count)
    choice = choice.transpose(1, 0, 2, 3).reshape(device_count, 2 * local_count, token_count)
    if as_tree:
        firsts = [tree_start(part) for part in parts]
        near, middle, own_x = firsts[0]
        near, middle, own_x, choice = together(near, middle, own_x, choice)
        firsts[0] = near, middle, own_x
    choices = lax.all_to_all(choice, axes, split_axis=0, concat_axis=0, tiled=True)
    if as_tree:
        seconds = []
        for chunk, (near, middle, own_x) in enumerate(firsts):
            if chunk == 0:
                cross, outer, near_x, choices = tree_second(near, middle, choices)
            else:
                cross, outer, near_x = tree_second(near, middle)
            seconds.append((cross, outer, near_x))
        mine, theirs, late_picker, spread, scale = tables(slot_sources(), choices, local_count)
        theirs = send(theirs, swap_core)
        thirds = []
        for (near, middle, own_x), (cross, outer, near_x) in zip(firsts, seconds):
            if not thirds:
                third, third_x, fourth, theirs = tree_third(cross, outer, middle, edge, theirs)
            else:
                third, third_x, fourth = tree_third(cross, outer, middle, edge)
            thirds.append((third, third_x, fourth))
        order = (0, 1, 2, 3, 4, 5, 8, 9, 10, 11, 12, 13, 6, 7, 14, 15)
        row_chunks, late_chunks = [], []
        for part, (near, middle, own_x), (cross, outer, near_x), (third, third_x, fourth) in zip(
            parts, firsts, seconds, thirds
        ):
            early = part, near, third, own_x, near_x, third_x
            rows, late = tree_rest(early, fourth, mine, theirs, local_count)
            row_chunks.append([rows_of.reshape(local_count, -1, width) for rows_of in rows])
            late_chunks.append(late)
    else:
        rank, named_weight = choices[:, :local_count], choices[:, local_count:]
        match = rank[:, :, None, :] == jnp.arange(slots, dtype=jnp.float32)[None, None, :, None]
        picker = match.astype(jnp.bfloat16).reshape(device_count, local_count * slots, token_count)
        scale = jnp.sum(jnp.where(match, named_weight[:, :, None, :], 0.0), axis=3)
        scale = scale.transpose(1, 0, 2).reshape(local_count, device_count * slots, 1)
        spread = picker.transpose(0, 2, 1)
        rows = [pick_rows(picker, lax.all_gather(part, axes), local_count) for part in parts]
        row_chunks = [[rows_of.reshape(local_count, -1, width)] for rows_of in rows]
        late_chunks, late_picker = [[]] * gather_chunks, None
        order = tuple(range(device_count))
    hidden = hidden_rows(row_chunks, late_chunks, late_picker, scale, w_gate, w_up)

    sums = []
    for chunk in range(return_chunks):
        mine, theirs = mix_rows(hidden, w_down, spread, order, chunk, return_chunks)
        if as_tree:
            sums.append(chip_sums(mine, theirs))
        else:
            whole = jnp.concatenate([mine, theirs], axis=0).astype(jnp.float32)
            total = lax.psum_scatter(whole, axes, scatter_dimension=0)
            sums.append(total.astype(jnp.bfloat16))
    results = [tree_return(chip) for chip in sums] if as_tree else sums
    return jnp.concatenate(results, axis=1)


def solution(mesh):
    split = P(("groups", "expert", "dp"), None)
    by_expert = P(("expert", "dp"), None, None)
    return jax.shard_map(
        shards,
        mesh=mesh,
        in_specs=(split, split, split, P(), by_expert, by_expert, by_expert),
        out_specs=split,
        check_vma=False,
    )
```

```python
import functools

import jax
import jax.numpy as jnp
from jax import lax
from jax.experimental import pallas as pl
from jax.experimental.pallas import tpu as pltpu
from jax.sharding import PartitionSpec as P

slots = 16
gather_chunks = 2
return_chunks = 2
mebi = 1024 * 1024


def grant(sources, tree_mebi):
    return (tree_mebi if sources <= 16 else 56) * mebi


def rounded_sum(first, *others):
    total = first.astype(jnp.float32)
    for other in others:
        total = total + other.astype(jnp.float32)
    return total.astype(jnp.bfloat16)


def pick_kernel(picker_ref, tokens_ref, rows_ref):
    sources = tokens_ref.shape[0]
    experts = rows_ref.shape[0]
    for source in range(sources):
        picked = jnp.dot(
            picker_ref[source], tokens_ref[source], preferred_element_type=jnp.float32
        ).astype(jnp.bfloat16)
        for expert in range(experts):
            rows_ref[expert, source] = picked[expert * slots : (expert + 1) * slots]


def pick_rows(picker, tokens, experts):
    sources, token_count, width = tokens.shape
    block = min(sources, 8)
    return pl.pallas_call(
        pick_kernel,
        grid=(sources // block,),
        in_specs=[
            pl.BlockSpec((block, experts * slots, token_count), lambda i: (i, 0, 0)),
            pl.BlockSpec((block, token_count, width), lambda i: (i, 0, 0)),
        ],
        out_specs=pl.BlockSpec((experts, block, slots, width), lambda i: (0, i, 0, 0)),
        out_shape=jax.ShapeDtypeStruct((experts, sources, slots, width), jnp.bfloat16),
        compiler_params=pltpu.CompilerParams(vmem_limit_bytes=grant(sources, 16)),
        cost_estimate=pl.CostEstimate(
            flops=2 * sources * experts * slots * token_count * width,
            bytes_accessed=2 * sources * width * (token_count + experts * slots),
            transcendentals=0,
        ),
    )(picker, tokens)


def rank_kernel(routes_ref, weight_ref, choice_ref):
    top_count, token_count = routes_ref.shape
    devices, experts = choice_ref.shape[0], choice_ref.shape[1] // 2
    shape = devices * experts, token_count
    every = lax.broadcasted_iota(jnp.int32, shape, 0)
    named, weight = jnp.zeros(shape, jnp.float32), jnp.zeros(shape, jnp.float32)
    for k in range(top_count):
        same = routes_ref[k : k + 1, :] == every
        named = jnp.where(same, 1.0, named)
        weight = jnp.where(same, weight_ref[k : k + 1, :], weight)
    square = token_count, token_count
    before = lax.broadcasted_iota(jnp.int32, square, 0) < lax.broadcasted_iota(jnp.int32, square, 1)
    before = jnp.where(before, 1.0, 0.0).astype(jnp.bfloat16)
    rank = jnp.dot(named.astype(jnp.bfloat16), before, preferred_element_type=jnp.float32)
    rank = jnp.where(named > 0.0, rank, -1.0)
    choice_ref[:, :experts] = rank.reshape(devices, experts, token_count)
    choice_ref[:, experts:] = weight.reshape(devices, experts, token_count)


def ranked(routes, route_weight, devices, experts):
    token_count = routes.shape[0]
    return pl.pallas_call(
        rank_kernel,
        in_specs=[pl.BlockSpec(memory_space=pltpu.VMEM)] * 2,
        out_specs=pl.BlockSpec(memory_space=pltpu.VMEM),
        out_shape=jax.ShapeDtypeStruct((devices, 2 * experts, token_count), jnp.float32),
        compiler_params=pltpu.CompilerParams(vmem_limit_bytes=8 * mebi),
    )(routes.T, route_weight.T)


def norm_kernel(tokens_ref, gain_ref, *part_refs):
    as_float = tokens_ref[...].astype(jnp.float32)
    mean = jnp.mean(as_float * as_float, axis=-1, keepdims=True)
    normed = (as_float * lax.rsqrt(mean + 1e-06) * gain_ref[...]).astype(jnp.bfloat16)
    width = part_refs[0].shape[1]
    for chunk, part_ref in enumerate(part_refs):
        part_ref[...] = normed[:, chunk * width : (chunk + 1) * width]


def normed_parts(tokens, norm_gain, chunks):
    token_count, feature_dim = tokens.shape
    part = jax.ShapeDtypeStruct((token_count, feature_dim // chunks), jnp.bfloat16)
    return pl.pallas_call(
        norm_kernel,
        in_specs=[pl.BlockSpec(memory_space=pltpu.VMEM)] * 2,
        out_specs=[pl.BlockSpec(memory_space=pltpu.VMEM)] * chunks,
        out_shape=[part] * chunks,
        compiler_params=pltpu.CompilerParams(vmem_limit_bytes=16 * mebi),
    )(tokens, norm_gain.reshape(1, feature_dim))


def slot_sources(z, dp):
    low = z < 2
    column = z, z ^ 1, jnp.where(low, 2, 1), jnp.where(low, 3, 0)
    early = [(column[i], side) for side in (0, 2) for i in range(3)]
    late = [(column[3], side) for side in (0, 2)]
    return [
        from_z * 4 + (dp ^ (side + core))
        for group in (early, late)
        for core in (0, 1)
        for from_z, side in group
    ]


def table_kernel(place_ref, choices_ref, *refs):
    picker_refs, spread_ref, scale_ref = refs[:3], refs[3], refs[4]
    experts = scale_ref.shape[0]
    token_count = choices_ref.shape[2]
    early, late = picker_refs[0].shape[0], picker_refs[2].shape[0] // 2
    place = lax.broadcasted_iota(jnp.int32, (experts, slots, token_count), 1).astype(jnp.float32)
    sources = slot_sources(place_ref[0], place_ref[1])
    for slot, source in enumerate(sources):
        choice = choices_ref[source]
        match = choice[:experts][:, None, :] == place
        weight = jnp.where(match, choice[experts:][:, None, :], 0.0)
        scale_ref[:, slot * slots : (slot + 1) * slots, :] = jnp.sum(weight, axis=2, keepdims=True)
        picker = jnp.where(match, 1.0, 0.0).reshape(experts * slots, token_count)
        if slot < 2 * early:
            picker_refs[slot // early][slot % early] = picker.astype(jnp.bfloat16)
        else:
            picker_refs[2][slot - 2 * early] = picker.astype(jnp.bfloat16)
        spread_ref[slot] = picker.T.astype(jnp.bfloat16)


def tables(place, choices, experts):
    count, _, token_count = choices.shape
    rows = experts * slots
    late = count // 8
    early = count // 2 - late
    shapes = [(early, rows, token_count), (early, rows, token_count), (2 * late, rows, token_count)]
    shapes = [jax.ShapeDtypeStruct(shape, jnp.bfloat16) for shape in shapes]
    shapes.append(jax.ShapeDtypeStruct((count, token_count, rows), jnp.bfloat16))
    shapes.append(jax.ShapeDtypeStruct((experts, count * slots, 1), jnp.float32))
    return pl.pallas_call(
        table_kernel,
        in_specs=[
            pl.BlockSpec(memory_space=pltpu.SMEM),
            pl.BlockSpec(memory_space=pltpu.VMEM),
        ],
        out_specs=[pl.BlockSpec(memory_space=pltpu.VMEM)] * 5,
        out_shape=shapes,
        compiler_params=pltpu.CompilerParams(vmem_limit_bytes=grant(count, 12)),
    )(place, choices)


def pair_kernel(count, *refs):
    token_refs = refs[:count]
    mine_ref, theirs_ref, mine_rows_ref, theirs_rows_ref = refs[count:]
    experts = mine_rows_ref.shape[0]
    for source in range(count):
        for picker_ref, rows_ref in ((mine_ref, mine_rows_ref), (theirs_ref, theirs_rows_ref)):
            picked = jnp.dot(
                picker_ref[source], token_refs[source][...], preferred_element_type=jnp.float32
            ).astype(jnp.bfloat16)
            rows_ref[:, source] = picked.reshape(experts, slots, picked.shape[1])


def pick_pair(blocks, mine, theirs, experts):
    count = len(blocks)
    token_count, width = blocks[0].shape
    rows = jax.ShapeDtypeStruct((experts, count, slots, width), jnp.bfloat16)
    return pl.pallas_call(
        functools.partial(pair_kernel, count),
        in_specs=[pl.BlockSpec(memory_space=pltpu.VMEM)] * (count + 2),
        out_specs=[pl.BlockSpec(memory_space=pltpu.VMEM)] * 2,
        out_shape=[rows, rows],
        compiler_params=pltpu.CompilerParams(vmem_limit_bytes=grant(count, 16)),
        cost_estimate=pl.CostEstimate(
            flops=4 * count * experts * slots * token_count * width,
            bytes_accessed=2 * count * width * (token_count + 2 * experts * slots),
            transcendentals=0,
        ),
    )(*blocks, mine, theirs)


def hidden_kernel(chunks, groups, late, *refs):
    row_refs = refs[: chunks * groups]
    refs = refs[chunks * groups :]
    late_refs = refs[: chunks * late]
    refs = refs[chunks * late :]
    width = row_refs[0].shape[-1]
    if late:
        picker_ref, scale_ref, gate_ref, up_ref, hidden_ref, late_rows = refs

        @pl.when(pl.program_id(0) == 0)
        def _():
            for chunk in range(chunks):
                for source in range(late):
                    picked = jnp.dot(
                        picker_ref[source],
                        late_refs[chunk * late + source][...],
                        preferred_element_type=jnp.float32,
                    ).astype(jnp.bfloat16)
                    late_rows[:, source, :, chunk * width : (chunk + 1) * width] = picked.reshape(
                        late_rows.shape[0], slots, width
                    )

    else:
        scale_ref, gate_ref, up_ref, hidden_ref = refs
    gate_part = None
    for chunk in range(chunks):
        pieces = [ref[0] for ref in row_refs[chunk * groups : (chunk + 1) * groups]]
        if late:
            extra = late_rows[pl.program_id(0), :, :, chunk * width : (chunk + 1) * width]
            pieces.append(extra.reshape(late * slots, width))
        rows = jnp.concatenate(pieces, axis=0)
        depth = pl.ds(chunk * width, width)
        gate_add = jnp.dot(rows, gate_ref[0, depth, :], preferred_element_type=jnp.float32)
        up_add = jnp.dot(rows, up_ref[0, depth, :], preferred_element_type=jnp.float32)
        if gate_part is None:
            gate_part, up_part = gate_add, up_add
        else:
            gate_part, up_part = gate_part + gate_add, up_part + up_add
    hidden = gate_part / (1.0 + jnp.exp(-gate_part)) * up_part * scale_ref[0]
    hidden_ref[0] = hidden.astype(jnp.bfloat16)


def hidden_rows(row_chunks, late_chunks, late_picker, scale, w_gate, w_up):
    experts, feature_dim, hidden_dim = w_gate.shape
    chunks, groups, late = len(row_chunks), len(row_chunks[0]), len(late_chunks[0])
    pieces = [piece for row_groups in row_chunks for piece in row_groups]
    late_pieces = [piece for blocks in late_chunks for piece in blocks]
    scratch = []
    if late:
        late_pieces.append(late_picker)
        scratch = [pltpu.VMEM((experts, late, slots, feature_dim), jnp.bfloat16)]
    whole = scale.shape[1]
    return pl.pallas_call(
        functools.partial(hidden_kernel, chunks, groups, late),
        grid=(experts,),
        in_specs=[pl.BlockSpec((1,) + piece.shape[1:], lambda e: (e, 0, 0)) for piece in pieces]
        + [pl.BlockSpec(memory_space=pltpu.VMEM)] * len(late_pieces)
        + [
            pl.BlockSpec((1, whole, 1), lambda e: (e, 0, 0)),
            pl.BlockSpec((1, feature_dim, hidden_dim), lambda e: (e, 0, 0)),
            pl.BlockSpec((1, feature_dim, hidden_dim), lambda e: (e, 0, 0)),
        ],
        out_specs=pl.BlockSpec((1, whole, hidden_dim), lambda e: (e, 0, 0)),
        out_shape=jax.ShapeDtypeStruct((experts, whole, hidden_dim), jnp.bfloat16),
        scratch_shapes=scratch,
        compiler_params=pltpu.CompilerParams(vmem_limit_bytes=grant(whole // slots, 32)),
        cost_estimate=pl.CostEstimate(
            flops=4 * experts * whole * feature_dim * hidden_dim,
            bytes_accessed=4 * experts * feature_dim * hidden_dim,
            transcendentals=experts * whole * hidden_dim,
        ),
    )(*pieces, *late_pieces, scale, w_gate, w_up)


def mix_kernel(order, hidden_ref, down_ref, spread_ref, first_ref, second_ref, made):
    step = pl.program_id(0)
    group = hidden_ref.shape[0]
    sources = spread_ref.shape[0]
    width = down_ref.shape[2]
    for one in range(group):
        made[step * group + one] = (
            jnp.dot(hidden_ref[one], down_ref[one], preferred_element_type=jnp.float32)
            .astype(jnp.bfloat16)
            .reshape(sources, slots, width)
        )

    @pl.when(step == pl.num_programs(0) - 1)
    def _():
        for source in range(sources):
            rows = made[:, source].reshape(spread_ref.shape[2], width)
            mixed = jnp.dot(
                spread_ref[source], rows, preferred_element_type=jnp.float32
            ).astype(jnp.bfloat16)
            if order[source] < sources // 2:
                first_ref[order[source]] = mixed
            else:
                second_ref[order[source] - sources // 2] = mixed


def mix_rows(hidden, w_down, spread, order, chunk, chunks):
    experts, whole, hidden_dim = hidden.shape
    width = w_down.shape[2] // chunks
    sources, token_count, local_rows = spread.shape
    group = 2 if experts % 2 == 0 else 1
    half = jax.ShapeDtypeStruct((sources // 2, token_count, width), jnp.bfloat16)
    return pl.pallas_call(
        functools.partial(mix_kernel, order),
        grid=(experts // group,),
        in_specs=[
            pl.BlockSpec((group, whole, hidden_dim), lambda e: (e, 0, 0)),
            pl.BlockSpec((group, hidden_dim, width), lambda e: (e, 0, chunk)),
            pl.BlockSpec(memory_space=pltpu.VMEM),
        ],
        out_specs=[pl.BlockSpec(memory_space=pltpu.VMEM)] * 2,
        out_shape=[half, half],
        scratch_shapes=[pltpu.VMEM((experts, sources, slots, width), jnp.bfloat16)],
        compiler_params=pltpu.CompilerParams(vmem_limit_bytes=grant(sources, 28)),
        cost_estimate=pl.CostEstimate(
            flops=2 * experts * whole * hidden_dim * width
            + 2 * sources * token_count * local_rows * width,
            bytes_accessed=2 * experts * hidden_dim * (width + whole)
            + 2 * sources * token_count * width,
            transcendentals=0,
        ),
    )(hidden, w_down, spread)


axes = ("expert", "dp")


def pairs_of(expert_pairs, dp_pairs, dp_size):
    return [
        (e_from * dp_size + d_from, e_to * dp_size + d_to)
        for e_from, e_to in expert_pairs
        for d_from, d_to in dp_pairs
    ]


stay_z = [(i, i) for i in range(4)]
stay_dp = [(i, i) for i in range(4)]
swap_z = pairs_of([(0, 1), (1, 0), (2, 3), (3, 2)], stay_dp, 4)
middle_z = pairs_of([(1, 2), (2, 1)], stay_dp, 4)
outward_z = pairs_of([(1, 0), (2, 3)], stay_dp, 4)
inward_z = pairs_of([(0, 1), (3, 2)], stay_dp, 4)
swap_x = pairs_of(stay_z, [(0, 2), (2, 0), (1, 3), (3, 1)], 4)
swap_core = pairs_of(stay_z, [(0, 1), (1, 0), (2, 3), (3, 2)], 4)


def send(value, pairs):
    return lax.ppermute(value, axes, pairs)


def together(*values):
    return lax.optimization_barrier(values)


def tree_start(own):
    near, middle, own_x = together(
        send(own, swap_z), send(own, middle_z), send(own, swap_x)
    )
    return near, middle, own_x


def tree_second(near, middle, own_x, *others):
    if own_x is None:
        near_x = send(near, swap_x)
    else:
        near_x = send(own_x, swap_z)
    return together(send(near, middle_z), send(middle, outward_z), near_x, *others)


def tree_third(cross, outer, middle, edge, *others):
    third = jnp.where(edge, outer, middle)
    far, third_x, *others = together(send(cross, outward_z), send(third, swap_x), *others)
    return third, third_x, jnp.where(edge, far, cross), *others


def tree_rest(early, fourth, mine, theirs, experts):
    mine_rows, theirs_rows = pick_pair(early, mine, theirs, experts)
    fourth_x, theirs_rows = together(send(fourth, swap_x), send(theirs_rows, swap_core))
    late = [fourth, fourth_x]
    return [mine_rows, theirs_rows], late + [send(block, swap_core) for block in late]


def chip_sums(mine, theirs):
    return rounded_sum(mine, send(theirs, swap_core))


def tree_return(chip, near_by_z):
    own, near, third, own_x, near_x, third_x, fourth, fourth_x = [chip[i] for i in range(8)]
    if near_by_z:
        near_x = send(near_x, swap_z)
    fourth_in, third_x, near_x, own_x = together(send(fourth_x, swap_x), third_x, near_x, own_x)
    if near_by_z:
        own_x = rounded_sum(own_x, near_x)
    fourth = rounded_sum(fourth, fourth_in)
    far, third_in, near_x, own_x = together(
        send(fourth, inward_z), send(third_x, swap_x), near_x, own_x
    )
    cross = rounded_sum(fourth, far)
    third = rounded_sum(third, third_in)
    sent = [send(third, inward_z), send(cross, middle_z)]
    if not near_by_z:
        sent.append(send(near_x, swap_x))
    outer, crossed, *near_in, own_x = together(*sent, own_x)
    middle = rounded_sum(third, outer)
    near = rounded_sum(near, crossed, *near_in)
    return rounded_sum(
        own, send(own_x, swap_x), send(middle, middle_z), send(near, swap_z)
    )


def shards(tokens, routes, route_weight, norm_gain, w_gate, w_up, w_down):
    token_count, top_count = routes.shape
    feature_dim = tokens.shape[1]
    expert_size = lax.axis_size("expert")
    dp_size = lax.axis_size("dp")
    device_count = expert_size * dp_size
    local_count = w_gate.shape[0]
    as_tree = expert_size == 4 and dp_size == 4
    edge = (lax.axis_index("expert") % 3) == 0

    width = feature_dim // gather_chunks
    parts = normed_parts(tokens, norm_gain, gather_chunks)
    if as_tree:
        choice = ranked(routes, route_weight, device_count, local_count)
        firsts = [tree_start(part) for part in parts]
        seconds = [
            tree_second(near, middle, own_x if chunk % 2 else None, choice)
            for chunk, (near, middle, own_x) in enumerate(firsts)
        ]
        choice = seconds[0][3]
    else:
        every = jnp.arange(device_count * local_count, dtype=jnp.int32)
        same = routes[:, :, None] == every
        named = jnp.any(same, axis=1)
        named_weight = jnp.sum(jnp.where(same, route_weight[:, :, None], 0.0), axis=1)
        count = jnp.arange(token_count)
        before = (count[:, None] > count[None, :]).astype(jnp.bfloat16)
        rank = jnp.dot(before, named.astype(jnp.bfloat16), preferred_element_type=jnp.float32)
        rank = jnp.where(named, rank, -1.0)
        choice = jnp.stack([rank.T, named_weight.T])
        choice = choice.reshape(2, device_count, local_count, token_count).transpose(1, 0, 2, 3)
        choice = choice.reshape(device_count, 2 * local_count, token_count)
    choices = lax.all_to_all(choice, axes, split_axis=0, concat_axis=0, tiled=True)
    if as_tree:
        place = jnp.stack([lax.axis_index("expert"), lax.axis_index("dp")])
        mine, theirs, late_picker, spread, scale = tables(place, choices, local_count)
        theirs = send(theirs, swap_core)
        thirds = []
        for cross, outer, near_x, _ in seconds:
            middle = firsts[len(thirds)][1]
            if not thirds:
                third, third_x, fourth = tree_third(cross, outer, middle, edge)
            else:
                third, third_x, fourth, theirs = tree_third(cross, outer, middle, edge, theirs)
            thirds.append((third, third_x, fourth))
        order = (0, 1, 2, 3, 4, 5, 8, 9, 10, 11, 12, 13, 6, 7, 14, 15)
        row_chunks, late_chunks = [], []
        for part, (near, middle, own_x), (cross, outer, near_x, _), (third, third_x, fourth) in zip(
            parts, firsts, seconds, thirds
        ):
            early = part, near, third, own_x, near_x, third_x
            rows, late = tree_rest(early, fourth, mine, theirs, local_count)
            row_chunks.append([rows_of.reshape(local_count, -1, width) for rows_of in rows])
            late_chunks.append(late)
    else:
        rank, named_weight = choices[:, :local_count], choices[:, local_count:]
        match = rank[:, :, None, :] == jnp.arange(slots, dtype=jnp.float32)[None, None, :, None]
        picker = match.astype(jnp.bfloat16).reshape(device_count, local_count * slots, token_count)
        scale = jnp.sum(jnp.where(match, named_weight[:, :, None, :], 0.0), axis=3)
        scale = scale.transpose(1, 0, 2).reshape(local_count, device_count * slots, 1)
        spread = picker.transpose(0, 2, 1)
        rows = [pick_rows(picker, lax.all_gather(part, axes), local_count) for part in parts]
        row_chunks = [[rows_of.reshape(local_count, -1, width)] for rows_of in rows]
        late_chunks, late_picker = [[]] * gather_chunks, None
        order = tuple(range(device_count))
    hidden = hidden_rows(row_chunks, late_chunks, late_picker, scale, w_gate, w_up)

    sums = []
    for chunk in range(return_chunks):
        mine, theirs = mix_rows(hidden, w_down, spread, order, chunk, return_chunks)
        if as_tree:
            sums.append(chip_sums(mine, theirs))
        else:
            whole = jnp.concatenate([mine, theirs], axis=0).astype(jnp.float32)
            total = lax.psum_scatter(whole, axes, scatter_dimension=0)
            sums.append(total.astype(jnp.bfloat16))
    results = sums
    if as_tree:
        results = [tree_return(chip, chunk % 2 == 1) for chunk, chip in enumerate(sums)]
    return jnp.concatenate(results, axis=1)


def solution(mesh):
    split = P(("groups", "expert", "dp"), None)
    by_expert = P(("expert", "dp"), None, None)
    return jax.shard_map(
        shards,
        mesh=mesh,
        in_specs=(split, split, split, P(), by_expert, by_expert, by_expert),
        out_specs=split,
        check_vma=False,
    )
```

```python
import functools

import jax
import jax.numpy as jnp
from jax import lax
from jax.experimental import pallas as pl
from jax.experimental.pallas import tpu as pltpu
from jax.sharding import PartitionSpec as P

slots = 16
gather_chunks = 2
return_chunks = 2
mebi = 1024 * 1024


def grant(sources, tree_mebi):
    return (tree_mebi if sources <= 16 else 56) * mebi


def rounded_sum(first, *others):
    total = first.astype(jnp.float32)
    for other in others:
        total = total + other.astype(jnp.float32)
    return total.astype(jnp.bfloat16)


def pick_kernel(picker_ref, tokens_ref, rows_ref):
    sources = tokens_ref.shape[0]
    experts = rows_ref.shape[0]
    for source in range(sources):
        picked = jnp.dot(
            picker_ref[source], tokens_ref[source], preferred_element_type=jnp.float32
        ).astype(jnp.bfloat16)
        for expert in range(experts):
            rows_ref[expert, source] = picked[expert * slots : (expert + 1) * slots]


def pick_rows(picker, tokens, experts):
    sources, token_count, width = tokens.shape
    block = min(sources, 8)
    return pl.pallas_call(
        pick_kernel,
        grid=(sources // block,),
        in_specs=[
            pl.BlockSpec((block, experts * slots, token_count), lambda i: (i, 0, 0)),
            pl.BlockSpec((block, token_count, width), lambda i: (i, 0, 0)),
        ],
        out_specs=pl.BlockSpec((experts, block, slots, width), lambda i: (0, i, 0, 0)),
        out_shape=jax.ShapeDtypeStruct((experts, sources, slots, width), jnp.bfloat16),
        compiler_params=pltpu.CompilerParams(vmem_limit_bytes=grant(sources, 16)),
        cost_estimate=pl.CostEstimate(
            flops=2 * sources * experts * slots * token_count * width,
            bytes_accessed=2 * sources * width * (token_count + experts * slots),
            transcendentals=0,
        ),
    )(picker, tokens)


def rank_kernel(routes_ref, weight_ref, choice_ref):
    top_count, token_count = routes_ref.shape
    devices, experts = choice_ref.shape[0], choice_ref.shape[1] // 2
    shape = devices * experts, token_count
    every = lax.broadcasted_iota(jnp.int32, shape, 0)
    named, weight = jnp.zeros(shape, jnp.float32), jnp.zeros(shape, jnp.float32)
    for k in range(top_count):
        same = routes_ref[k : k + 1, :] == every
        named = jnp.where(same, 1.0, named)
        weight = jnp.where(same, weight_ref[k : k + 1, :], weight)
    square = token_count, token_count
    before = lax.broadcasted_iota(jnp.int32, square, 0) < lax.broadcasted_iota(jnp.int32, square, 1)
    before = jnp.where(before, 1.0, 0.0).astype(jnp.bfloat16)
    rank = jnp.dot(named.astype(jnp.bfloat16), before, preferred_element_type=jnp.float32)
    rank = jnp.where(named > 0.0, rank, -1.0)
    choice_ref[:, :experts] = rank.reshape(devices, experts, token_count)
    choice_ref[:, experts:] = weight.reshape(devices, experts, token_count)


def ranked(routes, route_weight, devices, experts):
    token_count = routes.shape[0]
    return pl.pallas_call(
        rank_kernel,
        in_specs=[pl.BlockSpec(memory_space=pltpu.VMEM)] * 2,
        out_specs=pl.BlockSpec(memory_space=pltpu.VMEM),
        out_shape=jax.ShapeDtypeStruct((devices, 2 * experts, token_count), jnp.float32),
        compiler_params=pltpu.CompilerParams(vmem_limit_bytes=8 * mebi),
    )(routes.T, route_weight.T)


def norm_kernel(tokens_ref, gain_ref, *part_refs):
    as_float = tokens_ref[...].astype(jnp.float32)
    mean = jnp.mean(as_float * as_float, axis=-1, keepdims=True)
    normed = (as_float * lax.rsqrt(mean + 1e-06) * gain_ref[...]).astype(jnp.bfloat16)
    width = part_refs[0].shape[1]
    for chunk, part_ref in enumerate(part_refs):
        part_ref[...] = normed[:, chunk * width : (chunk + 1) * width]


def normed_parts(tokens, norm_gain, chunks):
    token_count, feature_dim = tokens.shape
    part = jax.ShapeDtypeStruct((token_count, feature_dim // chunks), jnp.bfloat16)
    return pl.pallas_call(
        norm_kernel,
        in_specs=[pl.BlockSpec(memory_space=pltpu.VMEM)] * 2,
        out_specs=[pl.BlockSpec(memory_space=pltpu.VMEM)] * chunks,
        out_shape=[part] * chunks,
        compiler_params=pltpu.CompilerParams(vmem_limit_bytes=16 * mebi),
    )(tokens, norm_gain.reshape(1, feature_dim))


def slot_sources(z, dp):
    low = z < 2
    column = z, z ^ 1, jnp.where(low, 2, 1), jnp.where(low, 3, 0)
    early = [(column[i], side) for side in (0, 2) for i in (0, 1)]
    late = [(column[i], side) for side in (0, 2) for i in (2, 3)]
    return [
        from_z * 4 + (dp ^ (side + core))
        for group in (early, late)
        for core in (0, 1)
        for from_z, side in group
    ]


def table_kernel(place_ref, choices_ref, *refs):
    picker_refs, spread_ref, scale_ref = refs[:3], refs[3], refs[4]
    experts = scale_ref.shape[0]
    token_count = choices_ref.shape[2]
    early, late = picker_refs[0].shape[0], picker_refs[2].shape[0] // 2
    place = lax.broadcasted_iota(jnp.int32, (experts, slots, token_count), 1).astype(jnp.float32)
    sources = slot_sources(place_ref[0], place_ref[1])
    for slot, source in enumerate(sources):
        choice = choices_ref[source]
        match = choice[:experts][:, None, :] == place
        weight = jnp.where(match, choice[experts:][:, None, :], 0.0)
        scale_ref[:, slot * slots : (slot + 1) * slots, :] = jnp.sum(weight, axis=2, keepdims=True)
        picker = jnp.where(match, 1.0, 0.0).reshape(experts * slots, token_count)
        if slot < 2 * early:
            picker_refs[slot // early][slot % early] = picker.astype(jnp.bfloat16)
        else:
            picker_refs[2][slot - 2 * early] = picker.astype(jnp.bfloat16)
        spread_ref[slot] = picker.T.astype(jnp.bfloat16)


def tables(place, choices, experts):
    count, _, token_count = choices.shape
    rows = experts * slots
    late = count // 4
    early = count // 2 - late
    shapes = [(early, rows, token_count), (early, rows, token_count), (2 * late, rows, token_count)]
    shapes = [jax.ShapeDtypeStruct(shape, jnp.bfloat16) for shape in shapes]
    shapes.append(jax.ShapeDtypeStruct((count, token_count, rows), jnp.bfloat16))
    shapes.append(jax.ShapeDtypeStruct((experts, count * slots, 1), jnp.float32))
    return pl.pallas_call(
        table_kernel,
        in_specs=[
            pl.BlockSpec(memory_space=pltpu.SMEM),
            pl.BlockSpec(memory_space=pltpu.VMEM),
        ],
        out_specs=[pl.BlockSpec(memory_space=pltpu.VMEM)] * 5,
        out_shape=shapes,
        compiler_params=pltpu.CompilerParams(vmem_limit_bytes=grant(count, 12)),
    )(place, choices)


def pair_kernel(count, *refs):
    token_refs = refs[:count]
    mine_ref, theirs_ref, mine_rows_ref, theirs_rows_ref = refs[count:]
    experts = mine_rows_ref.shape[0]
    for source in range(count):
        for picker_ref, rows_ref in ((mine_ref, mine_rows_ref), (theirs_ref, theirs_rows_ref)):
            picked = jnp.dot(
                picker_ref[source], token_refs[source][...], preferred_element_type=jnp.float32
            ).astype(jnp.bfloat16)
            rows_ref[:, source] = picked.reshape(experts, slots, picked.shape[1])


def pick_pair(blocks, mine, theirs, experts):
    count = len(blocks)
    token_count, width = blocks[0].shape
    rows = jax.ShapeDtypeStruct((experts, count, slots, width), jnp.bfloat16)
    return pl.pallas_call(
        functools.partial(pair_kernel, count),
        in_specs=[pl.BlockSpec(memory_space=pltpu.VMEM)] * (count + 2),
        out_specs=[pl.BlockSpec(memory_space=pltpu.VMEM)] * 2,
        out_shape=[rows, rows],
        compiler_params=pltpu.CompilerParams(vmem_limit_bytes=grant(count, 16)),
        cost_estimate=pl.CostEstimate(
            flops=4 * count * experts * slots * token_count * width,
            bytes_accessed=2 * count * width * (token_count + 2 * experts * slots),
            transcendentals=0,
        ),
    )(*blocks, mine, theirs)


def hidden_kernel(chunks, groups, late, *refs):
    row_refs = refs[: chunks * groups]
    refs = refs[chunks * groups :]
    late_refs = refs[: chunks * late]
    refs = refs[chunks * late :]
    width = row_refs[0].shape[-1]
    if late:
        picker_ref, scale_ref, gate_ref, up_ref, hidden_ref, late_rows = refs

        @pl.when(pl.program_id(0) == 0)
        def _():
            for chunk in range(chunks):
                for source in range(late):
                    picked = jnp.dot(
                        picker_ref[source],
                        late_refs[chunk * late + source][...],
                        preferred_element_type=jnp.float32,
                    ).astype(jnp.bfloat16)
                    late_rows[:, source, :, chunk * width : (chunk + 1) * width] = picked.reshape(
                        late_rows.shape[0], slots, width
                    )

    else:
        scale_ref, gate_ref, up_ref, hidden_ref = refs
    gate_part = None
    for chunk in range(chunks):
        pieces = [ref[0] for ref in row_refs[chunk * groups : (chunk + 1) * groups]]
        if late:
            extra = late_rows[pl.program_id(0), :, :, chunk * width : (chunk + 1) * width]
            pieces.append(extra.reshape(late * slots, width))
        rows = jnp.concatenate(pieces, axis=0)
        depth = pl.ds(chunk * width, width)
        gate_add = jnp.dot(rows, gate_ref[0, depth, :], preferred_element_type=jnp.float32)
        up_add = jnp.dot(rows, up_ref[0, depth, :], preferred_element_type=jnp.float32)
        if gate_part is None:
            gate_part, up_part = gate_add, up_add
        else:
            gate_part, up_part = gate_part + gate_add, up_part + up_add
    hidden = gate_part / (1.0 + jnp.exp(-gate_part)) * up_part * scale_ref[0]
    hidden_ref[0] = hidden.astype(jnp.bfloat16)


def hidden_rows(row_chunks, late_chunks, late_picker, scale, w_gate, w_up):
    experts, feature_dim, hidden_dim = w_gate.shape
    chunks, groups, late = len(row_chunks), len(row_chunks[0]), len(late_chunks[0])
    pieces = [piece for row_groups in row_chunks for piece in row_groups]
    late_pieces = [piece for blocks in late_chunks for piece in blocks]
    scratch = []
    if late:
        late_pieces.append(late_picker)
        scratch = [pltpu.VMEM((experts, late, slots, feature_dim), jnp.bfloat16)]
    whole = scale.shape[1]
    return pl.pallas_call(
        functools.partial(hidden_kernel, chunks, groups, late),
        grid=(experts,),
        in_specs=[pl.BlockSpec((1,) + piece.shape[1:], lambda e: (e, 0, 0)) for piece in pieces]
        + [pl.BlockSpec(memory_space=pltpu.VMEM)] * len(late_pieces)
        + [
            pl.BlockSpec((1, whole, 1), lambda e: (e, 0, 0)),
            pl.BlockSpec((1, feature_dim, hidden_dim), lambda e: (e, 0, 0)),
            pl.BlockSpec((1, feature_dim, hidden_dim), lambda e: (e, 0, 0)),
        ],
        out_specs=pl.BlockSpec((1, whole, hidden_dim), lambda e: (e, 0, 0)),
        out_shape=jax.ShapeDtypeStruct((experts, whole, hidden_dim), jnp.bfloat16),
        scratch_shapes=scratch,
        compiler_params=pltpu.CompilerParams(vmem_limit_bytes=grant(whole // slots, 32)),
        cost_estimate=pl.CostEstimate(
            flops=4 * experts * whole * feature_dim * hidden_dim,
            bytes_accessed=4 * experts * feature_dim * hidden_dim,
            transcendentals=experts * whole * hidden_dim,
        ),
    )(*pieces, *late_pieces, scale, w_gate, w_up)


def mix_kernel(order, hidden_ref, down_ref, spread_ref, first_ref, second_ref, made):
    step = pl.program_id(0)
    group = hidden_ref.shape[0]
    sources = spread_ref.shape[0]
    width = down_ref.shape[2]
    for one in range(group):
        made[step * group + one] = (
            jnp.dot(hidden_ref[one], down_ref[one], preferred_element_type=jnp.float32)
            .astype(jnp.bfloat16)
            .reshape(sources, slots, width)
        )

    @pl.when(step == pl.num_programs(0) - 1)
    def _():
        for source in range(sources):
            rows = made[:, source].reshape(spread_ref.shape[2], width)
            mixed = jnp.dot(
                spread_ref[source], rows, preferred_element_type=jnp.float32
            ).astype(jnp.bfloat16)
            if order[source] < sources // 2:
                first_ref[order[source]] = mixed
            else:
                second_ref[order[source] - sources // 2] = mixed


def mix_rows(hidden, w_down, spread, order, chunk, chunks):
    experts, whole, hidden_dim = hidden.shape
    width = w_down.shape[2] // chunks
    sources, token_count, local_rows = spread.shape
    group = 2 if experts % 2 == 0 else 1
    half = jax.ShapeDtypeStruct((sources // 2, token_count, width), jnp.bfloat16)
    return pl.pallas_call(
        functools.partial(mix_kernel, order),
        grid=(experts // group,),
        in_specs=[
            pl.BlockSpec((group, whole, hidden_dim), lambda e: (e, 0, 0)),
            pl.BlockSpec((group, hidden_dim, width), lambda e: (e, 0, chunk)),
            pl.BlockSpec(memory_space=pltpu.VMEM),
        ],
        out_specs=[pl.BlockSpec(memory_space=pltpu.VMEM)] * 2,
        out_shape=[half, half],
        scratch_shapes=[pltpu.VMEM((experts, sources, slots, width), jnp.bfloat16)],
        compiler_params=pltpu.CompilerParams(vmem_limit_bytes=grant(sources, 28)),
        cost_estimate=pl.CostEstimate(
            flops=2 * experts * whole * hidden_dim * width
            + 2 * sources * token_count * local_rows * width,
            bytes_accessed=2 * experts * hidden_dim * (width + whole)
            + 2 * sources * token_count * width,
            transcendentals=0,
        ),
    )(hidden, w_down, spread)


axes = ("expert", "dp")


def pairs_of(expert_pairs, dp_pairs, dp_size):
    return [
        (e_from * dp_size + d_from, e_to * dp_size + d_to)
        for e_from, e_to in expert_pairs
        for d_from, d_to in dp_pairs
    ]


stay_z = [(i, i) for i in range(4)]
stay_dp = [(i, i) for i in range(4)]
swap_z = pairs_of([(0, 1), (1, 0), (2, 3), (3, 2)], stay_dp, 4)
middle_z = pairs_of([(1, 2), (2, 1)], stay_dp, 4)
outward_z = pairs_of([(1, 0), (2, 3)], stay_dp, 4)
inward_z = pairs_of([(0, 1), (3, 2)], stay_dp, 4)
leap_out = pairs_of([(3, 1), (0, 2)], stay_dp, 4)
leap_back = pairs_of([(1, 3), (2, 0)], stay_dp, 4)
swap_x = pairs_of(stay_z, [(0, 2), (2, 0), (1, 3), (3, 1)], 4)
swap_core = pairs_of(stay_z, [(0, 1), (1, 0), (2, 3), (3, 2)], 4)


def send(value, pairs):
    return lax.ppermute(value, axes, pairs)


def together(*values):
    return lax.optimization_barrier(values)


def tree_start(own, *others):
    return together(
        send(own, swap_z),
        send(own, middle_z),
        send(own, leap_out),
        send(own, swap_x),
        *others,
    )


def tree_second(near, middle, cross, edge, *others):
    outer, far, near_x, *others = together(
        send(middle, outward_z), send(cross, outward_z), send(near, swap_x), *others
    )
    return jnp.where(edge, outer, middle), jnp.where(edge, far, cross), near_x, *others


def tree_rest(early, third, fourth, third_x, mine, theirs, experts):
    mine_rows, theirs_rows = pick_pair(early, mine, theirs, experts)
    fourth_x, theirs_rows = together(send(fourth, swap_x), send(theirs_rows, swap_core))
    late = [third, fourth, third_x, fourth_x]
    return [mine_rows, theirs_rows], late + [send(block, swap_core) for block in late]


def chip_sums(mine, theirs):
    return rounded_sum(mine, send(theirs, swap_core))


def tree_return(chip):
    own, near, own_x, near_x, third, fourth, third_x, fourth_x = [chip[i] for i in range(8)]
    third_in = send(third_x, swap_x)
    fourth_in, near_x, own_x = together(send(fourth_x, swap_x), near_x, own_x)
    fourth = rounded_sum(fourth, fourth_in)
    third = rounded_sum(third, third_in)
    far, outer, near_in, own_x = together(
        send(fourth, inward_z), send(third, inward_z), send(near_x, swap_x), own_x
    )
    return rounded_sum(
        own,
        send(own_x, swap_x),
        send(rounded_sum(fourth, far), leap_back),
        send(rounded_sum(third, outer), middle_z),
        send(rounded_sum(near, near_in), swap_z),
    )


def shards(tokens, routes, route_weight, norm_gain, w_gate, w_up, w_down):
    token_count, top_count = routes.shape
    feature_dim = tokens.shape[1]
    expert_size = lax.axis_size("expert")
    dp_size = lax.axis_size("dp")
    device_count = expert_size * dp_size
    local_count = w_gate.shape[0]
    as_tree = expert_size == 4 and dp_size == 4
    edge = (lax.axis_index("expert") % 3) == 0

    width = feature_dim // gather_chunks
    parts = normed_parts(tokens, norm_gain, gather_chunks)
    if as_tree:
        choice = ranked(routes, route_weight, device_count, local_count)
        firsts = []
        for part in parts:
            if not firsts:
                near, middle, cross, own_x, choice = tree_start(part, choice)
            else:
                near, middle, cross, own_x = tree_start(part)
            firsts.append((near, middle, cross, own_x))
    else:
        every = jnp.arange(device_count * local_count, dtype=jnp.int32)
        same = routes[:, :, None] == every
        named = jnp.any(same, axis=1)
        named_weight = jnp.sum(jnp.where(same, route_weight[:, :, None], 0.0), axis=1)
        count = jnp.arange(token_count)
        before = (count[:, None] > count[None, :]).astype(jnp.bfloat16)
        rank = jnp.dot(before, named.astype(jnp.bfloat16), preferred_element_type=jnp.float32)
        rank = jnp.where(named, rank, -1.0)
        choice = jnp.stack([rank.T, named_weight.T])
        choice = choice.reshape(2, device_count, local_count, token_count).transpose(1, 0, 2, 3)
        choice = choice.reshape(device_count, 2 * local_count, token_count)
    choices = lax.all_to_all(choice, axes, split_axis=0, concat_axis=0, tiled=True)
    if as_tree:
        place = jnp.stack([lax.axis_index("expert"), lax.axis_index("dp")])
        seconds = []
        for near, middle, cross, own_x in firsts:
            if not seconds:
                third, fourth, near_x, choices = tree_second(near, middle, cross, edge, choices)
            else:
                third, fourth, near_x, third_x = tree_second(
                    near, middle, cross, edge, seconds[-1][3]
                )
                seconds[-1] = (*seconds[-1][:3], third_x)
            seconds.append((third, fourth, near_x, send(third, swap_x)))
        mine, theirs, late_picker, spread, scale = tables(place, choices, local_count)
        theirs = send(theirs, swap_core)
        order = (0, 1, 2, 3, 8, 9, 10, 11, 4, 5, 6, 7, 12, 13, 14, 15)
        row_chunks, late_chunks = [], []
        for part, (near, middle, cross, own_x), (third, fourth, near_x, third_x) in zip(
            parts, firsts, seconds
        ):
            early = part, near, own_x, near_x
            rows, late = tree_rest(
                early, third, fourth, third_x, mine, theirs, local_count
            )
            row_chunks.append([rows_of.reshape(local_count, -1, width) for rows_of in rows])
            late_chunks.append(late)
    else:
        rank, named_weight = choices[:, :local_count], choices[:, local_count:]
        match = rank[:, :, None, :] == jnp.arange(slots, dtype=jnp.float32)[None, None, :, None]
        picker = match.astype(jnp.bfloat16).reshape(device_count, local_count * slots, token_count)
        scale = jnp.sum(jnp.where(match, named_weight[:, :, None, :], 0.0), axis=3)
        scale = scale.transpose(1, 0, 2).reshape(local_count, device_count * slots, 1)
        spread = picker.transpose(0, 2, 1)
        rows = [pick_rows(picker, lax.all_gather(part, axes), local_count) for part in parts]
        row_chunks = [[rows_of.reshape(local_count, -1, width)] for rows_of in rows]
        late_chunks, late_picker = [[]] * gather_chunks, None
        order = tuple(range(device_count))
    hidden = hidden_rows(row_chunks, late_chunks, late_picker, scale, w_gate, w_up)

    sums = []
    for chunk in range(return_chunks):
        mine, theirs = mix_rows(hidden, w_down, spread, order, chunk, return_chunks)
        if as_tree:
            sums.append(chip_sums(mine, theirs))
        else:
            whole = jnp.concatenate([mine, theirs], axis=0).astype(jnp.float32)
            total = lax.psum_scatter(whole, axes, scatter_dimension=0)
            sums.append(total.astype(jnp.bfloat16))
    results = sums
    if as_tree:
        results = [tree_return(chip) for chip in sums]
    return jnp.concatenate(results, axis=1)


def solution(mesh):
    split = P(("groups", "expert", "dp"), None)
    by_expert = P(("expert", "dp"), None, None)
    return jax.shard_map(
        shards,
        mesh=mesh,
        in_specs=(split, split, split, P(), by_expert, by_expert, by_expert),
        out_specs=split,
        check_vma=False,
    )
```

```python
import functools

import jax
import jax.numpy as jnp
from jax import lax
from jax.experimental import pallas as pl
from jax.experimental.pallas import tpu as pltpu
from jax.sharding import PartitionSpec as P

slots = 16
gather_chunks = 2
return_chunks = 2
mebi = 1024 * 1024


def grant(sources, tree_mebi):
    return (tree_mebi if sources <= 16 else 56) * mebi


def rounded_sum(first, *others):
    total = first.astype(jnp.float32)
    for other in others:
        total = total + other.astype(jnp.float32)
    return total.astype(jnp.bfloat16)


def pick_kernel(picker_ref, tokens_ref, rows_ref):
    sources = tokens_ref.shape[0]
    experts = rows_ref.shape[0]
    for source in range(sources):
        picked = jnp.dot(
            picker_ref[source], tokens_ref[source], preferred_element_type=jnp.float32
        ).astype(jnp.bfloat16)
        for expert in range(experts):
            rows_ref[expert, source] = picked[expert * slots : (expert + 1) * slots]


def pick_rows(picker, tokens, experts):
    sources, token_count, width = tokens.shape
    block = min(sources, 8)
    return pl.pallas_call(
        pick_kernel,
        grid=(sources // block,),
        in_specs=[
            pl.BlockSpec((block, experts * slots, token_count), lambda i: (i, 0, 0)),
            pl.BlockSpec((block, token_count, width), lambda i: (i, 0, 0)),
        ],
        out_specs=pl.BlockSpec((experts, block, slots, width), lambda i: (0, i, 0, 0)),
        out_shape=jax.ShapeDtypeStruct((experts, sources, slots, width), jnp.bfloat16),
        compiler_params=pltpu.CompilerParams(vmem_limit_bytes=grant(sources, 16)),
        cost_estimate=pl.CostEstimate(
            flops=2 * sources * experts * slots * token_count * width,
            bytes_accessed=2 * sources * width * (token_count + experts * slots),
            transcendentals=0,
        ),
    )(picker, tokens)


def rank_kernel(routes_ref, weight_ref, choice_ref):
    top_count, token_count = routes_ref.shape
    devices, experts = choice_ref.shape[0], choice_ref.shape[1] // 2
    shape = devices * experts, token_count
    every = lax.broadcasted_iota(jnp.int32, shape, 0)
    named, weight = jnp.zeros(shape, jnp.float32), jnp.zeros(shape, jnp.float32)
    for k in range(top_count):
        same = routes_ref[k : k + 1, :] == every
        named = jnp.where(same, 1.0, named)
        weight = jnp.where(same, weight_ref[k : k + 1, :], weight)
    square = token_count, token_count
    before = lax.broadcasted_iota(jnp.int32, square, 0) < lax.broadcasted_iota(jnp.int32, square, 1)
    before = jnp.where(before, 1.0, 0.0).astype(jnp.bfloat16)
    rank = jnp.dot(named.astype(jnp.bfloat16), before, preferred_element_type=jnp.float32)
    rank = jnp.where(named > 0.0, rank, -1.0)
    choice_ref[:, :experts] = rank.reshape(devices, experts, token_count)
    choice_ref[:, experts:] = weight.reshape(devices, experts, token_count)


def ranked(routes, route_weight, devices, experts):
    token_count = routes.shape[0]
    return pl.pallas_call(
        rank_kernel,
        in_specs=[pl.BlockSpec(memory_space=pltpu.VMEM)] * 2,
        out_specs=pl.BlockSpec(memory_space=pltpu.VMEM),
        out_shape=jax.ShapeDtypeStruct((devices, 2 * experts, token_count), jnp.float32),
        compiler_params=pltpu.CompilerParams(vmem_limit_bytes=8 * mebi),
    )(routes.T, route_weight.T)


def norm_kernel(tokens_ref, gain_ref, *part_refs):
    as_float = tokens_ref[...].astype(jnp.float32)
    mean = jnp.mean(as_float * as_float, axis=-1, keepdims=True)
    normed = (as_float * lax.rsqrt(mean + 1e-06) * gain_ref[...]).astype(jnp.bfloat16)
    width = part_refs[0].shape[1]
    for chunk, part_ref in enumerate(part_refs):
        part_ref[...] = normed[:, chunk * width : (chunk + 1) * width]


def normed_parts(tokens, norm_gain, chunks):
    token_count, feature_dim = tokens.shape
    part = jax.ShapeDtypeStruct((token_count, feature_dim // chunks), jnp.bfloat16)
    return pl.pallas_call(
        norm_kernel,
        in_specs=[pl.BlockSpec(memory_space=pltpu.VMEM)] * 2,
        out_specs=[pl.BlockSpec(memory_space=pltpu.VMEM)] * chunks,
        out_shape=[part] * chunks,
        compiler_params=pltpu.CompilerParams(vmem_limit_bytes=16 * mebi),
    )(tokens, norm_gain.reshape(1, feature_dim))


def slot_sources(z, dp):
    low = z < 2
    column = z, z ^ 1, jnp.where(low, 2, 1), jnp.where(low, 3, 0)
    early = [(column[i], side) for side in (0, 2) for i in range(3)]
    late = [(column[3], side) for side in (0, 2)]
    return [
        from_z * 4 + (dp ^ (side + core))
        for group in (early, late)
        for core in (0, 1)
        for from_z, side in group
    ]


def table_kernel(place_ref, choices_ref, *refs):
    picker_refs, spread_ref, scale_ref = refs[:3], refs[3], refs[4]
    experts = scale_ref.shape[0]
    token_count = choices_ref.shape[2]
    early, late = picker_refs[0].shape[0], picker_refs[2].shape[0] // 2
    place = lax.broadcasted_iota(jnp.int32, (experts, slots, token_count), 1).astype(jnp.float32)
    sources = slot_sources(place_ref[0], place_ref[1])
    for slot, source in enumerate(sources):
        choice = choices_ref[source]
        match = choice[:experts][:, None, :] == place
        weight = jnp.where(match, choice[experts:][:, None, :], 0.0)
        scale_ref[:, slot * slots : (slot + 1) * slots, :] = jnp.sum(weight, axis=2, keepdims=True)
        picker = jnp.where(match, 1.0, 0.0).reshape(experts * slots, token_count)
        if slot < 2 * early:
            picker_refs[slot // early][slot % early] = picker.astype(jnp.bfloat16)
        else:
            picker_refs[2][slot - 2 * early] = picker.astype(jnp.bfloat16)
        spread_ref[slot] = picker.T.astype(jnp.bfloat16)


def tables(place, choices, experts):
    count, _, token_count = choices.shape
    rows = experts * slots
    late = count // 8
    early = count // 2 - late
    shapes = [(early, rows, token_count), (early, rows, token_count), (2 * late, rows, token_count)]
    shapes = [jax.ShapeDtypeStruct(shape, jnp.bfloat16) for shape in shapes]
    shapes.append(jax.ShapeDtypeStruct((count, token_count, rows), jnp.bfloat16))
    shapes.append(jax.ShapeDtypeStruct((experts, count * slots, 1), jnp.float32))
    return pl.pallas_call(
        table_kernel,
        in_specs=[
            pl.BlockSpec(memory_space=pltpu.SMEM),
            pl.BlockSpec(memory_space=pltpu.VMEM),
        ],
        out_specs=[pl.BlockSpec(memory_space=pltpu.VMEM)] * 5,
        out_shape=shapes,
        compiler_params=pltpu.CompilerParams(vmem_limit_bytes=grant(count, 12)),
    )(place, choices)


def pair_kernel(count, *refs):
    token_refs = refs[:count]
    mine_ref, theirs_ref, mine_rows_ref, theirs_rows_ref = refs[count:]
    experts = mine_rows_ref.shape[0]
    for source in range(count):
        for picker_ref, rows_ref in ((mine_ref, mine_rows_ref), (theirs_ref, theirs_rows_ref)):
            picked = jnp.dot(
                picker_ref[source], token_refs[source][...], preferred_element_type=jnp.float32
            ).astype(jnp.bfloat16)
            rows_ref[:, source] = picked.reshape(experts, slots, picked.shape[1])


def pick_pair(blocks, mine, theirs, experts):
    count = len(blocks)
    token_count, width = blocks[0].shape
    rows = jax.ShapeDtypeStruct((experts, count, slots, width), jnp.bfloat16)
    return pl.pallas_call(
        functools.partial(pair_kernel, count),
        in_specs=[pl.BlockSpec(memory_space=pltpu.VMEM)] * (count + 2),
        out_specs=[pl.BlockSpec(memory_space=pltpu.VMEM)] * 2,
        out_shape=[rows, rows],
        compiler_params=pltpu.CompilerParams(vmem_limit_bytes=grant(count, 16)),
        cost_estimate=pl.CostEstimate(
            flops=4 * count * experts * slots * token_count * width,
            bytes_accessed=2 * count * width * (token_count + 2 * experts * slots),
            transcendentals=0,
        ),
    )(*blocks, mine, theirs)


def hidden_kernel(chunks, groups, late, *refs):
    row_refs = refs[: chunks * groups]
    refs = refs[chunks * groups :]
    late_refs = refs[: chunks * late]
    refs = refs[chunks * late :]
    width = row_refs[0].shape[-1]
    if late:
        picker_ref, scale_ref, gate_ref, up_ref, hidden_ref, late_rows = refs

        @pl.when(pl.program_id(0) == 0)
        def _():
            for chunk in range(chunks):
                for source in range(late):
                    picked = jnp.dot(
                        picker_ref[source],
                        late_refs[chunk * late + source][...],
                        preferred_element_type=jnp.float32,
                    ).astype(jnp.bfloat16)
                    late_rows[:, source, :, chunk * width : (chunk + 1) * width] = picked.reshape(
                        late_rows.shape[0], slots, width
                    )

    else:
        scale_ref, gate_ref, up_ref, hidden_ref = refs
    gate_part = None
    for chunk in range(chunks):
        pieces = [ref[0] for ref in row_refs[chunk * groups : (chunk + 1) * groups]]
        if late:
            extra = late_rows[pl.program_id(0), :, :, chunk * width : (chunk + 1) * width]
            pieces.append(extra.reshape(late * slots, width))
        rows = jnp.concatenate(pieces, axis=0)
        depth = pl.ds(chunk * width, width)
        gate_add = jnp.dot(rows, gate_ref[0, depth, :], preferred_element_type=jnp.float32)
        up_add = jnp.dot(rows, up_ref[0, depth, :], preferred_element_type=jnp.float32)
        if gate_part is None:
            gate_part, up_part = gate_add, up_add
        else:
            gate_part, up_part = gate_part + gate_add, up_part + up_add
    hidden = gate_part / (1.0 + jnp.exp(-gate_part)) * up_part * scale_ref[0]
    hidden_ref[0] = hidden.astype(jnp.bfloat16)


def hidden_rows(row_chunks, late_chunks, late_picker, scale, w_gate, w_up):
    experts, feature_dim, hidden_dim = w_gate.shape
    chunks, groups, late = len(row_chunks), len(row_chunks[0]), len(late_chunks[0])
    pieces = [piece for row_groups in row_chunks for piece in row_groups]
    late_pieces = [piece for blocks in late_chunks for piece in blocks]
    scratch = []
    if late:
        late_pieces.append(late_picker)
        scratch = [pltpu.VMEM((experts, late, slots, feature_dim), jnp.bfloat16)]
    whole = scale.shape[1]
    return pl.pallas_call(
        functools.partial(hidden_kernel, chunks, groups, late),
        grid=(experts,),
        in_specs=[pl.BlockSpec((1,) + piece.shape[1:], lambda e: (e, 0, 0)) for piece in pieces]
        + [pl.BlockSpec(memory_space=pltpu.VMEM)] * len(late_pieces)
        + [
            pl.BlockSpec((1, whole, 1), lambda e: (e, 0, 0)),
            pl.BlockSpec((1, feature_dim, hidden_dim), lambda e: (e, 0, 0)),
            pl.BlockSpec((1, feature_dim, hidden_dim), lambda e: (e, 0, 0)),
        ],
        out_specs=pl.BlockSpec((1, whole, hidden_dim), lambda e: (e, 0, 0)),
        out_shape=jax.ShapeDtypeStruct((experts, whole, hidden_dim), jnp.bfloat16),
        scratch_shapes=scratch,
        compiler_params=pltpu.CompilerParams(vmem_limit_bytes=grant(whole // slots, 32)),
        cost_estimate=pl.CostEstimate(
            flops=4 * experts * whole * feature_dim * hidden_dim,
            bytes_accessed=4 * experts * feature_dim * hidden_dim,
            transcendentals=experts * whole * hidden_dim,
        ),
    )(*pieces, *late_pieces, scale, w_gate, w_up)


def mix_kernel(order, hidden_ref, down_ref, spread_ref, first_ref, second_ref, made):
    step = pl.program_id(0)
    group = hidden_ref.shape[0]
    sources = spread_ref.shape[0]
    width = down_ref.shape[2]
    for one in range(group):
        made[step * group + one] = (
            jnp.dot(hidden_ref[one], down_ref[one], preferred_element_type=jnp.float32)
            .astype(jnp.bfloat16)
            .reshape(sources, slots, width)
        )

    @pl.when(step == pl.num_programs(0) - 1)
    def _():
        for source in range(sources):
            rows = made[:, source].reshape(spread_ref.shape[2], width)
            mixed = jnp.dot(
                spread_ref[source], rows, preferred_element_type=jnp.float32
            ).astype(jnp.bfloat16)
            if order[source] < sources // 2:
                first_ref[order[source]] = mixed
            else:
                second_ref[order[source] - sources // 2] = mixed


def mix_rows(hidden, w_down, spread, order, chunk, chunks):
    experts, whole, hidden_dim = hidden.shape
    width = w_down.shape[2] // chunks
    sources, token_count, local_rows = spread.shape
    group = 2 if experts % 2 == 0 else 1
    half = jax.ShapeDtypeStruct((sources // 2, token_count, width), jnp.bfloat16)
    return pl.pallas_call(
        functools.partial(mix_kernel, order),
        grid=(experts // group,),
        in_specs=[
            pl.BlockSpec((group, whole, hidden_dim), lambda e: (e, 0, 0)),
            pl.BlockSpec((group, hidden_dim, width), lambda e: (e, 0, chunk)),
            pl.BlockSpec(memory_space=pltpu.VMEM),
        ],
        out_specs=[pl.BlockSpec(memory_space=pltpu.VMEM)] * 2,
        out_shape=[half, half],
        scratch_shapes=[pltpu.VMEM((experts, sources, slots, width), jnp.bfloat16)],
        compiler_params=pltpu.CompilerParams(vmem_limit_bytes=grant(sources, 28)),
        cost_estimate=pl.CostEstimate(
            flops=2 * experts * whole * hidden_dim * width
            + 2 * sources * token_count * local_rows * width,
            bytes_accessed=2 * experts * hidden_dim * (width + whole)
            + 2 * sources * token_count * width,
            transcendentals=0,
        ),
    )(hidden, w_down, spread)


axes = ("expert", "dp")


def pairs_of(expert_pairs, dp_pairs, dp_size):
    return [
        (e_from * dp_size + d_from, e_to * dp_size + d_to)
        for e_from, e_to in expert_pairs
        for d_from, d_to in dp_pairs
    ]


stay_z = [(i, i) for i in range(4)]
stay_dp = [(i, i) for i in range(4)]
swap_z = pairs_of([(0, 1), (1, 0), (2, 3), (3, 2)], stay_dp, 4)
middle_z = pairs_of([(1, 2), (2, 1)], stay_dp, 4)
outward_z = pairs_of([(1, 0), (2, 3)], stay_dp, 4)
inward_z = pairs_of([(0, 1), (3, 2)], stay_dp, 4)
swap_x = pairs_of(stay_z, [(0, 2), (2, 0), (1, 3), (3, 1)], 4)
swap_core = pairs_of(stay_z, [(0, 1), (1, 0), (2, 3), (3, 2)], 4)


def send(value, pairs):
    return lax.ppermute(value, axes, pairs)


def together(*values):
    return lax.optimization_barrier(values)


def tree_start(own, *others):
    return together(send(own, swap_z), send(own, middle_z), send(own, swap_x), *others)


def tree_second(near, middle, *others):
    return together(
        send(near, middle_z), send(middle, outward_z), send(near, swap_x), *others
    )


def tree_third(cross, outer, middle, edge, *others):
    third = jnp.where(edge, outer, middle)
    far, third_x, *others = together(send(cross, outward_z), send(third, swap_x), *others)
    return third, third_x, jnp.where(edge, far, cross), *others


def tree_rest(early, fourth, mine, theirs, experts):
    mine_rows, theirs_rows = pick_pair(early, mine, theirs, experts)
    fourth_x, theirs_rows = together(send(fourth, swap_x), send(theirs_rows, swap_core))
    late = [fourth, fourth_x]
    return [mine_rows, theirs_rows], late + [send(block, swap_core) for block in late]


def chip_sums(mine, theirs):
    return rounded_sum(mine, send(theirs, swap_core))


def tree_return(chip):
    own, near, third, own_x, near_x, third_x, fourth, fourth_x = [chip[i] for i in range(8)]
    fourth_in, third_x, near_x, own_x = together(send(fourth_x, swap_x), third_x, near_x, own_x)
    fourth = rounded_sum(fourth, fourth_in)
    far, third_in, near_x, own_x = together(
        send(fourth, inward_z), send(third_x, swap_x), near_x, own_x
    )
    cross = rounded_sum(fourth, far)
    third = rounded_sum(third, third_in)
    outer, crossed, near_in, own_x = together(
        send(third, inward_z), send(cross, middle_z), send(near_x, swap_x), own_x
    )
    middle = rounded_sum(third, outer)
    near = rounded_sum(near, near_in, crossed)
    return rounded_sum(
        own, send(own_x, swap_x), send(middle, middle_z), send(near, swap_z)
    )


def shards(tokens, routes, route_weight, norm_gain, w_gate, w_up, w_down):
    token_count, top_count = routes.shape
    feature_dim = tokens.shape[1]
    expert_size = lax.axis_size("expert")
    dp_size = lax.axis_size("dp")
    device_count = expert_size * dp_size
    local_count = w_gate.shape[0]
    as_tree = expert_size == 4 and dp_size == 4
    edge = (lax.axis_index("expert") % 3) == 0

    width = feature_dim // gather_chunks
    parts = normed_parts(tokens, norm_gain, gather_chunks)
    if as_tree:
        choice = ranked(routes, route_weight, device_count, local_count)
        firsts = []
        for part in parts:
            if not firsts:
                near, middle, own_x, choice = tree_start(part, choice)
            else:
                near, middle, own_x = tree_start(part)
            firsts.append((near, middle, own_x))
    else:
        every = jnp.arange(device_count * local_count, dtype=jnp.int32)
        same = routes[:, :, None] == every
        named = jnp.any(same, axis=1)
        named_weight = jnp.sum(jnp.where(same, route_weight[:, :, None], 0.0), axis=1)
        count = jnp.arange(token_count)
        before = (count[:, None] > count[None, :]).astype(jnp.bfloat16)
        rank = jnp.dot(before, named.astype(jnp.bfloat16), preferred_element_type=jnp.float32)
        rank = jnp.where(named, rank, -1.0)
        choice = jnp.stack([rank.T, named_weight.T])
        choice = choice.reshape(2, device_count, local_count, token_count).transpose(1, 0, 2, 3)
        choice = choice.reshape(device_count, 2 * local_count, token_count)
    choices = lax.all_to_all(choice, axes, split_axis=0, concat_axis=0, tiled=True)
    if as_tree:
        place = jnp.stack([lax.axis_index("expert"), lax.axis_index("dp")])
        seconds = []
        for near, middle, own_x in firsts:
            if not seconds:
                cross, outer, near_x, choices = tree_second(near, middle, choices)
            else:
                cross, outer, near_x = tree_second(near, middle)
            seconds.append((cross, outer, near_x))
        mine, theirs, late_picker, spread, scale = tables(place, choices, local_count)
        theirs = send(theirs, swap_core)
        thirds = []
        for (near, middle, own_x), (cross, outer, near_x) in zip(firsts, seconds):
            if not thirds:
                third, third_x, fourth, theirs = tree_third(cross, outer, middle, edge, theirs)
            else:
                third, third_x, fourth = tree_third(cross, outer, middle, edge)
            thirds.append((third, third_x, fourth))
        order = (0, 1, 2, 3, 4, 5, 8, 9, 10, 11, 12, 13, 6, 7, 14, 15)
        row_chunks, late_chunks = [], []
        for part, (near, middle, own_x), (cross, outer, near_x), (third, third_x, fourth) in zip(
            parts, firsts, seconds, thirds
        ):
            early = part, near, third, own_x, near_x, third_x
            rows, late = tree_rest(early, fourth, mine, theirs, local_count)
            row_chunks.append([rows_of.reshape(local_count, -1, width) for rows_of in rows])
            late_chunks.append(late)
    else:
        rank, named_weight = choices[:, :local_count], choices[:, local_count:]
        match = rank[:, :, None, :] == jnp.arange(slots, dtype=jnp.float32)[None, None, :, None]
        picker = match.astype(jnp.bfloat16).reshape(device_count, local_count * slots, token_count)
        scale = jnp.sum(jnp.where(match, named_weight[:, :, None, :], 0.0), axis=3)
        scale = scale.transpose(1, 0, 2).reshape(local_count, device_count * slots, 1)
        spread = picker.transpose(0, 2, 1)
        rows = [pick_rows(picker, lax.all_gather(part, axes), local_count) for part in parts]
        row_chunks = [[rows_of.reshape(local_count, -1, width)] for rows_of in rows]
        late_chunks, late_picker = [[]] * gather_chunks, None
        order = tuple(range(device_count))
    hidden = hidden_rows(row_chunks, late_chunks, late_picker, scale, w_gate, w_up)

    sums = []
    for chunk in range(return_chunks):
        mine, theirs = mix_rows(hidden, w_down, spread, order, chunk, return_chunks)
        if as_tree:
            sums.append(chip_sums(mine, theirs))
        else:
            whole = jnp.concatenate([mine, theirs], axis=0).astype(jnp.float32)
            total = lax.psum_scatter(whole, axes, scatter_dimension=0)
            sums.append(total.astype(jnp.bfloat16))
    results = sums
    if as_tree:
        results = [tree_return(chip) for chip in sums]
    return jnp.concatenate(results, axis=1)


def solution(mesh):
    split = P(("groups", "expert", "dp"), None)
    by_expert = P(("expert", "dp"), None, None)
    return jax.shard_map(
        shards,
        mesh=mesh,
        in_specs=(split, split, split, P(), by_expert, by_expert, by_expert),
        out_specs=split,
        check_vma=False,
    )
```

```python
import functools

import jax
import jax.numpy as jnp
from jax import lax
from jax.experimental import pallas as pl
from jax.experimental.pallas import tpu as pltpu
from jax.sharding import PartitionSpec as P

slots = 16
gather_chunks = 2
return_chunks = 2
mebi = 1024 * 1024


def grant(sources, tree_mebi):
    return (tree_mebi if sources <= 16 else 56) * mebi


def rounded_sum(first, *others):
    total = first.astype(jnp.float32)
    for other in others:
        total = total + other.astype(jnp.float32)
    return total.astype(jnp.bfloat16)


def pick_kernel(picker_ref, tokens_ref, rows_ref):
    sources = tokens_ref.shape[0]
    experts = rows_ref.shape[0]
    for source in range(sources):
        picked = jnp.dot(
            picker_ref[source], tokens_ref[source], preferred_element_type=jnp.float32
        ).astype(jnp.bfloat16)
        for expert in range(experts):
            rows_ref[expert, source] = picked[expert * slots : (expert + 1) * slots]


def pick_rows(picker, tokens, experts):
    sources, token_count, width = tokens.shape
    block = min(sources, 8)
    return pl.pallas_call(
        pick_kernel,
        grid=(sources // block,),
        in_specs=[
            pl.BlockSpec((block, experts * slots, token_count), lambda i: (i, 0, 0)),
            pl.BlockSpec((block, token_count, width), lambda i: (i, 0, 0)),
        ],
        out_specs=pl.BlockSpec((experts, block, slots, width), lambda i: (0, i, 0, 0)),
        out_shape=jax.ShapeDtypeStruct((experts, sources, slots, width), jnp.bfloat16),
        compiler_params=pltpu.CompilerParams(vmem_limit_bytes=grant(sources, 16)),
        cost_estimate=pl.CostEstimate(
            flops=2 * sources * experts * slots * token_count * width,
            bytes_accessed=2 * sources * width * (token_count + experts * slots),
            transcendentals=0,
        ),
    )(picker, tokens)


def rank_kernel(routes_ref, weight_ref, choice_ref):
    top_count, token_count = routes_ref.shape
    devices, experts = choice_ref.shape[0], choice_ref.shape[1] // 2
    shape = devices * experts, token_count
    every = lax.broadcasted_iota(jnp.int32, shape, 0)
    named, weight = jnp.zeros(shape, jnp.float32), jnp.zeros(shape, jnp.float32)
    for k in range(top_count):
        same = routes_ref[k : k + 1, :] == every
        named = jnp.where(same, 1.0, named)
        weight = jnp.where(same, weight_ref[k : k + 1, :], weight)
    square = token_count, token_count
    before = lax.broadcasted_iota(jnp.int32, square, 0) < lax.broadcasted_iota(jnp.int32, square, 1)
    before = jnp.where(before, 1.0, 0.0).astype(jnp.bfloat16)
    rank = jnp.dot(named.astype(jnp.bfloat16), before, preferred_element_type=jnp.float32)
    rank = jnp.where(named > 0.0, rank, -1.0)
    choice_ref[:, :experts] = rank.reshape(devices, experts, token_count)
    choice_ref[:, experts:] = weight.reshape(devices, experts, token_count)


def ranked(routes, route_weight, devices, experts):
    token_count = routes.shape[0]
    return pl.pallas_call(
        rank_kernel,
        in_specs=[pl.BlockSpec(memory_space=pltpu.VMEM)] * 2,
        out_specs=pl.BlockSpec(memory_space=pltpu.VMEM),
        out_shape=jax.ShapeDtypeStruct((devices, 2 * experts, token_count), jnp.float32),
        compiler_params=pltpu.CompilerParams(vmem_limit_bytes=8 * mebi),
    )(routes.T, route_weight.T)


def norm_kernel(tokens_ref, gain_ref, *part_refs):
    as_float = tokens_ref[...].astype(jnp.float32)
    mean = jnp.mean(as_float * as_float, axis=-1, keepdims=True)
    normed = (as_float * lax.rsqrt(mean + 1e-06) * gain_ref[...]).astype(jnp.bfloat16)
    width = part_refs[0].shape[1]
    for chunk, part_ref in enumerate(part_refs):
        part_ref[...] = normed[:, chunk * width : (chunk + 1) * width]


def normed_parts(tokens, norm_gain, chunks):
    token_count, feature_dim = tokens.shape
    part = jax.ShapeDtypeStruct((token_count, feature_dim // chunks), jnp.bfloat16)
    return pl.pallas_call(
        norm_kernel,
        in_specs=[pl.BlockSpec(memory_space=pltpu.VMEM)] * 2,
        out_specs=[pl.BlockSpec(memory_space=pltpu.VMEM)] * chunks,
        out_shape=[part] * chunks,
        compiler_params=pltpu.CompilerParams(vmem_limit_bytes=16 * mebi),
    )(tokens, norm_gain.reshape(1, feature_dim))


def slot_sources(z, dp):
    low = z < 2
    column = z, z ^ 1, jnp.where(low, 2, 1), jnp.where(low, 3, 0)
    early = [(column[i], side) for side in (0, 2) for i in range(3)]
    late = [(column[3], side) for side in (0, 2)]
    return [
        from_z * 4 + (dp ^ (side + core))
        for group in (early, late)
        for core in (0, 1)
        for from_z, side in group
    ]


def table_kernel(place_ref, choices_ref, *refs):
    picker_refs, spread_ref, scale_ref = refs[:3], refs[3], refs[4]
    experts = scale_ref.shape[0]
    token_count = choices_ref.shape[2]
    early, late = picker_refs[0].shape[0], picker_refs[2].shape[0] // 2
    place = lax.broadcasted_iota(jnp.int32, (experts, slots, token_count), 1).astype(jnp.float32)
    sources = slot_sources(place_ref[0], place_ref[1])
    for slot, source in enumerate(sources):
        choice = choices_ref[source]
        match = choice[:experts][:, None, :] == place
        weight = jnp.where(match, choice[experts:][:, None, :], 0.0)
        scale_ref[:, slot * slots : (slot + 1) * slots, :] = jnp.sum(weight, axis=2, keepdims=True)
        picker = jnp.where(match, 1.0, 0.0).reshape(experts * slots, token_count)
        if slot < 2 * early:
            picker_refs[slot // early][slot % early] = picker.astype(jnp.bfloat16)
        else:
            picker_refs[2][slot - 2 * early] = picker.astype(jnp.bfloat16)
        spread_ref[slot] = picker.T.astype(jnp.bfloat16)


def tables(place, choices, experts):
    count, _, token_count = choices.shape
    rows = experts * slots
    late = count // 8
    early = count // 2 - late
    shapes = [(early, rows, token_count), (early, rows, token_count), (2 * late, rows, token_count)]
    shapes = [jax.ShapeDtypeStruct(shape, jnp.bfloat16) for shape in shapes]
    shapes.append(jax.ShapeDtypeStruct((count, token_count, rows), jnp.bfloat16))
    shapes.append(jax.ShapeDtypeStruct((experts, count * slots, 1), jnp.float32))
    return pl.pallas_call(
        table_kernel,
        in_specs=[
            pl.BlockSpec(memory_space=pltpu.SMEM),
            pl.BlockSpec(memory_space=pltpu.VMEM),
        ],
        out_specs=[pl.BlockSpec(memory_space=pltpu.VMEM)] * 5,
        out_shape=shapes,
        compiler_params=pltpu.CompilerParams(vmem_limit_bytes=grant(count, 12)),
    )(place, choices)


def pair_kernel(count, *refs):
    token_refs = refs[:count]
    mine_ref, theirs_ref, mine_rows_ref, theirs_rows_ref = refs[count:]
    experts = mine_rows_ref.shape[0]
    for source in range(count):
        for picker_ref, rows_ref in ((mine_ref, mine_rows_ref), (theirs_ref, theirs_rows_ref)):
            picked = jnp.dot(
                picker_ref[source], token_refs[source][...], preferred_element_type=jnp.float32
            ).astype(jnp.bfloat16)
            rows_ref[:, source] = picked.reshape(experts, slots, picked.shape[1])


def pick_pair(blocks, mine, theirs, experts):
    count = len(blocks)
    token_count, width = blocks[0].shape
    rows = jax.ShapeDtypeStruct((experts, count, slots, width), jnp.bfloat16)
    return pl.pallas_call(
        functools.partial(pair_kernel, count),
        in_specs=[pl.BlockSpec(memory_space=pltpu.VMEM)] * (count + 2),
        out_specs=[pl.BlockSpec(memory_space=pltpu.VMEM)] * 2,
        out_shape=[rows, rows],
        compiler_params=pltpu.CompilerParams(vmem_limit_bytes=grant(count, 16)),
        cost_estimate=pl.CostEstimate(
            flops=4 * count * experts * slots * token_count * width,
            bytes_accessed=2 * count * width * (token_count + 2 * experts * slots),
            transcendentals=0,
        ),
    )(*blocks, mine, theirs)


def hidden_kernel(chunks, groups, late, *refs):
    row_refs = refs[: chunks * groups]
    refs = refs[chunks * groups :]
    late_refs = refs[: chunks * late]
    refs = refs[chunks * late :]
    width = row_refs[0].shape[-1]
    if late:
        picker_ref, scale_ref, gate_ref, up_ref, hidden_ref, late_rows = refs

        @pl.when(pl.program_id(0) == 0)
        def _():
            for chunk in range(chunks):
                for source in range(late):
                    picked = jnp.dot(
                        picker_ref[source],
                        late_refs[chunk * late + source][...],
                        preferred_element_type=jnp.float32,
                    ).astype(jnp.bfloat16)
                    late_rows[:, source, :, chunk * width : (chunk + 1) * width] = picked.reshape(
                        late_rows.shape[0], slots, width
                    )

    else:
        scale_ref, gate_ref, up_ref, hidden_ref = refs
    gate_part = None
    for chunk in range(chunks):
        pieces = [ref[0] for ref in row_refs[chunk * groups : (chunk + 1) * groups]]
        if late:
            extra = late_rows[pl.program_id(0), :, :, chunk * width : (chunk + 1) * width]
            pieces.append(extra.reshape(late * slots, width))
        rows = jnp.concatenate(pieces, axis=0)
        depth = pl.ds(chunk * width, width)
        gate_add = jnp.dot(rows, gate_ref[0, depth, :], preferred_element_type=jnp.float32)
        up_add = jnp.dot(rows, up_ref[0, depth, :], preferred_element_type=jnp.float32)
        if gate_part is None:
            gate_part, up_part = gate_add, up_add
        else:
            gate_part, up_part = gate_part + gate_add, up_part + up_add
    hidden = gate_part / (1.0 + jnp.exp(-gate_part)) * up_part * scale_ref[0]
    hidden_ref[0] = hidden.astype(jnp.bfloat16)


def hidden_rows(row_chunks, late_chunks, late_picker, scale, w_gate, w_up):
    experts, feature_dim, hidden_dim = w_gate.shape
    chunks, groups, late = len(row_chunks), len(row_chunks[0]), len(late_chunks[0])
    pieces = [piece for row_groups in row_chunks for piece in row_groups]
    late_pieces = [piece for blocks in late_chunks for piece in blocks]
    scratch = []
    if late:
        late_pieces.append(late_picker)
        scratch = [pltpu.VMEM((experts, late, slots, feature_dim), jnp.bfloat16)]
    whole = scale.shape[1]
    return pl.pallas_call(
        functools.partial(hidden_kernel, chunks, groups, late),
        grid=(experts,),
        in_specs=[pl.BlockSpec((1,) + piece.shape[1:], lambda e: (e, 0, 0)) for piece in pieces]
        + [pl.BlockSpec(memory_space=pltpu.VMEM)] * len(late_pieces)
        + [
            pl.BlockSpec((1, whole, 1), lambda e: (e, 0, 0)),
            pl.BlockSpec((1, feature_dim, hidden_dim), lambda e: (e, 0, 0)),
            pl.BlockSpec((1, feature_dim, hidden_dim), lambda e: (e, 0, 0)),
        ],
        out_specs=pl.BlockSpec((1, whole, hidden_dim), lambda e: (e, 0, 0)),
        out_shape=jax.ShapeDtypeStruct((experts, whole, hidden_dim), jnp.bfloat16),
        scratch_shapes=scratch,
        compiler_params=pltpu.CompilerParams(vmem_limit_bytes=grant(whole // slots, 32)),
        cost_estimate=pl.CostEstimate(
            flops=4 * experts * whole * feature_dim * hidden_dim,
            bytes_accessed=4 * experts * feature_dim * hidden_dim,
            transcendentals=experts * whole * hidden_dim,
        ),
    )(*pieces, *late_pieces, scale, w_gate, w_up)


def mix_kernel(order, hidden_ref, down_ref, spread_ref, first_ref, second_ref, made):
    step = pl.program_id(0)
    group = hidden_ref.shape[0]
    sources = spread_ref.shape[0]
    width = down_ref.shape[2]
    for one in range(group):
        made[step * group + one] = (
            jnp.dot(hidden_ref[one], down_ref[one], preferred_element_type=jnp.float32)
            .astype(jnp.bfloat16)
            .reshape(sources, slots, width)
        )

    @pl.when(step == pl.num_programs(0) - 1)
    def _():
        for source in range(sources):
            rows = made[:, source].reshape(spread_ref.shape[2], width)
            mixed = jnp.dot(
                spread_ref[source], rows, preferred_element_type=jnp.float32
            ).astype(jnp.bfloat16)
            if order[source] < sources // 2:
                first_ref[order[source]] = mixed
            else:
                second_ref[order[source] - sources // 2] = mixed


def mix_rows(hidden, w_down, spread, order, chunk, chunks):
    experts, whole, hidden_dim = hidden.shape
    width = w_down.shape[2] // chunks
    sources, token_count, local_rows = spread.shape
    group = 2 if experts % 2 == 0 else 1
    half = jax.ShapeDtypeStruct((sources // 2, token_count, width), jnp.bfloat16)
    return pl.pallas_call(
        functools.partial(mix_kernel, order),
        grid=(experts // group,),
        in_specs=[
            pl.BlockSpec((group, whole, hidden_dim), lambda e: (e, 0, 0)),
            pl.BlockSpec((group, hidden_dim, width), lambda e: (e, 0, chunk)),
            pl.BlockSpec(memory_space=pltpu.VMEM),
        ],
        out_specs=[pl.BlockSpec(memory_space=pltpu.VMEM)] * 2,
        out_shape=[half, half],
        scratch_shapes=[pltpu.VMEM((experts, sources, slots, width), jnp.bfloat16)],
        compiler_params=pltpu.CompilerParams(vmem_limit_bytes=grant(sources, 28)),
        cost_estimate=pl.CostEstimate(
            flops=2 * experts * whole * hidden_dim * width
            + 2 * sources * token_count * local_rows * width,
            bytes_accessed=2 * experts * hidden_dim * (width + whole)
            + 2 * sources * token_count * width,
            transcendentals=0,
        ),
    )(hidden, w_down, spread)


axes = ("expert", "dp")


def pairs_of(expert_pairs, dp_pairs, dp_size):
    return [
        (e_from * dp_size + d_from, e_to * dp_size + d_to)
        for e_from, e_to in expert_pairs
        for d_from, d_to in dp_pairs
    ]


stay_z = [(i, i) for i in range(4)]
stay_dp = [(i, i) for i in range(4)]
swap_z = pairs_of([(0, 1), (1, 0), (2, 3), (3, 2)], stay_dp, 4)
middle_z = pairs_of([(1, 2), (2, 1)], stay_dp, 4)
outward_z = pairs_of([(1, 0), (2, 3)], stay_dp, 4)
inward_z = pairs_of([(0, 1), (3, 2)], stay_dp, 4)
swap_x = pairs_of(stay_z, [(0, 2), (2, 0), (1, 3), (3, 1)], 4)
swap_core = pairs_of(stay_z, [(0, 1), (1, 0), (2, 3), (3, 2)], 4)


def send(value, pairs):
    return lax.ppermute(value, axes, pairs)


def together(*values):
    return lax.optimization_barrier(values)


def tree_start(own, *others):
    return together(send(own, swap_z), send(own, middle_z), send(own, swap_x), *others)


def tree_second(near, middle, *others):
    return together(
        send(near, middle_z), send(middle, outward_z), send(near, swap_x), *others
    )


def tree_third(cross, outer, middle, edge, *others):
    third = jnp.where(edge, outer, middle)
    far, third_x, *others = together(send(cross, outward_z), send(third, swap_x), *others)
    return third, third_x, jnp.where(edge, far, cross), *others


def tree_rest(early, fourth, mine, theirs, experts):
    mine_rows, theirs_rows = pick_pair(early, mine, theirs, experts)
    fourth_x, theirs_rows = together(send(fourth, swap_x), send(theirs_rows, swap_core))
    late = [fourth, fourth_x]
    return [mine_rows, theirs_rows], late + [send(block, swap_core) for block in late]


def chip_sums(mine, theirs):
    return rounded_sum(mine, send(theirs, swap_core))


def tree_return(chip, near_by_z):
    own, near, third, own_x, near_x, third_x, fourth, fourth_x = [chip[i] for i in range(8)]
    if near_by_z:
        near_x = send(near_x, swap_z)
    fourth_in, third_x, near_x, own_x = together(send(fourth_x, swap_x), third_x, near_x, own_x)
    if near_by_z:
        own_x = rounded_sum(own_x, near_x)
    fourth = rounded_sum(fourth, fourth_in)
    far, third_in, near_x, own_x = together(
        send(fourth, inward_z), send(third_x, swap_x), near_x, own_x
    )
    cross = rounded_sum(fourth, far)
    third = rounded_sum(third, third_in)
    outer, crossed, by_x, own_x = together(
        send(third, inward_z),
        send(cross, middle_z),
        send(own_x if near_by_z else near_x, swap_x),
        own_x,
    )
    middle = rounded_sum(third, outer)
    if near_by_z:
        near = rounded_sum(near, crossed)
        own_in = by_x
    else:
        near = rounded_sum(near, by_x, crossed)
        own_in = send(own_x, swap_x)
    return rounded_sum(own, own_in, send(middle, middle_z), send(near, swap_z))


def shards(tokens, routes, route_weight, norm_gain, w_gate, w_up, w_down):
    token_count, top_count = routes.shape
    feature_dim = tokens.shape[1]
    expert_size = lax.axis_size("expert")
    dp_size = lax.axis_size("dp")
    device_count = expert_size * dp_size
    local_count = w_gate.shape[0]
    as_tree = expert_size == 4 and dp_size == 4
    edge = (lax.axis_index("expert") % 3) == 0

    width = feature_dim // gather_chunks
    parts = normed_parts(tokens, norm_gain, gather_chunks)
    if as_tree:
        choice = ranked(routes, route_weight, device_count, local_count)
        firsts = []
        for part in parts:
            if not firsts:
                near, middle, own_x, choice = tree_start(part, choice)
            else:
                near, middle, own_x = tree_start(part)
            firsts.append((near, middle, own_x))
    else:
        every = jnp.arange(device_count * local_count, dtype=jnp.int32)
        same = routes[:, :, None] == every
        named = jnp.any(same, axis=1)
        named_weight = jnp.sum(jnp.where(same, route_weight[:, :, None], 0.0), axis=1)
        count = jnp.arange(token_count)
        before = (count[:, None] > count[None, :]).astype(jnp.bfloat16)
        rank = jnp.dot(before, named.astype(jnp.bfloat16), preferred_element_type=jnp.float32)
        rank = jnp.where(named, rank, -1.0)
        choice = jnp.stack([rank.T, named_weight.T])
        choice = choice.reshape(2, device_count, local_count, token_count).transpose(1, 0, 2, 3)
        choice = choice.reshape(device_count, 2 * local_count, token_count)
    choices = lax.all_to_all(choice, axes, split_axis=0, concat_axis=0, tiled=True)
    if as_tree:
        place = jnp.stack([lax.axis_index("expert"), lax.axis_index("dp")])
        seconds = []
        for near, middle, own_x in firsts:
            if not seconds:
                cross, outer, near_x, choices = tree_second(near, middle, choices)
            else:
                cross, outer, near_x = tree_second(near, middle)
            seconds.append((cross, outer, near_x))
        mine, theirs, late_picker, spread, scale = tables(place, choices, local_count)
        theirs = send(theirs, swap_core)
        thirds = []
        for (near, middle, own_x), (cross, outer, near_x) in zip(firsts, seconds):
            if not thirds:
                third, third_x, fourth, theirs = tree_third(cross, outer, middle, edge, theirs)
            else:
                third, third_x, fourth = tree_third(cross, outer, middle, edge)
            thirds.append((third, third_x, fourth))
        order = (0, 1, 2, 3, 4, 5, 8, 9, 10, 11, 12, 13, 6, 7, 14, 15)
        row_chunks, late_chunks = [], []
        for part, (near, middle, own_x), (cross, outer, near_x), (third, third_x, fourth) in zip(
            parts, firsts, seconds, thirds
        ):
            early = part, near, third, own_x, near_x, third_x
            rows, late = tree_rest(early, fourth, mine, theirs, local_count)
            row_chunks.append([rows_of.reshape(local_count, -1, width) for rows_of in rows])
            late_chunks.append(late)
    else:
        rank, named_weight = choices[:, :local_count], choices[:, local_count:]
        match = rank[:, :, None, :] == jnp.arange(slots, dtype=jnp.float32)[None, None, :, None]
        picker = match.astype(jnp.bfloat16).reshape(device_count, local_count * slots, token_count)
        scale = jnp.sum(jnp.where(match, named_weight[:, :, None, :], 0.0), axis=3)
        scale = scale.transpose(1, 0, 2).reshape(local_count, device_count * slots, 1)
        spread = picker.transpose(0, 2, 1)
        rows = [pick_rows(picker, lax.all_gather(part, axes), local_count) for part in parts]
        row_chunks = [[rows_of.reshape(local_count, -1, width)] for rows_of in rows]
        late_chunks, late_picker = [[]] * gather_chunks, None
        order = tuple(range(device_count))
    hidden = hidden_rows(row_chunks, late_chunks, late_picker, scale, w_gate, w_up)

    sums = []
    for chunk in range(return_chunks):
        mine, theirs = mix_rows(hidden, w_down, spread, order, chunk, return_chunks)
        if as_tree:
            sums.append(chip_sums(mine, theirs))
        else:
            whole = jnp.concatenate([mine, theirs], axis=0).astype(jnp.float32)
            total = lax.psum_scatter(whole, axes, scatter_dimension=0)
            sums.append(total.astype(jnp.bfloat16))
    results = sums
    if as_tree:
        results = [tree_return(chip, chunk % 2 == 1) for chunk, chip in enumerate(sums)]
    return jnp.concatenate(results, axis=1)


def solution(mesh):
    split = P(("groups", "expert", "dp"), None)
    by_expert = P(("expert", "dp"), None, None)
    return jax.shard_map(
        shards,
        mesh=mesh,
        in_specs=(split, split, split, P(), by_expert, by_expert, by_expert),
        out_specs=split,
        check_vma=False,
    )
```

```python
import functools

import jax
import jax.numpy as jnp
from jax import lax
from jax.experimental import pallas as pl
from jax.experimental.pallas import tpu as pltpu
from jax.sharding import PartitionSpec as P

slots = 16
gather_chunks = 2
return_chunks = 2
mebi = 1024 * 1024


def grant(sources, tree_mebi):
    return (tree_mebi if sources <= 16 else 56) * mebi


def rounded_sum(first, *others):
    total = first.astype(jnp.float32)
    for other in others:
        total = total + other.astype(jnp.float32)
    return total.astype(jnp.bfloat16)


def pick_kernel(picker_ref, tokens_ref, rows_ref):
    sources = tokens_ref.shape[0]
    experts = rows_ref.shape[0]
    for source in range(sources):
        picked = jnp.dot(
            picker_ref[source], tokens_ref[source], preferred_element_type=jnp.float32
        ).astype(jnp.bfloat16)
        for expert in range(experts):
            rows_ref[expert, source] = picked[expert * slots : (expert + 1) * slots]


def pick_rows(picker, tokens, experts):
    sources, token_count, width = tokens.shape
    block = min(sources, 8)
    return pl.pallas_call(
        pick_kernel,
        grid=(sources // block,),
        in_specs=[
            pl.BlockSpec((block, experts * slots, token_count), lambda i: (i, 0, 0)),
            pl.BlockSpec((block, token_count, width), lambda i: (i, 0, 0)),
        ],
        out_specs=pl.BlockSpec((experts, block, slots, width), lambda i: (0, i, 0, 0)),
        out_shape=jax.ShapeDtypeStruct((experts, sources, slots, width), jnp.bfloat16),
        compiler_params=pltpu.CompilerParams(vmem_limit_bytes=grant(sources, 16)),
        cost_estimate=pl.CostEstimate(
            flops=2 * sources * experts * slots * token_count * width,
            bytes_accessed=2 * sources * width * (token_count + experts * slots),
            transcendentals=0,
        ),
    )(picker, tokens)


def rank_kernel(routes_ref, weight_ref, choice_ref):
    top_count, token_count = routes_ref.shape
    devices, experts = choice_ref.shape[0], choice_ref.shape[1] // 2
    shape = devices * experts, token_count
    every = lax.broadcasted_iota(jnp.int32, shape, 0)
    named, weight = jnp.zeros(shape, jnp.float32), jnp.zeros(shape, jnp.float32)
    for k in range(top_count):
        same = routes_ref[k : k + 1, :] == every
        named = jnp.where(same, 1.0, named)
        weight = jnp.where(same, weight_ref[k : k + 1, :], weight)
    square = token_count, token_count
    before = lax.broadcasted_iota(jnp.int32, square, 0) < lax.broadcasted_iota(jnp.int32, square, 1)
    before = jnp.where(before, 1.0, 0.0).astype(jnp.bfloat16)
    rank = jnp.dot(named.astype(jnp.bfloat16), before, preferred_element_type=jnp.float32)
    rank = jnp.where(named > 0.0, rank, -1.0)
    choice_ref[:, :experts] = rank.reshape(devices, experts, token_count)
    choice_ref[:, experts:] = weight.reshape(devices, experts, token_count)


def ranked(routes, route_weight, devices, experts):
    token_count = routes.shape[0]
    return pl.pallas_call(
        rank_kernel,
        in_specs=[pl.BlockSpec(memory_space=pltpu.VMEM)] * 2,
        out_specs=pl.BlockSpec(memory_space=pltpu.VMEM),
        out_shape=jax.ShapeDtypeStruct((devices, 2 * experts, token_count), jnp.float32),
        compiler_params=pltpu.CompilerParams(vmem_limit_bytes=8 * mebi),
    )(routes.T, route_weight.T)


def norm_kernel(tokens_ref, gain_ref, *part_refs):
    as_float = tokens_ref[...].astype(jnp.float32)
    mean = jnp.mean(as_float * as_float, axis=-1, keepdims=True)
    normed = (as_float * lax.rsqrt(mean + 1e-06) * gain_ref[...]).astype(jnp.bfloat16)
    width = part_refs[0].shape[1]
    for chunk, part_ref in enumerate(part_refs):
        part_ref[...] = normed[:, chunk * width : (chunk + 1) * width]


def normed_parts(tokens, norm_gain, chunks):
    token_count, feature_dim = tokens.shape
    part = jax.ShapeDtypeStruct((token_count, feature_dim // chunks), jnp.bfloat16)
    return pl.pallas_call(
        norm_kernel,
        in_specs=[pl.BlockSpec(memory_space=pltpu.VMEM)] * 2,
        out_specs=[pl.BlockSpec(memory_space=pltpu.VMEM)] * chunks,
        out_shape=[part] * chunks,
        compiler_params=pltpu.CompilerParams(vmem_limit_bytes=16 * mebi),
    )(tokens, norm_gain.reshape(1, feature_dim))


def slot_sources(z, dp):
    low = z < 2
    column = z, z ^ 1, jnp.where(low, 2, 1), jnp.where(low, 3, 0)
    early = [(column[i], side) for side in (0, 2) for i in range(3)]
    late = [(column[3], side) for side in (0, 2)]
    return [
        from_z * 4 + (dp ^ (side + core))
        for group in (early, late)
        for core in (0, 1)
        for from_z, side in group
    ]


def table_kernel(place_ref, choices_ref, *refs):
    picker_refs, spread_ref, scale_ref = refs[:3], refs[3], refs[4]
    experts = scale_ref.shape[0]
    token_count = choices_ref.shape[2]
    early, late = picker_refs[0].shape[0], picker_refs[2].shape[0] // 2
    place = lax.broadcasted_iota(jnp.int32, (experts, slots, token_count), 1).astype(jnp.float32)
    sources = slot_sources(place_ref[0], place_ref[1])
    for slot, source in enumerate(sources):
        choice = choices_ref[source]
        match = choice[:experts][:, None, :] == place
        weight = jnp.where(match, choice[experts:][:, None, :], 0.0)
        scale_ref[:, slot * slots : (slot + 1) * slots, :] = jnp.sum(weight, axis=2, keepdims=True)
        picker = jnp.where(match, 1.0, 0.0).reshape(experts * slots, token_count)
        if slot < 2 * early:
            picker_refs[slot // early][slot % early] = picker.astype(jnp.bfloat16)
        else:
            picker_refs[2][slot - 2 * early] = picker.astype(jnp.bfloat16)
        spread = picker.T.astype(jnp.bfloat16)
        blank = jnp.zeros_like(spread)
        halves = (blank, spread) if slot % 2 else (spread, blank)
        token_rows = pl.ds(slot % 2 * token_count, token_count)
        spread_ref[slot // 2, token_rows] = jnp.concatenate(halves, axis=1)


def tables(place, choices, experts):
    count, _, token_count = choices.shape
    rows = experts * slots
    late = count // 8
    early = count // 2 - late
    shapes = [(early, rows, token_count), (early, rows, token_count), (2 * late, rows, token_count)]
    shapes = [jax.ShapeDtypeStruct(shape, jnp.bfloat16) for shape in shapes]
    shapes.append(jax.ShapeDtypeStruct((count // 2, 2 * token_count, 2 * rows), jnp.bfloat16))
    shapes.append(jax.ShapeDtypeStruct((experts, count * slots, 1), jnp.float32))
    return pl.pallas_call(
        table_kernel,
        in_specs=[
            pl.BlockSpec(memory_space=pltpu.SMEM),
            pl.BlockSpec(memory_space=pltpu.VMEM),
        ],
        out_specs=[pl.BlockSpec(memory_space=pltpu.VMEM)] * 5,
        out_shape=shapes,
        compiler_params=pltpu.CompilerParams(vmem_limit_bytes=grant(count, 12)),
    )(place, choices)


def pair_kernel(count, *refs):
    token_refs = refs[:count]
    mine_ref, theirs_ref, mine_rows_ref, theirs_rows_ref = refs[count:]
    experts = mine_rows_ref.shape[0]
    for source in range(count):
        for picker_ref, rows_ref in ((mine_ref, mine_rows_ref), (theirs_ref, theirs_rows_ref)):
            picked = jnp.dot(
                picker_ref[source], token_refs[source][...], preferred_element_type=jnp.float32
            ).astype(jnp.bfloat16)
            rows_ref[:, source] = picked.reshape(experts, slots, picked.shape[1])


def pick_pair(blocks, mine, theirs, experts):
    count = len(blocks)
    token_count, width = blocks[0].shape
    rows = jax.ShapeDtypeStruct((experts, count, slots, width), jnp.bfloat16)
    return pl.pallas_call(
        functools.partial(pair_kernel, count),
        in_specs=[pl.BlockSpec(memory_space=pltpu.VMEM)] * (count + 2),
        out_specs=[pl.BlockSpec(memory_space=pltpu.VMEM)] * 2,
        out_shape=[rows, rows],
        compiler_params=pltpu.CompilerParams(vmem_limit_bytes=grant(count, 16)),
        cost_estimate=pl.CostEstimate(
            flops=4 * count * experts * slots * token_count * width,
            bytes_accessed=2 * count * width * (token_count + 2 * experts * slots),
            transcendentals=0,
        ),
    )(*blocks, mine, theirs)


def hidden_kernel(chunks, groups, late, *refs):
    row_refs = refs[: chunks * groups]
    refs = refs[chunks * groups :]
    late_refs = refs[: chunks * late]
    refs = refs[chunks * late :]
    width = row_refs[0].shape[-1]
    if late:
        picker_ref, scale_ref, gate_ref, up_ref, hidden_ref, late_rows = refs

        @pl.when(pl.program_id(0) == 0)
        def _():
            for chunk in range(chunks):
                for source in range(late):
                    picked = jnp.dot(
                        picker_ref[source],
                        late_refs[chunk * late + source][...],
                        preferred_element_type=jnp.float32,
                    ).astype(jnp.bfloat16)
                    late_rows[:, source, :, chunk * width : (chunk + 1) * width] = picked.reshape(
                        late_rows.shape[0], slots, width
                    )

    else:
        scale_ref, gate_ref, up_ref, hidden_ref = refs
    gate_part = None
    for chunk in range(chunks):
        pieces = [ref[0] for ref in row_refs[chunk * groups : (chunk + 1) * groups]]
        if late:
            extra = late_rows[pl.program_id(0), :, :, chunk * width : (chunk + 1) * width]
            pieces.append(extra.reshape(late * slots, width))
        rows = jnp.concatenate(pieces, axis=0)
        depth = pl.ds(chunk * width, width)
        gate_add = jnp.dot(rows, gate_ref[0, depth, :], preferred_element_type=jnp.float32)
        up_add = jnp.dot(rows, up_ref[0, depth, :], preferred_element_type=jnp.float32)
        if gate_part is None:
            gate_part, up_part = gate_add, up_add
        else:
            gate_part, up_part = gate_part + gate_add, up_part + up_add
    hidden = gate_part / (1.0 + jnp.exp(-gate_part)) * up_part * scale_ref[0]
    hidden_ref[0] = hidden.astype(jnp.bfloat16)


def hidden_rows(row_chunks, late_chunks, late_picker, scale, w_gate, w_up):
    experts, feature_dim, hidden_dim = w_gate.shape
    chunks, groups, late = len(row_chunks), len(row_chunks[0]), len(late_chunks[0])
    pieces = [piece for row_groups in row_chunks for piece in row_groups]
    late_pieces = [piece for blocks in late_chunks for piece in blocks]
    scratch = []
    if late:
        late_pieces.append(late_picker)
        scratch = [pltpu.VMEM((experts, late, slots, feature_dim), jnp.bfloat16)]
    whole = scale.shape[1]
    return pl.pallas_call(
        functools.partial(hidden_kernel, chunks, groups, late),
        grid=(experts,),
        in_specs=[pl.BlockSpec((1,) + piece.shape[1:], lambda e: (e, 0, 0)) for piece in pieces]
        + [pl.BlockSpec(memory_space=pltpu.VMEM)] * len(late_pieces)
        + [
            pl.BlockSpec((1, whole, 1), lambda e: (e, 0, 0)),
            pl.BlockSpec((1, feature_dim, hidden_dim), lambda e: (e, 0, 0)),
            pl.BlockSpec((1, feature_dim, hidden_dim), lambda e: (e, 0, 0)),
        ],
        out_specs=pl.BlockSpec((1, whole, hidden_dim), lambda e: (e, 0, 0)),
        out_shape=jax.ShapeDtypeStruct((experts, whole, hidden_dim), jnp.bfloat16),
        scratch_shapes=scratch,
        compiler_params=pltpu.CompilerParams(vmem_limit_bytes=grant(whole // slots, 32)),
        cost_estimate=pl.CostEstimate(
            flops=4 * experts * whole * feature_dim * hidden_dim,
            bytes_accessed=4 * experts * feature_dim * hidden_dim,
            transcendentals=experts * whole * hidden_dim,
        ),
    )(*pieces, *late_pieces, scale, w_gate, w_up)


def mix_kernel(order, hidden_ref, down_ref, spread_ref, first_ref, second_ref, made):
    step = pl.program_id(0)
    group = hidden_ref.shape[0]
    sources = made.shape[1]
    width = down_ref.shape[2]
    for one in range(group):
        made[step * group + one] = (
            jnp.dot(hidden_ref[one], down_ref[one], preferred_element_type=jnp.float32)
            .astype(jnp.bfloat16)
            .reshape(sources, slots, width)
        )

    @pl.when(step == pl.num_programs(0) - 1)
    def _():
        local_rows, token_count = spread_ref.shape[2] // 2, spread_ref.shape[1] // 2
        for pair in range(sources // 2):
            rows = [made[:, 2 * pair + i].reshape(local_rows, width) for i in (0, 1)]
            mixed = jnp.dot(
                spread_ref[pair], jnp.concatenate(rows, axis=0), preferred_element_type=jnp.float32
            ).astype(jnp.bfloat16)
            for i in (0, 1):
                to = order[2 * pair + i]
                out_ref = first_ref if to < sources // 2 else second_ref
                out_ref[to % (sources // 2)] = mixed[i * token_count : (i + 1) * token_count]


def mix_rows(hidden, w_down, spread, order, chunk, chunks):
    experts, whole, hidden_dim = hidden.shape
    width = w_down.shape[2] // chunks
    pairs, token_count, local_rows = spread.shape
    sources, token_count, local_rows = 2 * pairs, token_count // 2, local_rows // 2
    group = 2 if experts % 2 == 0 else 1
    half = jax.ShapeDtypeStruct((sources // 2, token_count, width), jnp.bfloat16)
    return pl.pallas_call(
        functools.partial(mix_kernel, order),
        grid=(experts // group,),
        in_specs=[
            pl.BlockSpec((group, whole, hidden_dim), lambda e: (e, 0, 0)),
            pl.BlockSpec((group, hidden_dim, width), lambda e: (e, 0, chunk)),
            pl.BlockSpec(memory_space=pltpu.VMEM),
        ],
        out_specs=[pl.BlockSpec(memory_space=pltpu.VMEM)] * 2,
        out_shape=[half, half],
        scratch_shapes=[pltpu.VMEM((experts, sources, slots, width), jnp.bfloat16)],
        compiler_params=pltpu.CompilerParams(vmem_limit_bytes=grant(sources, 28)),
        cost_estimate=pl.CostEstimate(
            flops=2 * experts * whole * hidden_dim * width
            + 2 * sources * token_count * local_rows * width,
            bytes_accessed=2 * experts * hidden_dim * (width + whole)
            + 2 * sources * token_count * width,
            transcendentals=0,
        ),
    )(hidden, w_down, spread)


axes = ("expert", "dp")


def pairs_of(expert_pairs, dp_pairs, dp_size):
    return [
        (e_from * dp_size + d_from, e_to * dp_size + d_to)
        for e_from, e_to in expert_pairs
        for d_from, d_to in dp_pairs
    ]


stay_z = [(i, i) for i in range(4)]
stay_dp = [(i, i) for i in range(4)]
swap_z = pairs_of([(0, 1), (1, 0), (2, 3), (3, 2)], stay_dp, 4)
middle_z = pairs_of([(1, 2), (2, 1)], stay_dp, 4)
outward_z = pairs_of([(1, 0), (2, 3)], stay_dp, 4)
inward_z = pairs_of([(0, 1), (3, 2)], stay_dp, 4)
swap_x = pairs_of(stay_z, [(0, 2), (2, 0), (1, 3), (3, 1)], 4)
swap_core = pairs_of(stay_z, [(0, 1), (1, 0), (2, 3), (3, 2)], 4)


def send(value, pairs):
    return lax.ppermute(value, axes, pairs)


def together(*values):
    return lax.optimization_barrier(values)


def tree_start(own, *others):
    return together(send(own, swap_z), send(own, middle_z), send(own, swap_x), *others)


def tree_second(near, middle, *others):
    return together(
        send(near, middle_z), send(middle, outward_z), send(near, swap_x), *others
    )


def tree_third(cross, outer, middle, edge, *others):
    third = jnp.where(edge, outer, middle)
    far, third_x, *others = together(send(cross, outward_z), send(third, swap_x), *others)
    return third, third_x, jnp.where(edge, far, cross), *others


def tree_rest(early, fourth, mine, theirs, experts):
    mine_rows, theirs_rows = pick_pair(early, mine, theirs, experts)
    late = [fourth, send(fourth, swap_x)]
    return [mine_rows, send(theirs_rows, swap_core)], late + [send(block, swap_core) for block in late]


def chip_sums(mine, theirs):
    return rounded_sum(mine, send(theirs, swap_core))


def tree_return(chip, near_by_z):
    own, near, third, own_x, near_x, third_x, fourth, fourth_x = [chip[i] for i in range(8)]
    if near_by_z:
        near_x = send(near_x, swap_z)
    fourth_in, third_x, near_x, own_x = together(send(fourth_x, swap_x), third_x, near_x, own_x)
    if near_by_z:
        own_x = rounded_sum(own_x, near_x)
    fourth = rounded_sum(fourth, fourth_in)
    far, third_in, near_x, own_x = together(
        send(fourth, inward_z), send(third_x, swap_x), near_x, own_x
    )
    cross = rounded_sum(fourth, far)
    third = rounded_sum(third, third_in)
    outer, crossed, by_x, own_x = together(
        send(third, inward_z),
        send(cross, middle_z),
        send(own_x if near_by_z else near_x, swap_x),
        own_x,
    )
    middle = rounded_sum(third, outer)
    if near_by_z:
        near = rounded_sum(near, crossed)
        own_in = by_x
    else:
        near = rounded_sum(near, by_x, crossed)
        own_in = send(own_x, swap_x)
    return rounded_sum(own, own_in, send(middle, middle_z), send(near, swap_z))


def shards(tokens, routes, route_weight, norm_gain, w_gate, w_up, w_down):
    token_count, top_count = routes.shape
    feature_dim = tokens.shape[1]
    expert_size = lax.axis_size("expert")
    dp_size = lax.axis_size("dp")
    device_count = expert_size * dp_size
    local_count = w_gate.shape[0]
    as_tree = expert_size == 4 and dp_size == 4
    edge = (lax.axis_index("expert") % 3) == 0

    width = feature_dim // gather_chunks
    parts = normed_parts(tokens, norm_gain, gather_chunks)
    if as_tree:
        choice = ranked(routes, route_weight, device_count, local_count)
        firsts = []
        for part in parts:
            if not firsts:
                near, middle, own_x, choice = tree_start(part, choice)
            else:
                near, middle, own_x = tree_start(part)
            firsts.append((near, middle, own_x))
    else:
        every = jnp.arange(device_count * local_count, dtype=jnp.int32)
        same = routes[:, :, None] == every
        named = jnp.any(same, axis=1)
        named_weight = jnp.sum(jnp.where(same, route_weight[:, :, None], 0.0), axis=1)
        count = jnp.arange(token_count)
        before = (count[:, None] > count[None, :]).astype(jnp.bfloat16)
        rank = jnp.dot(before, named.astype(jnp.bfloat16), preferred_element_type=jnp.float32)
        rank = jnp.where(named, rank, -1.0)
        choice = jnp.stack([rank.T, named_weight.T])
        choice = choice.reshape(2, device_count, local_count, token_count).transpose(1, 0, 2, 3)
        choice = choice.reshape(device_count, 2 * local_count, token_count)
    choices = lax.all_to_all(choice, axes, split_axis=0, concat_axis=0, tiled=True)
    if as_tree:
        place = jnp.stack([lax.axis_index("expert"), lax.axis_index("dp")])
        seconds = []
        for near, middle, own_x in firsts:
            if not seconds:
                cross, outer, near_x, choices = tree_second(near, middle, choices)
            else:
                cross, outer, near_x = tree_second(near, middle)
            seconds.append((cross, outer, near_x))
        mine, theirs, late_picker, spread, scale = tables(place, choices, local_count)
        theirs = send(theirs, swap_core)
        thirds = []
        for (near, middle, own_x), (cross, outer, near_x) in zip(firsts, seconds):
            if not thirds:
                third, third_x, fourth, theirs = tree_third(cross, outer, middle, edge, theirs)
            else:
                third, third_x, fourth = tree_third(cross, outer, middle, edge)
            thirds.append((third, third_x, fourth))
        order = (0, 1, 2, 3, 4, 5, 8, 9, 10, 11, 12, 13, 6, 7, 14, 15)
        row_chunks, late_chunks = [], []
        for part, (near, middle, own_x), (cross, outer, near_x), (third, third_x, fourth) in zip(
            parts, firsts, seconds, thirds
        ):
            early = part, near, third, own_x, near_x, third_x
            rows, late = tree_rest(early, fourth, mine, theirs, local_count)
            row_chunks.append([rows_of.reshape(local_count, -1, width) for rows_of in rows])
            late_chunks.append(late)
    else:
        rank, named_weight = choices[:, :local_count], choices[:, local_count:]
        match = rank[:, :, None, :] == jnp.arange(slots, dtype=jnp.float32)[None, None, :, None]
        picker = match.astype(jnp.bfloat16).reshape(device_count, local_count * slots, token_count)
        scale = jnp.sum(jnp.where(match, named_weight[:, :, None, :], 0.0), axis=3)
        scale = scale.transpose(1, 0, 2).reshape(local_count, device_count * slots, 1)
        spread = picker.transpose(0, 2, 1).reshape(device_count // 2, 2, token_count, -1)
        blank = jnp.zeros_like(spread[:, 0])
        spread = jnp.concatenate(
            [
                jnp.concatenate([spread[:, 0], blank], axis=2),
                jnp.concatenate([blank, spread[:, 1]], axis=2),
            ],
            axis=1,
        )
        rows = [pick_rows(picker, lax.all_gather(part, axes), local_count) for part in parts]
        row_chunks = [[rows_of.reshape(local_count, -1, width)] for rows_of in rows]
        late_chunks, late_picker = [[]] * gather_chunks, None
        order = tuple(range(device_count))
    hidden = hidden_rows(row_chunks, late_chunks, late_picker, scale, w_gate, w_up)

    sums = []
    for chunk in range(return_chunks):
        mine, theirs = mix_rows(hidden, w_down, spread, order, chunk, return_chunks)
        if as_tree:
            sums.append(chip_sums(mine, theirs))
        else:
            whole = jnp.concatenate([mine, theirs], axis=0).astype(jnp.float32)
            total = lax.psum_scatter(whole, axes, scatter_dimension=0)
            sums.append(total.astype(jnp.bfloat16))
    results = sums
    if as_tree:
        results = [tree_return(chip, chunk % 2 == 1) for chunk, chip in enumerate(sums)]
    return jnp.concatenate(results, axis=1)


def solution(mesh):
    split = P(("groups", "expert", "dp"), None)
    by_expert = P(("expert", "dp"), None, None)
    return jax.shard_map(
        shards,
        mesh=mesh,
        in_specs=(split, split, split, P(), by_expert, by_expert, by_expert),
        out_specs=split,
        check_vma=False,
    )
```

```python
import functools

import jax
import jax.numpy as jnp
from jax import lax
from jax.experimental import pallas as pl
from jax.experimental.pallas import tpu as pltpu
from jax.sharding import PartitionSpec as P

slots = 16
gather_chunks = 2
return_chunks = 2
mebi = 1024 * 1024


def grant(sources, tree_mebi):
    return (tree_mebi if sources <= 16 else 56) * mebi


def rounded_sum(first, *others):
    total = first.astype(jnp.float32)
    for other in others:
        total = total + other.astype(jnp.float32)
    return total.astype(jnp.bfloat16)


def pick_kernel(picker_ref, tokens_ref, rows_ref):
    sources = tokens_ref.shape[0]
    experts = rows_ref.shape[0]
    for source in range(sources):
        picked = jnp.dot(
            picker_ref[source], tokens_ref[source], preferred_element_type=jnp.float32
        ).astype(jnp.bfloat16)
        for expert in range(experts):
            rows_ref[expert, source] = picked[expert * slots : (expert + 1) * slots]


def pick_rows(picker, tokens, experts):
    sources, token_count, width = tokens.shape
    block = min(sources, 8)
    return pl.pallas_call(
        pick_kernel,
        grid=(sources // block,),
        in_specs=[
            pl.BlockSpec((block, experts * slots, token_count), lambda i: (i, 0, 0)),
            pl.BlockSpec((block, token_count, width), lambda i: (i, 0, 0)),
        ],
        out_specs=pl.BlockSpec((experts, block, slots, width), lambda i: (0, i, 0, 0)),
        out_shape=jax.ShapeDtypeStruct((experts, sources, slots, width), jnp.bfloat16),
        compiler_params=pltpu.CompilerParams(vmem_limit_bytes=grant(sources, 16)),
        cost_estimate=pl.CostEstimate(
            flops=2 * sources * experts * slots * token_count * width,
            bytes_accessed=2 * sources * width * (token_count + experts * slots),
            transcendentals=0,
        ),
    )(picker, tokens)


def rank_kernel(routes_ref, weight_ref, choice_ref):
    top_count, token_count = routes_ref.shape
    devices, experts = choice_ref.shape[0], choice_ref.shape[1] // 2
    shape = devices * experts, token_count
    every = lax.broadcasted_iota(jnp.int32, shape, 0)
    named, weight = jnp.zeros(shape, jnp.float32), jnp.zeros(shape, jnp.float32)
    for k in range(top_count):
        same = routes_ref[k : k + 1, :] == every
        named = jnp.where(same, 1.0, named)
        weight = jnp.where(same, weight_ref[k : k + 1, :], weight)
    square = token_count, token_count
    before = lax.broadcasted_iota(jnp.int32, square, 0) < lax.broadcasted_iota(jnp.int32, square, 1)
    before = jnp.where(before, 1.0, 0.0).astype(jnp.bfloat16)
    rank = jnp.dot(named.astype(jnp.bfloat16), before, preferred_element_type=jnp.float32)
    rank = jnp.where(named > 0.0, rank, -1.0)
    choice_ref[:, :experts] = rank.reshape(devices, experts, token_count)
    choice_ref[:, experts:] = weight.reshape(devices, experts, token_count)


def ranked(routes, route_weight, devices, experts):
    token_count = routes.shape[0]
    return pl.pallas_call(
        rank_kernel,
        in_specs=[pl.BlockSpec(memory_space=pltpu.VMEM)] * 2,
        out_specs=pl.BlockSpec(memory_space=pltpu.VMEM),
        out_shape=jax.ShapeDtypeStruct((devices, 2 * experts, token_count), jnp.float32),
        compiler_params=pltpu.CompilerParams(vmem_limit_bytes=8 * mebi),
    )(routes.T, route_weight.T)


def norm_kernel(tokens_ref, gain_ref, *part_refs):
    as_float = tokens_ref[...].astype(jnp.float32)
    mean = jnp.mean(as_float * as_float, axis=-1, keepdims=True)
    normed = (as_float * lax.rsqrt(mean + 1e-06) * gain_ref[...]).astype(jnp.bfloat16)
    width = part_refs[0].shape[1]
    for chunk, part_ref in enumerate(part_refs):
        part_ref[...] = normed[:, chunk * width : (chunk + 1) * width]


def normed_parts(tokens, norm_gain, chunks):
    token_count, feature_dim = tokens.shape
    part = jax.ShapeDtypeStruct((token_count, feature_dim // chunks), jnp.bfloat16)
    return pl.pallas_call(
        norm_kernel,
        in_specs=[pl.BlockSpec(memory_space=pltpu.VMEM)] * 2,
        out_specs=[pl.BlockSpec(memory_space=pltpu.VMEM)] * chunks,
        out_shape=[part] * chunks,
        compiler_params=pltpu.CompilerParams(vmem_limit_bytes=16 * mebi),
    )(tokens, norm_gain.reshape(1, feature_dim))


def slot_sources(z, dp):
    low = z < 2
    column = z, z ^ 1, jnp.where(low, 2, 1), jnp.where(low, 3, 0)
    early = [(column[i], side) for side in (0, 2) for i in (0, 1)]
    late = [(column[i], side) for side in (0, 2) for i in (2, 3)]
    return [
        from_z * 4 + (dp ^ (side + core))
        for group in (early, late)
        for core in (0, 1)
        for from_z, side in group
    ]


def table_kernel(place_ref, choices_ref, *refs):
    picker_refs, spread_ref, scale_ref = refs[:3], refs[3], refs[4]
    experts = scale_ref.shape[0]
    token_count = choices_ref.shape[2]
    early, late = picker_refs[0].shape[0], picker_refs[2].shape[0] // 2
    place = lax.broadcasted_iota(jnp.int32, (experts, slots, token_count), 1).astype(jnp.float32)
    sources = slot_sources(place_ref[0], place_ref[1])
    for slot, source in enumerate(sources):
        choice = choices_ref[source]
        match = choice[:experts][:, None, :] == place
        weight = jnp.where(match, choice[experts:][:, None, :], 0.0)
        scale_ref[:, slot * slots : (slot + 1) * slots, :] = jnp.sum(weight, axis=2, keepdims=True)
        picker = jnp.where(match, 1.0, 0.0).reshape(experts * slots, token_count)
        if slot < 2 * early:
            picker_refs[slot // early][slot % early] = picker.astype(jnp.bfloat16)
        else:
            picker_refs[2][slot - 2 * early] = picker.astype(jnp.bfloat16)
        spread_ref[slot] = picker.T.astype(jnp.bfloat16)


def tables(place, choices, experts):
    count, _, token_count = choices.shape
    rows = experts * slots
    late = count // 4
    early = count // 2 - late
    shapes = [(early, rows, token_count), (early, rows, token_count), (2 * late, rows, token_count)]
    shapes = [jax.ShapeDtypeStruct(shape, jnp.bfloat16) for shape in shapes]
    shapes.append(jax.ShapeDtypeStruct((count, token_count, rows), jnp.bfloat16))
    shapes.append(jax.ShapeDtypeStruct((experts, count * slots, 1), jnp.float32))
    return pl.pallas_call(
        table_kernel,
        in_specs=[
            pl.BlockSpec(memory_space=pltpu.SMEM),
            pl.BlockSpec(memory_space=pltpu.VMEM),
        ],
        out_specs=[pl.BlockSpec(memory_space=pltpu.VMEM)] * 5,
        out_shape=shapes,
        compiler_params=pltpu.CompilerParams(vmem_limit_bytes=grant(count, 12)),
    )(place, choices)


def pair_kernel(count, *refs):
    token_refs = refs[:count]
    mine_ref, theirs_ref, mine_rows_ref, theirs_rows_ref = refs[count:]
    experts = mine_rows_ref.shape[0]
    for source in range(count):
        for picker_ref, rows_ref in ((mine_ref, mine_rows_ref), (theirs_ref, theirs_rows_ref)):
            picked = jnp.dot(
                picker_ref[source], token_refs[source][...], preferred_element_type=jnp.float32
            ).astype(jnp.bfloat16)
            rows_ref[:, source] = picked.reshape(experts, slots, picked.shape[1])


def pick_pair(blocks, mine, theirs, experts):
    count = len(blocks)
    token_count, width = blocks[0].shape
    rows = jax.ShapeDtypeStruct((experts, count, slots, width), jnp.bfloat16)
    return pl.pallas_call(
        functools.partial(pair_kernel, count),
        in_specs=[pl.BlockSpec(memory_space=pltpu.VMEM)] * (count + 2),
        out_specs=[pl.BlockSpec(memory_space=pltpu.VMEM)] * 2,
        out_shape=[rows, rows],
        compiler_params=pltpu.CompilerParams(vmem_limit_bytes=grant(count, 16)),
        cost_estimate=pl.CostEstimate(
            flops=4 * count * experts * slots * token_count * width,
            bytes_accessed=2 * count * width * (token_count + 2 * experts * slots),
            transcendentals=0,
        ),
    )(*blocks, mine, theirs)


def hidden_kernel(chunks, groups, late, *refs):
    row_refs = refs[: chunks * groups]
    refs = refs[chunks * groups :]
    late_refs = refs[: chunks * late]
    refs = refs[chunks * late :]
    width = row_refs[0].shape[-1]
    if late:
        picker_ref, scale_ref, gate_ref, up_ref, hidden_ref, late_rows = refs

        @pl.when(pl.program_id(0) == 0)
        def _():
            for chunk in range(chunks):
                for source in range(late):
                    picked = jnp.dot(
                        picker_ref[source],
                        late_refs[chunk * late + source][...],
                        preferred_element_type=jnp.float32,
                    ).astype(jnp.bfloat16)
                    late_rows[:, source, :, chunk * width : (chunk + 1) * width] = picked.reshape(
                        late_rows.shape[0], slots, width
                    )

    else:
        scale_ref, gate_ref, up_ref, hidden_ref = refs
    gate_part = None
    for chunk in range(chunks):
        pieces = [ref[0] for ref in row_refs[chunk * groups : (chunk + 1) * groups]]
        if late:
            extra = late_rows[pl.program_id(0), :, :, chunk * width : (chunk + 1) * width]
            pieces.append(extra.reshape(late * slots, width))
        rows = jnp.concatenate(pieces, axis=0)
        depth = pl.ds(chunk * width, width)
        gate_add = jnp.dot(rows, gate_ref[0, depth, :], preferred_element_type=jnp.float32)
        up_add = jnp.dot(rows, up_ref[0, depth, :], preferred_element_type=jnp.float32)
        if gate_part is None:
            gate_part, up_part = gate_add, up_add
        else:
            gate_part, up_part = gate_part + gate_add, up_part + up_add
    hidden = gate_part / (1.0 + jnp.exp(-gate_part)) * up_part * scale_ref[0]
    hidden_ref[0] = hidden.astype(jnp.bfloat16)


def hidden_rows(row_chunks, late_chunks, late_picker, scale, w_gate, w_up):
    experts, feature_dim, hidden_dim = w_gate.shape
    chunks, groups, late = len(row_chunks), len(row_chunks[0]), len(late_chunks[0])
    pieces = [piece for row_groups in row_chunks for piece in row_groups]
    late_pieces = [piece for blocks in late_chunks for piece in blocks]
    scratch = []
    if late:
        late_pieces.append(late_picker)
        scratch = [pltpu.VMEM((experts, late, slots, feature_dim), jnp.bfloat16)]
    whole = scale.shape[1]
    return pl.pallas_call(
        functools.partial(hidden_kernel, chunks, groups, late),
        grid=(experts,),
        in_specs=[pl.BlockSpec((1,) + piece.shape[1:], lambda e: (e, 0, 0)) for piece in pieces]
        + [pl.BlockSpec(memory_space=pltpu.VMEM)] * len(late_pieces)
        + [
            pl.BlockSpec((1, whole, 1), lambda e: (e, 0, 0)),
            pl.BlockSpec((1, feature_dim, hidden_dim), lambda e: (e, 0, 0)),
            pl.BlockSpec((1, feature_dim, hidden_dim), lambda e: (e, 0, 0)),
        ],
        out_specs=pl.BlockSpec((1, whole, hidden_dim), lambda e: (e, 0, 0)),
        out_shape=jax.ShapeDtypeStruct((experts, whole, hidden_dim), jnp.bfloat16),
        scratch_shapes=scratch,
        compiler_params=pltpu.CompilerParams(vmem_limit_bytes=grant(whole // slots, 32)),
        cost_estimate=pl.CostEstimate(
            flops=4 * experts * whole * feature_dim * hidden_dim,
            bytes_accessed=4 * experts * feature_dim * hidden_dim,
            transcendentals=experts * whole * hidden_dim,
        ),
    )(*pieces, *late_pieces, scale, w_gate, w_up)


def mix_kernel(order, hidden_ref, down_ref, spread_ref, first_ref, second_ref, made):
    step = pl.program_id(0)
    group = hidden_ref.shape[0]
    sources = spread_ref.shape[0]
    width = down_ref.shape[2]
    for one in range(group):
        made[step * group + one] = (
            jnp.dot(hidden_ref[one], down_ref[one], preferred_element_type=jnp.float32)
            .astype(jnp.bfloat16)
            .reshape(sources, slots, width)
        )

    @pl.when(step == pl.num_programs(0) - 1)
    def _():
        for source in range(sources):
            rows = made[:, source].reshape(spread_ref.shape[2], width)
            mixed = jnp.dot(
                spread_ref[source], rows, preferred_element_type=jnp.float32
            ).astype(jnp.bfloat16)
            if order[source] < sources // 2:
                first_ref[order[source]] = mixed
            else:
                second_ref[order[source] - sources // 2] = mixed


def mix_rows(hidden, w_down, spread, order, chunk, chunks):
    experts, whole, hidden_dim = hidden.shape
    width = w_down.shape[2] // chunks
    sources, token_count, local_rows = spread.shape
    group = 2 if experts % 2 == 0 else 1
    half = jax.ShapeDtypeStruct((sources // 2, token_count, width), jnp.bfloat16)
    return pl.pallas_call(
        functools.partial(mix_kernel, order),
        grid=(experts // group,),
        in_specs=[
            pl.BlockSpec((group, whole, hidden_dim), lambda e: (e, 0, 0)),
            pl.BlockSpec((group, hidden_dim, width), lambda e: (e, 0, chunk)),
            pl.BlockSpec(memory_space=pltpu.VMEM),
        ],
        out_specs=[pl.BlockSpec(memory_space=pltpu.VMEM)] * 2,
        out_shape=[half, half],
        scratch_shapes=[pltpu.VMEM((experts, sources, slots, width), jnp.bfloat16)],
        compiler_params=pltpu.CompilerParams(vmem_limit_bytes=grant(sources, 28)),
        cost_estimate=pl.CostEstimate(
            flops=2 * experts * whole * hidden_dim * width
            + 2 * sources * token_count * local_rows * width,
            bytes_accessed=2 * experts * hidden_dim * (width + whole)
            + 2 * sources * token_count * width,
            transcendentals=0,
        ),
    )(hidden, w_down, spread)


axes = ("expert", "dp")


def pairs_of(expert_pairs, dp_pairs, dp_size):
    return [
        (e_from * dp_size + d_from, e_to * dp_size + d_to)
        for e_from, e_to in expert_pairs
        for d_from, d_to in dp_pairs
    ]


stay_z = [(i, i) for i in range(4)]
stay_dp = [(i, i) for i in range(4)]
swap_z = pairs_of([(0, 1), (1, 0), (2, 3), (3, 2)], stay_dp, 4)
middle_z = pairs_of([(1, 2), (2, 1)], stay_dp, 4)
outward_z = pairs_of([(1, 0), (2, 3)], stay_dp, 4)
inward_z = pairs_of([(0, 1), (3, 2)], stay_dp, 4)
swap_x = pairs_of(stay_z, [(0, 2), (2, 0), (1, 3), (3, 1)], 4)
swap_core = pairs_of(stay_z, [(0, 1), (1, 0), (2, 3), (3, 2)], 4)


def send(value, pairs):
    return lax.ppermute(value, axes, pairs)


def together(*values):
    return lax.optimization_barrier(values)


def tree_start(own, *others):
    return together(send(own, swap_z), send(own, middle_z), send(own, swap_x), *others)


def tree_second(near, middle, *others):
    return together(
        send(near, middle_z), send(middle, outward_z), send(near, swap_x), *others
    )


def tree_third(cross, outer, middle, edge, *others):
    third = jnp.where(edge, outer, middle)
    far, third_x, *others = together(send(cross, outward_z), send(third, swap_x), *others)
    return third, third_x, jnp.where(edge, far, cross), *others


def late_blocks(third, fourth, third_x):
    late = [third, fourth, third_x, send(fourth, swap_x)]
    return late + [send(block, swap_core) for block in late]


def chip_sums(mine, theirs):
    return rounded_sum(mine, send(theirs, swap_core))


def tree_return(chip, near_by_z):
    own, near, own_x, near_x, third, fourth, third_x, fourth_x = [chip[i] for i in range(8)]
    if near_by_z:
        near_x = send(near_x, swap_z)
    fourth_in, third_x, near_x, own_x = together(send(fourth_x, swap_x), third_x, near_x, own_x)
    if near_by_z:
        own_x = rounded_sum(own_x, near_x)
    fourth = rounded_sum(fourth, fourth_in)
    far, third_in, near_x, own_x = together(
        send(fourth, inward_z), send(third_x, swap_x), near_x, own_x
    )
    cross = rounded_sum(fourth, far)
    third = rounded_sum(third, third_in)
    outer, crossed, by_x, own_x = together(
        send(third, inward_z),
        send(cross, middle_z),
        send(own_x if near_by_z else near_x, swap_x),
        own_x,
    )
    middle = rounded_sum(third, outer)
    if near_by_z:
        near = rounded_sum(near, crossed)
        own_in = by_x
    else:
        near = rounded_sum(near, by_x, crossed)
        own_in = send(own_x, swap_x)
    return rounded_sum(own, own_in, send(middle, middle_z), send(near, swap_z))


def shards(tokens, routes, route_weight, norm_gain, w_gate, w_up, w_down):
    token_count, top_count = routes.shape
    feature_dim = tokens.shape[1]
    expert_size = lax.axis_size("expert")
    dp_size = lax.axis_size("dp")
    device_count = expert_size * dp_size
    local_count = w_gate.shape[0]
    as_tree = expert_size == 4 and dp_size == 4
    edge = (lax.axis_index("expert") % 3) == 0

    width = feature_dim // gather_chunks
    parts = normed_parts(tokens, norm_gain, gather_chunks)
    if as_tree:
        choice = ranked(routes, route_weight, device_count, local_count)
        firsts = []
        for part in parts:
            if not firsts:
                near, middle, own_x, choice = tree_start(part, choice)
            else:
                near, middle, own_x = tree_start(part)
            firsts.append((near, middle, own_x))
    else:
        every = jnp.arange(device_count * local_count, dtype=jnp.int32)
        same = routes[:, :, None] == every
        named = jnp.any(same, axis=1)
        named_weight = jnp.sum(jnp.where(same, route_weight[:, :, None], 0.0), axis=1)
        count = jnp.arange(token_count)
        before = (count[:, None] > count[None, :]).astype(jnp.bfloat16)
        rank = jnp.dot(before, named.astype(jnp.bfloat16), preferred_element_type=jnp.float32)
        rank = jnp.where(named, rank, -1.0)
        choice = jnp.stack([rank.T, named_weight.T])
        choice = choice.reshape(2, device_count, local_count, token_count).transpose(1, 0, 2, 3)
        choice = choice.reshape(device_count, 2 * local_count, token_count)
    choices = lax.all_to_all(choice, axes, split_axis=0, concat_axis=0, tiled=True)
    if as_tree:
        place = jnp.stack([lax.axis_index("expert"), lax.axis_index("dp")])
        seconds = []
        for near, middle, own_x in firsts:
            if not seconds:
                cross, outer, near_x, choices = tree_second(near, middle, choices)
            else:
                cross, outer, near_x = tree_second(near, middle)
            seconds.append((cross, outer, near_x))
        mine, theirs, late_picker, spread, scale = tables(place, choices, local_count)
        theirs = send(theirs, swap_core)
        order = (0, 1, 2, 3, 8, 9, 10, 11, 4, 5, 6, 7, 12, 13, 14, 15)
        row_chunks, late_chunks = [], []
        for part, (near, middle, own_x), (cross, outer, near_x) in zip(parts, firsts, seconds):
            mine_rows, theirs_rows = pick_pair(
                (part, near, own_x, near_x), mine, theirs, local_count
            )
            theirs_rows = send(theirs_rows, swap_core)
            if len(late_chunks) == gather_chunks - 1:
                third, third_x, fourth, mine_rows = tree_third(
                    cross, outer, middle, edge, mine_rows
                )
            else:
                third, third_x, fourth = tree_third(cross, outer, middle, edge)
            rows = mine_rows, theirs_rows
            row_chunks.append([rows_of.reshape(local_count, -1, width) for rows_of in rows])
            late_chunks.append(late_blocks(third, fourth, third_x))
    else:
        rank, named_weight = choices[:, :local_count], choices[:, local_count:]
        match = rank[:, :, None, :] == jnp.arange(slots, dtype=jnp.float32)[None, None, :, None]
        picker = match.astype(jnp.bfloat16).reshape(device_count, local_count * slots, token_count)
        scale = jnp.sum(jnp.where(match, named_weight[:, :, None, :], 0.0), axis=3)
        scale = scale.transpose(1, 0, 2).reshape(local_count, device_count * slots, 1)
        spread = picker.transpose(0, 2, 1)
        rows = [pick_rows(picker, lax.all_gather(part, axes), local_count) for part in parts]
        row_chunks = [[rows_of.reshape(local_count, -1, width)] for rows_of in rows]
        late_chunks, late_picker = [[]] * gather_chunks, None
        order = tuple(range(device_count))
    hidden = hidden_rows(row_chunks, late_chunks, late_picker, scale, w_gate, w_up)

    sums = []
    for chunk in range(return_chunks):
        mine, theirs = mix_rows(hidden, w_down, spread, order, chunk, return_chunks)
        if as_tree:
            sums.append(chip_sums(mine, theirs))
        else:
            whole = jnp.concatenate([mine, theirs], axis=0).astype(jnp.float32)
            total = lax.psum_scatter(whole, axes, scatter_dimension=0)
            sums.append(total.astype(jnp.bfloat16))
    results = sums
    if as_tree:
        results = [tree_return(chip, chunk % 2 == 1) for chunk, chip in enumerate(sums)]
    return jnp.concatenate(results, axis=1)


def solution(mesh):
    split = P(("groups", "expert", "dp"), None)
    by_expert = P(("expert", "dp"), None, None)
    return jax.shard_map(
        shards,
        mesh=mesh,
        in_specs=(split, split, split, P(), by_expert, by_expert, by_expert),
        out_specs=split,
        check_vma=False,
    )
```
